256 devices in a mesh: gx: 2 (over z_lo), gy: 2 (over core), gz: 64 (over y, z_hi, x).
Axes of the slice: x: 4, y: 4, z: 8 (z_hi: 4, z_lo: 2; z = z_hi * 2 + z_lo), core: 2. Of those that a mesh axis runs over, the one named last changes fastest.
Arguments:
- phase: float32 [256, 64, 256], P('gz', 'gx', 'gy'), may hold values from -2 to 2
- velocity: float32 [3, 256, 64, 256], P(None, 'gz', 'gx', 'gy'), may hold values from -3 to 3
- phase_obs: float32 [256, 64, 256], P('gz', 'gx', 'gy'), may hold values from -2 to 2
- velocity_obs: float32 [3, 256, 64, 256], P(None, 'gz', 'gx', 'gy'), may hold values from -3 to 3
- coefs: float32 [4], replicated, may hold values from 0.5 to 2
Outputs:
- phase_back: float32 [256, 64, 256], P('gz', 'gx', 'gy')
- velocity_back: float32 [3, 256, 64, 256], P(None, 'gz', 'gx', 'gy')
- param_grads: float32 [4], replicated
The draws below stay inside these ranges and needn't reach their ends.
All inputs are finite; a program needn't handle non-finite values.
Results may differ from the reference program's by a relative error of at most 0.00045.
Values sent between devices are 32-bit elements; how exact they have to be, the bound alone decides.
No kernel may reach another device: no remote copies, remote signals or barrier semaphores. Data moves between devices by JAX's collectives and lax.ppermute only.
A program may use at most 64 MiB of HBM per device.

```python
import math
import jax
import jax.numpy as jnp

CZ = 4
CX = 32
CY = 128
ITERS = 2
NZ = 256
NX = 64
NY = 256


def jet_profile(radius_scale, waves):
    along = (jnp.arange(NZ, dtype=jnp.float32) + 0.5) / NZ
    first = ((jnp.arange(NX, dtype=jnp.float32) + 0.5) / NX - 0.5)[None, :, None]
    second = ((jnp.arange(NY, dtype=jnp.float32) + 0.5) / NY - 0.5)[None, None, :]
    radius = (0.25 * radius_scale * (1.0 + 0.15 * jnp.sin(2.0 * math.pi * waves * along)))[:, None, None]
    distance = jnp.sqrt(first * first + second * second)
    envelope = (1.0 + 2.0 * along)[:, None, None]
    return (jnp.tanh((radius - distance) / 0.04), envelope)


def rough_part(key, envelope):
    noise = jnp.clip(jax.random.normal(key, (NZ, NX, NY), jnp.float32), -3.5, 3.5)
    return 0.1 * envelope * noise


def draw_phase(key, part):
    key = jax.random.fold_in(key, 11)
    profile, envelope = jet_profile(1.0, 4.0)
    return jnp.clip(profile + rough_part(key, envelope), -2.0, 2.0).astype(jnp.float32)


def draw_phase_obs(key, part):
    key = jax.random.fold_in(key, 23)
    profile, envelope = jet_profile(0.95, 3.0)
    return jnp.clip(profile + rough_part(key, envelope), -2.0, 2.0).astype(jnp.float32)


def brick_weight(key):
    weight = jax.random.uniform(key, (NZ // CZ, NX // CX, NY // CY), jnp.float32, 0.1, 1.0)
    weight = jnp.repeat(weight, CZ, axis=0)
    weight = jnp.repeat(weight, CX, axis=1)
    return jnp.repeat(weight, CY, axis=2)


def smooth_flow(key, strength):
    cell_z = jnp.arange(NZ, dtype=jnp.int32)[:, None, None]
    cell_x = jnp.arange(NX, dtype=jnp.int32)[None, :, None]
    cell_y = jnp.arange(NY, dtype=jnp.int32)[None, None, :]
    components = []
    for component in range(3):
        total = jnp.zeros((NZ, NX, NY), jnp.float32)
        for wave_index in range(2):
            wave_key = jax.random.fold_in(key, 10 * component + wave_index)
            lengthwise = jax.random.randint(jax.random.fold_in(wave_key, 1), (), 1, 3)
            crosswise = jax.random.randint(jax.random.fold_in(wave_key, 2), (2,), -2, 3)
            offset = jax.random.uniform(jax.random.fold_in(wave_key, 3), (), jnp.float32, -math.pi, math.pi)
            height = jax.random.uniform(jax.random.fold_in(wave_key, 4), (), jnp.float32, 0.6, 1.0)
            wave_turns = (lengthwise * cell_z + crosswise[0] * cell_x + crosswise[1] * cell_y) % 32
            total = total + height * jnp.sin(2.0 * math.pi * wave_turns.astype(jnp.float32) / 32.0 + offset)
        components.append(strength * 0.7071 * total)
    return jnp.stack(components)


def mixed_flow(key, rough, strength):
    weight = brick_weight(jax.random.fold_in(key, 1))[None]
    smooth = smooth_flow(jax.random.fold_in(key, 3), strength)
    return jnp.clip((1.0 - weight) * smooth + 0.6 * weight * rough, -3.0, 3.0).astype(jnp.float32)


def draw_velocity(key, part):
    key = jax.random.fold_in(key, 31)
    noise_key = jax.random.fold_in(key, 2)
    rough = jnp.clip(jax.random.normal(noise_key, (3, NZ, NX, NY), jnp.float32), -3.5, 3.5)
    strength = 1.2
    return mixed_flow(key, rough, strength)


def draw_velocity_obs(key, part):
    key = jax.random.fold_in(key, 37)
    noise_key = jax.random.fold_in(key, 2)
    rough = jnp.clip(jax.random.normal(noise_key, (3, NZ, NX, NY), jnp.float32), -3.5, 3.5)
    strength = 1.2
    return mixed_flow(key, rough, strength)


def setup_inputs(seed: int = 0) -> dict:
    seeds = jax.random.split(jax.random.key(seed), 6)
    phase = draw_phase(jax.random.fold_in(seeds[5], 71), 0)
    velocity = draw_velocity(jax.random.fold_in(seeds[5], 71), 0)
    phase_obs = draw_phase_obs(jax.random.fold_in(seeds[5], 71), 0)
    velocity_obs = draw_velocity_obs(jax.random.fold_in(seeds[5], 71), 0)
    coefs = jnp.clip(jnp.exp(jax.random.uniform(seeds[4], (4,), jnp.float32, math.log(0.5), math.log(2.0))), 0.5, 2.0)
    return {"phase": phase, "velocity": velocity, "phase_obs": phase_obs, "velocity_obs": velocity_obs, "coefs": coefs}


DT = 0.1
SHIFT = 0.01


def neighbour(field, axis, moved):
    return jnp.roll(field, -moved, axis=field.ndim - 3 + axis)


def laplace(field):
    total = -6.0 * field
    for axis in range(3):
        total = total + neighbour(field, axis, 1) + neighbour(field, axis, -1)
    return total


def centred(field, axis):
    return (neighbour(field, axis, 1) - neighbour(field, axis, -1)) * 0.5


def gradient(field):
    return jnp.stack([centred(field, axis) for axis in range(3)])


def divergence(vector):
    return centred(vector[0], 0) + centred(vector[1], 1) + centred(vector[2], 2)


def solve(source):
    solution = jnp.zeros_like(source)
    residual = source
    direction = source
    norm_now = jnp.sum(residual * residual)
    for step in range(ITERS):
        image = SHIFT * direction - laplace(direction)
        alpha = norm_now / jnp.sum(direction * image)
        solution = solution + alpha * direction
        residual = residual - alpha * image
        norm_next = jnp.sum(residual * residual)
        direction = residual + (norm_next / norm_now) * direction
        norm_now = norm_next
    return solution


def reference(phase, velocity, phase_obs, velocity_obs, coefs):
    mobility = 0.1 * coefs[0]
    tension = 0.5 * coefs[1]
    viscosity = 0.1 * coefs[2]
    interface = 0.5 * coefs[3]
    lap_phase = laplace(phase)
    potential = phase * phase * phase - phase - interface * lap_phase
    lap_potential = laplace(potential)
    phase_grad = gradient(phase)
    vel_grad = jnp.stack([centred(velocity, axis) for axis in range(3)])
    advect = jnp.sum(velocity[:, None] * vel_grad, axis=0)
    lap_vel = laplace(velocity)
    provisional = velocity - DT * advect + DT * viscosity * lap_vel + DT * tension * potential * phase_grad
    pressure = solve(-divergence(provisional))
    new_velocity = provisional - gradient(pressure)
    new_phase = phase - DT * jnp.sum(velocity * phase_grad, axis=0) + DT * mobility * lap_potential
    phase_adj = new_phase - phase_obs
    velocity_adj = new_velocity - velocity_obs
    source_adj = solve(divergence(velocity_adj))
    prov_adj = velocity_adj + gradient(source_adj)
    potential_adj = DT * mobility * laplace(phase_adj) + DT * tension * jnp.sum(prov_adj * phase_grad, axis=0)
    phase_back = (phase_adj + DT * divergence(velocity * phase_adj[None])
                  + (3.0 * phase * phase - 1.0) * potential_adj - interface * laplace(potential_adj)
                  - DT * tension * divergence(potential[None] * prov_adj))
    transport = centred(velocity[0][None] * prov_adj, 0)
    transport = transport + centred(velocity[1][None] * prov_adj, 1)
    transport = transport + centred(velocity[2][None] * prov_adj, 2)
    velocity_back = (prov_adj - DT * phase_adj[None] * phase_grad
                     - DT * jnp.sum(prov_adj[None] * vel_grad, axis=1)
                     + DT * transport + DT * viscosity * laplace(prov_adj))
    partial_value = jnp.stack([DT * jnp.sum(phase_adj * lap_potential),
                         DT * jnp.sum(prov_adj * potential * phase_grad),
                         DT * jnp.sum(prov_adj * lap_vel),
                         -jnp.sum(potential_adj * lap_phase)])
    return phase_back, velocity_back, partial_value / phase.size
```

```python
import jax
import jax.numpy as jnp
from jax import lax
from jax.experimental import pallas as pl
from jax.experimental.pallas import tpu as pltpu
from jax.sharding import PartitionSpec as P

DT = 0.1
SHIFT = 0.01
CZ, CX, CY = 4, 32, 128
HX = 8
ROWS = CX + 2 * HX
LANES = 2 * CY
DEVICES = 256

V0, V1, V2, PH, PO, O0, O1, O2 = range(8)
HALO = (4, 3, 3, 4, 2, 1, 1, 1)
BASE = []
_at = 0
for _h in HALO:
    BASE.append(_at)
    _at += CZ + 2 * _h
TOTAL = _at
NUM_SUMS = 45


def x_up(a):
    return pltpu.roll(a, a.shape[0] - 1, 0)


def x_dn(a):
    return pltpu.roll(a, 1, 0)


def y_up(a):
    return pltpu.roll(a, a.shape[1] - 1, 1)


def y_dn(a):
    return pltpu.roll(a, 1, 1)


def dx(a):
    return 0.5 * (x_up(a) - x_dn(a))


def dy(a):
    return 0.5 * (y_up(a) - y_dn(a))


def own(a):
    return a[HX : HX + CX, :CY]


def loop(count, body):
    def step(t, carry):
        body(t)
        return carry

    lax.fori_loop(0, count, step, 0)


def first_kernel(coefs, e, b, u, q, adj, pot, lph, g, lv, p0, p1, p2):
    mobility = 0.1 * coefs[0]
    tension = 0.5 * coefs[1]
    viscosity = 0.1 * coefs[2]
    interface = 0.5 * coefs[3]

    def at(field, z):
        return e[BASE[field] + HALO[field] + z]

    def around(field, z):
        c = at(field, z)
        zu, zd = at(field, z + 1), at(field, z - 1)
        xu, xd, yu, yd = x_up(c), x_dn(c), y_up(c), y_dn(c)
        lap = (zu + zd) + (xu + xd) + (yu + yd) - 6.0 * c
        return c, 0.5 * (zu - zd), 0.5 * (xu - xd), 0.5 * (yu - yd), lap

    def potential(t):
        c = at(PH, t - 3)
        lap = at(PH, t - 2) + at(PH, t - 4) + (x_up(c) + x_dn(c)) + (y_up(c) + y_dn(c)) - 6.0 * c
        lph[t] = lap
        pot[t] = c * c * c - c - interface * lap

    loop(10, potential)

    def provisional(field, z, grad, potential_here):
        c, d0, d1, d2, lap = around(field, z)
        advect = at(V0, z) * d0 + at(V1, z) * d1 + at(V2, z) * d2
        value = c - DT * advect + (DT * viscosity) * lap + (DT * tension) * (potential_here * grad)
        return value, lap

    def along(t):
        z = t - 3
        grad = 0.5 * (at(PH, z + 1) - at(PH, z - 1))
        p0[t], lap = provisional(V0, z, grad, pot[t])
        lv[0, t] = lap

    loop(10, along)

    def across(t):
        z = t - 2
        c = at(PH, z)
        here = pot[t + 1]
        g0 = 0.5 * (at(PH, z + 1) - at(PH, z - 1))
        g1 = dx(c)
        g2 = dy(c)
        g[0, t] = g0
        g[1, t] = g1
        g[2, t] = g2
        p1[t], lap1 = provisional(V1, z, g1, here)
        p2[t], lap2 = provisional(V2, z, g2, here)
        lv[1, t + 1] = lap1
        lv[2, t + 1] = lap2
        lap_pot = pot[t + 2] + pot[t] + (x_up(here) + x_dn(here)) + (y_up(here) + y_dn(here)) - 6.0 * here
        flow = at(V0, z) * g0 + at(V1, z) * g1 + at(V2, z) * g2
        adj[t] = c - DT * flow + (DT * mobility) * lap_pot - at(PO, z)

    loop(8, across)

    def source(t):
        b[t] = -(0.5 * (p0[t + 2] - p0[t]) + dx(p1[t]) + dy(p2[t]))

    loop(8, source)

    def misfit(t):
        z = t - 1
        q[0, t] = p0[t + 2] - at(O0, z)
        q[1, t] = p1[t + 1] - at(O1, z)
        q[2, t] = p2[t + 1] - at(O2, z)

    loop(6, misfit)

    def second_source(t):
        u[t] = 0.5 * (q[0, t + 2] - q[0, t]) + dx(q[1, t + 1]) + dy(q[2, t + 1])

    loop(4, second_source)


def rows_of(a):
    return (a[0:8] + a[8:16]) + (a[16:24] + a[24:32])


def weight_kernel(q, adj, pot, lph, g, lv, w, part):
    zero = jnp.zeros((8, CY), jnp.float32)
    sums = [zero] * 5
    for t in range(CZ):
        here = pot[t + 3]
        lap = lph[t + 3]
        up, dn = pot[t + 4] * g[0, t + 3], pot[t + 2] * g[0, t + 1]
        w1 = 0.5 * (up - dn) + dx(here * g[1, t + 2]) + dy(here * g[2, t + 2])
        w2 = 0.5 * (lv[0, t + 4] - lv[0, t + 2]) + dx(lv[1, t + 3]) + dy(lv[2, t + 3])
        up, dn = lph[t + 4] * g[0, t + 3], lph[t + 2] * g[0, t + 1]
        w3 = 0.5 * (up - dn) + dx(lap * g[1, t + 2]) + dy(lap * g[2, t + 2])
        w[0, t] = own(w1)
        w[1, t] = own(w2)
        w[2, t] = own(w3)
        lap_pot = pot[t + 4] + pot[t + 2] + (x_up(here) + x_dn(here)) + (y_up(here) + y_dn(here)) - 6.0 * here
        c = adj[t + 2]
        lap_adj = adj[t + 3] + adj[t + 1] + (x_up(c) + x_dn(c)) + (y_up(c) + y_dn(c)) - 6.0 * c
        qg = q[0, t + 1] * g[0, t + 2] + q[1, t + 1] * g[1, t + 2] + q[2, t + 1] * g[2, t + 2]
        ql = q[0, t + 1] * lv[0, t + 3] + q[1, t + 1] * lv[1, t + 3] + q[2, t + 1] * lv[2, t + 3]
        terms = (own(c * lap_pot), own(here * qg), own(ql), own(lap * qg), own(lap_adj * lap))
        sums = [s + rows_of(a) for s, a in zip(sums, terms)]
    for k in range(5):
        part[k] = sums[k]


def shifted(c, zu, zd):
    return (6.0 + SHIFT) * c - ((zu + zd) + (x_up(c) + x_dn(c)) + (y_up(c) + y_dn(c)))


def moment_kernel(b8, u4, lo, hi, w, part, psi, out, bb, uu, f, af, a2f, a3f, ab, a2b, au, a2u):
    bb[0:4] = lo[0:4]
    bb[4:12] = b8[...]
    bb[12:16] = hi[0:4]
    uu[0:3] = lo[4:7]
    uu[3:7] = u4[...]
    uu[7:10] = hi[4:7]

    def wide(t):
        c = bb[t + 2]
        n = c.shape[0]
        across = (pltpu.roll(c, n - 2, 0) + pltpu.roll(c, 2, 0)) + (pltpu.roll(c, LANES - 2, 1) + pltpu.roll(c, 2, 1))
        f[t] = 0.25 * ((bb[t + 4] + bb[t]) + across) - 1.5 * c

    loop(12, wide)

    def apply(src, dst, count):
        def body(t):
            dst[t] = shifted(src[t + 1], src[t + 2], src[t])

        loop(count, body)

    apply(f, af, 10)
    apply(af, a2f, 8)
    apply(a2f.at[pl.ds(1, 6)], a3f, 4)
    apply(bb.at[pl.ds(3, 10)], ab, 8)
    apply(ab.at[pl.ds(1, 6)], a2b, 4)
    apply(uu, au, 8)
    apply(au.at[pl.ds(1, 6)], a2u, 4)

    def keep(t):
        psi[0, t] = uu[t + 1]
        psi[1, t] = au[t]
        psi[2, t] = f[t + 2]
        psi[3, t] = af[t + 1]
        psi[4, t] = a2f[t]
        psi[5, t] = bb[t + 4]
        psi[6, t] = ab[t]

    loop(8, keep)

    rows = pl.ds(HX, CX)
    lanes = pl.ds(0, CY)
    acc = [jnp.zeros((8, CY), jnp.float32)] * 40
    for t in range(CZ):
        vb, vab, va2b = bb[t + 6, rows, lanes], ab[t + 2, rows, lanes], a2b[t, rows, lanes]
        vu, vau, va2u = uu[t + 3, rows, lanes], au[t + 2, rows, lanes], a2u[t, rows, lanes]
        vf, vaf, va2f, va3f = (
            f[t + 4, rows, lanes], af[t + 3, rows, lanes], a2f[t + 2, rows, lanes], a3f[t, rows, lanes],
        )
        terms = [
            vb * vb, vb * vab, vab * vab, vab * va2b,
            vu * vu, vu * vau, vau * vau, vau * va2u,
            vu * vf, vu * vaf, vu * va2f, vau * va2f, va2u * va2f,
            vf * vf, vf * vaf, vaf * vaf, vaf * va2f, va2f * va2f, va2f * va3f,
        ]
        for k in range(3):
            wk = w[k, t]
            terms += [a * wk for a in (vu, vau, vf, vaf, va2f, vb, vab)]
        acc = [s + rows_of(a) for s, a in zip(acc, terms)]
    rows_list = [jnp.sum(a, axis=0, keepdims=True) for a in acc]
    rows_list += [jnp.sum(part[k], axis=0, keepdims=True) for k in range(5)]
    rows_list += [jnp.zeros((1, CY), jnp.float32)] * (48 - NUM_SUMS)
    table = jnp.concatenate(rows_list, axis=0)
    totals = jnp.sum(table, axis=1, keepdims=True)
    line = lax.broadcasted_iota(jnp.int32, (48, CY), 1)
    which = lax.broadcasted_iota(jnp.int32, (48, CY), 0)
    row = jnp.sum(jnp.where(line == which, totals, 0.0), axis=0, keepdims=True)
    out[...] = jnp.broadcast_to(row, (DEVICES, CY))


def steps(m0, m1, m2, m3):
    alpha = m0 / m1
    norm = m0 * ((m0 * m2) / (m1 * m1) - 1.0)
    beta = norm / m0
    one = 1.0 + beta
    curve = one * one * m1 - 2.0 * one * alpha * m2 + alpha * alpha * m3
    second = norm / curve
    return alpha + second * one, -second * alpha


def last_kernel(coefs, gathered, psi, e, q, adj, pot, g, phase_back, velocity_back, params, phi, pr, pa):
    mobility = 0.1 * coefs[0]
    tension = 0.5 * coefs[1]
    viscosity = 0.1 * coefs[2]
    interface = 0.5 * coefs[3]

    total = jnp.sum(gathered[...], axis=0, keepdims=True)
    line = lax.broadcasted_iota(jnp.int32, (1, CY), 1)

    def s(k):
        return jnp.sum(jnp.where(line == k, total, 0.0), axis=1, keepdims=True)

    c0, c1 = steps(s(0), s(1), s(2), s(3))
    uu = [s(4 + k) for k in range(4)]
    uf = [s(8 + k) for k in range(5)]
    ff = [s(13 + k) for k in range(6)]
    moments = [
        uu[k] - 2.0 * (c0 * uf[k] + c1 * uf[k + 1])
        + (c0 * c0) * ff[k] + (2.0 * c0 * c1) * ff[k + 1] + (c1 * c1) * ff[k + 2]
        for k in range(4)
    ]
    e0, e1 = steps(*moments)
    coef = (e0, e1, -e0 * c0, -(e0 * c1 + e1 * c0), -e1 * c1, -c0, -c1)

    def meet(k):
        value = coef[0] * s(19 + 7 * k)
        for j in range(1, 7):
            value = value + coef[j] * s(19 + 7 * k + j)
        return value

    scale = 1.0 / (256 * 64 * 256)
    g0 = DT * s(40)
    g1 = DT * (s(41) - meet(0))
    g2 = DT * (s(42) - meet(1))
    g3 = -((DT * mobility) * s(44) + (DT * tension) * (s(43) - meet(2)))
    place = lax.broadcasted_iota(jnp.int32, (1, CY), 1)
    packed = jnp.where(place == 0, g0, jnp.where(place == 1, g1, jnp.where(place == 2, g2, g3)))
    params[...] = packed * scale

    def combine(t):
        value = coef[0] * psi[0, t]
        for j in range(1, 7):
            value = value + coef[j] * psi[j, t]
        phi[t] = value

    loop(8, combine)

    def at(field, z):
        return e[BASE[field] + HALO[field] + z]

    def project(t):
        c = phi[t + 1]
        r0 = q[0, t] + 0.5 * (phi[t + 2] - phi[t])
        r1 = q[1, t] + dx(c)
        r2 = q[2, t] + dy(c)
        pr[0, t] = r0
        pr[1, t] = r1
        pr[2, t] = r2
        d = adj[t + 1]
        lap = adj[t + 2] + adj[t] + (x_up(d) + x_dn(d)) + (y_up(d) + y_dn(d)) - 6.0 * d
        pa[t] = (DT * mobility) * lap + (DT * tension) * (r0 * g[0, t + 1] + r1 * g[1, t + 1] + r2 * g[2, t + 1])

    loop(6, project)

    def finish(t):
        v0, v1, v2 = at(V0, t), at(V1, t), at(V2, t)
        v0u, v0d = at(V0, t + 1), at(V0, t - 1)
        c = adj[t + 2]
        here = pot[t + 3]
        ph = at(PH, t)
        lam = pa[t + 1]
        lap = pa[t + 2] + pa[t] + (x_up(lam) + x_dn(lam)) + (y_up(lam) + y_dn(lam)) - 6.0 * lam
        up = v0u * adj[t + 3] - tension * (pot[t + 4] * pr[0, t + 2])
        dn = v0d * adj[t + 1] - tension * (pot[t + 2] * pr[0, t])
        div = 0.5 * (up - dn)
        div = div + dx(v1 * c - tension * (here * pr[1, t + 1]))
        div = div + dy(v2 * c - tension * (here * pr[2, t + 1]))
        value = c + DT * div + (3.0 * ph * ph - 1.0) * lam - interface * lap
        phase_back[t] = own(value)
        r = [pr[i, t + 1] for i in range(3)]
        vel = (v0, v1, v2)
        grads = [[], [], []]
        for i, field in enumerate((V0, V1, V2)):
            grads[0].append(0.5 * (at(field, t + 1) - at(field, t - 1)))
            grads[1].append(dx(vel[i]))
            grads[2].append(dy(vel[i]))
        for k in range(3):
            mix = r[0] * grads[k][0] + r[1] * grads[k][1] + r[2] * grads[k][2]
            ru, rd = pr[k, t + 2], pr[k, t]
            moved = (viscosity + 0.5 * v0u) * ru + (viscosity - 0.5 * v0d) * rd
            moved = moved + x_up((viscosity + 0.5 * v1) * r[k]) + x_dn((viscosity - 0.5 * v1) * r[k])
            moved = moved + y_up((viscosity + 0.5 * v2) * r[k]) + y_dn((viscosity - 0.5 * v2) * r[k])
            moved = moved - (6.0 * viscosity) * r[k]
            value = r[k] + DT * (moved - mix - c * g[k, t + 2])
            velocity_back[k, t] = own(value)

    loop(4, finish)


def f32(*shape):
    return jax.ShapeDtypeStruct(shape, jnp.float32)


def layers(*lead):
    return f32(*lead, ROWS, LANES)


def scratch(*lead):
    return pltpu.VMEM((*lead, ROWS, LANES), jnp.float32)


VM = pl.BlockSpec(memory_space=pltpu.VMEM)
SM = pl.BlockSpec(memory_space=pltpu.SMEM)
PARAMS = pltpu.CompilerParams(vmem_limit_bytes=48 * 1024 * 1024)
SWAP = [(0, 1), (1, 0)]


def ring(value, step):
    count = lax.axis_size("gz")
    return lax.ppermute(value, "gz", [(i, (i + step) % count) for i in range(count)])


def extend(fields):
    lo = ring(jnp.concatenate([f[CZ - h :] for f, h in zip(fields, HALO)], 0), 1)
    hi = ring(jnp.concatenate([f[:h] for f, h in zip(fields, HALO)], 0), -1)
    parts = []
    at = 0
    for f, h in zip(fields, HALO):
        parts += [lo[at : at + h], f, hi[at : at + h]]
        at += h
    block = jnp.concatenate(parts, 0)
    got = lax.ppermute(jnp.concatenate([block[:, CX - HX :], block[:, :HX]], 1), "gx", SWAP)
    block = jnp.concatenate([got[:, :HX], block, got[:, HX:]], 1)
    other = lax.ppermute(block, "gy", SWAP)
    return jnp.concatenate([block, other], 2)


def local(phase, velocity, phase_obs, velocity_obs, coefs):
    fields = (
        velocity[0], velocity[1], velocity[2], phase, phase_obs,
        velocity_obs[0], velocity_obs[1], velocity_obs[2],
    )
    e = extend(fields)
    b, u, q, adj, pot, lph, g, lv = pl.pallas_call(
        first_kernel,
        out_shape=(layers(8), layers(4), layers(3, 6), layers(8), layers(10), layers(10), layers(3, 8), layers(3, 10)),
        in_specs=[SM, VM],
        out_specs=(VM,) * 8,
        scratch_shapes=[scratch(10), scratch(8), scratch(8)],
        compiler_params=PARAMS,
        name="first",
    )(coefs, e)
    lo = ring(jnp.concatenate([b[0:4], u[1:4]], 0), 1)
    hi = ring(jnp.concatenate([b[4:8], u[0:3]], 0), -1)
    w, part = pl.pallas_call(
        weight_kernel,
        out_shape=(f32(3, CZ, CX, CY), f32(5, 8, CY)),
        in_specs=[VM] * 6,
        out_specs=(VM, VM),
        compiler_params=PARAMS,
        name="weights",
    )(q, adj, pot, lph, g, lv)
    psi, sums = pl.pallas_call(
        moment_kernel,
        out_shape=(layers(7, 8), f32(DEVICES, CY)),
        in_specs=[VM] * 6,
        out_specs=(VM, VM),
        scratch_shapes=[
            scratch(16), scratch(10), scratch(12), scratch(10), scratch(8),
            scratch(4), scratch(8), scratch(4), scratch(8), scratch(4),
        ],
        compiler_params=PARAMS,
        name="moments",
    )(b, u, lo, hi, w, part)
    gathered = lax.all_to_all(sums.reshape(DEVICES, 1, CY), ("gx", "gy", "gz"), 0, 0).reshape(DEVICES, CY)
    phase_back, velocity_back, params = pl.pallas_call(
        last_kernel,
        out_shape=(f32(CZ, CX, CY), f32(3, CZ, CX, CY), f32(1, CY)),
        in_specs=[SM] + [VM] * 7,
        out_specs=(VM, VM, VM),
        scratch_shapes=[scratch(8), scratch(3, 6), scratch(6)],
        compiler_params=PARAMS,
        name="last",
    )(coefs, gathered, psi, e, q, adj, pot, g)
    return phase_back, velocity_back, params[0, :4]


def solution(mesh):
    return jax.shard_map(
        local,
        mesh=mesh,
        in_specs=(
            P("gz", "gx", "gy"),
            P(None, "gz", "gx", "gy"),
            P("gz", "gx", "gy"),
            P(None, "gz", "gx", "gy"),
            P(),
        ),
        out_specs=(P("gz", "gx", "gy"), P(None, "gz", "gx", "gy"), P()),
        check_vma=False,
    )
```

```python
import jax
import jax.numpy as jnp
from jax import lax
from jax.experimental import pallas as pl
from jax.experimental.pallas import tpu as pltpu
from jax.sharding import PartitionSpec as P

DT = 0.1
SHIFT = 0.01
CZ, CX, CY = 4, 32, 128
HX = 8
NEAR = 4
ROWS = CX + 2 * HX
LANES = 2 * CY
DEVICES = 256

V0, V1, V2, PH, PO, O0, O1, O2 = range(8)
HALO = (3, 2, 2, 3, 0, 1, 0, 0)
BASE = []
_at = 0
for _h in HALO:
    BASE.append(_at)
    _at += CZ + 2 * _h
TOTAL = _at
SENT = sum(HALO)
NUM_SUMS = 45
SLOTS = 64


def x_up(a):
    return pltpu.roll(a, a.shape[0] - 1, 0)


def x_dn(a):
    return pltpu.roll(a, 1, 0)


def y_up(a):
    return pltpu.roll(a, a.shape[1] - 1, 1)


def y_dn(a):
    return pltpu.roll(a, 1, 1)


def dx(a):
    return 0.5 * (x_up(a) - x_dn(a))


def dy(a):
    return 0.5 * (y_up(a) - y_dn(a))


def own(a):
    return a[HX : HX + CX, :CY]


def lap_of(c, zu, zd):
    return (zu + zd) + (x_up(c) + x_dn(c)) + (y_up(c) + y_dn(c)) - 6.0 * c


def other_first(a):
    return jnp.concatenate([a[:, CY:], a[:, :CY]], 1)


def loop(count, body):
    def step(t, carry):
        body(t)
        return carry

    lax.fori_loop(0, count, step, 0)


def low_high(core, mine, theirs, j):
    a, b = mine[j], other_first(theirs[j])
    return jnp.where(core == 0, a, b), jnp.where(core == 0, b, a)


def load_kernel(vel, ph, po, vo, coefs, stack, out, coefs_out, sems):
    copies = [
        pltpu.make_async_copy(ph, stack.at[pl.ds(CZ * PH, CZ)], sems.at[6]),
        pltpu.make_async_copy(po, stack.at[pl.ds(CZ * PO, CZ)], sems.at[7]),
        pltpu.make_async_copy(coefs, coefs_out, sems.at[8]),
    ]
    for i in range(3):
        copies.append(pltpu.make_async_copy(vel.at[i], stack.at[pl.ds(CZ * (V0 + i), CZ)], sems.at[i]))
        copies.append(pltpu.make_async_copy(vo.at[i], stack.at[pl.ds(CZ * (O0 + i), CZ)], sems.at[3 + i]))
    for copy in copies:
        copy.start()
    for copy in copies:
        copy.wait()
    wide = CZ * PO
    out[0:wide, 0:HX] = stack[0:wide, CX - HX :]
    out[0:wide, HX:] = stack[0:wide, :HX]
    for n in range(wide):
        at, row = wide + n // 2, HX * (n % 2)
        out[at, row : row + NEAR] = stack[wide + n, CX - NEAR :]
        out[at, row + NEAR : row + HX] = stack[wide + n, :NEAR]


def pack_kernel(core, stack, vel_s, ph_s, vo_s, main, diag):
    c = core[0]
    n = 0
    for f, h in enumerate(HALO):
        for j in range(h):
            z = j + (CZ - h) * (1 - c)
            for half in range(2):
                if half == 0:
                    src = stack[CZ * f + z]
                else:
                    src = vel_s[f, z] if f < 3 else ph_s[z] if f == PH else vo_s[f - O0, z]
                lanes = pl.ds(CY * half, CY)
                main[n, :, lanes] = src
                diag[n, 0:HX, lanes] = src[CX - HX :]
                diag[n, HX:, lanes] = src[:HX]
            n += 1


def first_kernel(
    coefs, core, stack, vel_s, ph_s, po_s, vo_s, gxr, gxs, mr, ms, dr, ds,
    e, b, u, q, pot, lph, g, lv, send, p0, p1, p2,
):
    tension = 0.5 * coefs[1]
    viscosity = 0.1 * coefs[2]
    interface = 0.5 * coefs[3]
    c = core[0]

    n = 0
    for f, h in enumerate(HALO):
        mid = BASE[f] + h
        for z in range(CZ):
            for half, x in enumerate((gxr, gxs)):
                if half == 0:
                    src = stack[CZ * f + z]
                else:
                    src = vel_s[f, z] if f < 3 else ph_s[z] if f == PH else po_s[z] if f == PO else vo_s[f - O0, z]
                lanes = pl.ds(CY * half, CY)
                e[mid + z, HX : HX + CX, lanes] = src
                if f <= PH:
                    e[mid + z, 0:HX, lanes] = x[CZ * f + z, 0:HX]
                    e[mid + z, HX + CX :, lanes] = x[CZ * f + z, HX:]
                else:
                    k = CZ * (f - PO) + z
                    pair, row = CZ * PO + k // 2, HX * (k % 2)
                    e[mid + z, HX - NEAR : HX, lanes] = x[pair, row : row + NEAR]
                    e[mid + z, HX + CX : HX + CX + NEAR, lanes] = x[pair, row + NEAR : row + HX]
        for j in range(h):
            lo, hi = low_high(c, mr, ms, n)
            e[BASE[f] + j, HX : HX + CX] = lo
            e[mid + CZ + j, HX : HX + CX] = hi
            lo, hi = low_high(c, dr, ds, n)
            e[BASE[f] + j, 0:HX] = lo[0:HX]
            e[BASE[f] + j, HX + CX :] = lo[HX:]
            e[mid + CZ + j, 0:HX] = hi[0:HX]
            e[mid + CZ + j, HX + CX :] = hi[HX:]
            n += 1

    def at(field, z):
        return e[BASE[field] + HALO[field] + z]

    def potential(t):
        z = t - 2
        a = at(PH, z)
        lap = lap_of(a, at(PH, z + 1), at(PH, z - 1))
        lph[t] = lap
        pot[t] = a * a * a - a - interface * lap

    loop(8, potential)

    def provisional(field, z, grad, here):
        a = at(field, z)
        zu, zd = at(field, z + 1), at(field, z - 1)
        xu, xd, yu, yd = x_up(a), x_dn(a), y_up(a), y_dn(a)
        lap = (zu + zd) + (xu + xd) + (yu + yd) - 6.0 * a
        advect = at(V0, z) * (zu - zd) + at(V1, z) * (xu - xd) + at(V2, z) * (yu - yd)
        value = a - (0.5 * DT) * advect + (DT * viscosity) * lap + (DT * tension) * (here * grad)
        return value, lap

    def along(t):
        z = t - 2
        grad = 0.5 * (at(PH, z + 1) - at(PH, z - 1))
        p0[t], lv[0, t] = provisional(V0, z, grad, pot[t])

    loop(8, along)

    def across(t):
        z = t - 1
        a = at(PH, z)
        here = pot[t + 1]
        g0 = 0.5 * (at(PH, z + 1) - at(PH, z - 1))
        g1 = dx(a)
        g2 = dy(a)
        g[0, t] = g0
        g[1, t] = g1
        g[2, t] = g2
        p1[t], lv[1, t] = provisional(V1, z, g1, here)
        p2[t], lv[2, t] = provisional(V2, z, g2, here)

    loop(6, across)

    def source(t):
        b[t] = -(0.5 * (p0[t + 2] - p0[t]) + dx(p1[t]) + dy(p2[t]))
        q[0, t] = p0[t + 1] - at(O0, t - 1)

    loop(6, source)

    def second_source(t):
        q1 = p1[t + 1] - at(O1, t)
        q2 = p2[t + 1] - at(O2, t)
        q[1, t + 1] = q1
        q[2, t + 1] = q2
        u[t] = 0.5 * (q[0, t + 2] - q[0, t]) + dx(q1) + dy(q2)

    loop(4, second_source)

    for j in range(4):
        send[j] = b[j + 2 * c, NEAR : ROWS - NEAR]
    for j in range(2):
        send[4 + j] = u[j + 2 * (1 - c), NEAR : ROWS - NEAR]


def rows_of(a):
    return (a[0:8] + a[8:16]) + (a[16:24] + a[24:32])


def weight_kernel(coefs, e, q, pot, lph, g, lv, adj, w, part, edge):
    mobility = 0.1 * coefs[0]

    def at(field, z):
        return e[BASE[field] + HALO[field] + z]

    sums = [jnp.zeros((8, CY), jnp.float32)] * 5
    for t in range(CZ):
        here = pot[t + 2]
        lap = lph[t + 2]
        gs = [g[i, t + 1] for i in range(3)]
        up, dn = pot[t + 3] * g[0, t + 2], pot[t + 1] * g[0, t]
        w1 = 0.5 * (up - dn) + dx(here * gs[1]) + dy(here * gs[2])
        w2 = 0.5 * (lv[0, t + 3] - lv[0, t + 1]) + dx(lv[1, t + 1]) + dy(lv[2, t + 1])
        up, dn = lph[t + 3] * g[0, t + 2], lph[t + 1] * g[0, t]
        w3 = 0.5 * (up - dn) + dx(lap * gs[1]) + dy(lap * gs[2])
        w[0, t] = own(w1)
        w[1, t] = own(w2)
        w[2, t] = own(w3)
        lap_pot = lap_of(here, pot[t + 3], pot[t + 1])
        lap_lap = lap_of(lap, lph[t + 3], lph[t + 1])
        flow = at(V0, t) * gs[0] + at(V1, t) * gs[1] + at(V2, t) * gs[2]
        c = at(PH, t) - DT * flow + (DT * mobility) * lap_pot - at(PO, t)
        adj[t] = c
        qs = [q[i, t + 1] for i in range(3)]
        qg = qs[0] * gs[0] + qs[1] * gs[1] + qs[2] * gs[2]
        ql = qs[0] * lv[0, t + 2] + qs[1] * lv[1, t + 1] + qs[2] * lv[2, t + 1]
        terms = (own(c * lap_pot), own(here * qg), own(ql), own(lap * qg), own(c * lap_lap))
        sums = [s + rows_of(a) for s, a in zip(sums, terms)]
    for k in range(5):
        part[k] = sums[k]
    for k, z in ((0, CZ - 1), (1, 0)):
        edge[k, 0] = q[1, z + 1, NEAR : ROWS - NEAR]
        edge[k, 1] = q[2, z + 1, NEAR : ROWS - NEAR]
        for j in range(2):
            edge[k, 2 + j] = adj[2 * (1 - k) + j, NEAR : ROWS - NEAR]


def shifted(c, zu, zd):
    return (6.0 + SHIFT) * c - ((zu + zd) + (x_up(c) + x_dn(c)) + (y_up(c) + y_dn(c)))


def moment_kernel(core, b6, u4, r, s, w, part, edge, out, bb, uu, f, af, a2f, ab, au, send, a3f, a2b, a2u):
    c = core[0]
    near = pl.ds(NEAR, ROWS - 2 * NEAR)
    for j in range(4):
        lo, hi = low_high(c, r, s, j)
        bb[j, near] = lo
        bb[10 + j, near] = hi
    for j in range(2):
        lo, hi = low_high(c, r, s, 4 + j)
        uu[j, near] = lo
        uu[6 + j, near] = hi
    bb[4:10] = b6[...]
    uu[2:6] = u4[...]

    def wide(t):
        a = bb[t + 2]
        across = (pltpu.roll(a, ROWS - 2, 0) + pltpu.roll(a, 2, 0)) + (
            pltpu.roll(a, LANES - 2, 1) + pltpu.roll(a, 2, 1)
        )
        f[t] = 0.25 * ((bb[t + 4] + bb[t]) + across) - 1.5 * a

    loop(10, wide)

    def apply(src, dst, count):
        def body(t):
            dst[t] = shifted(src[t + 1], src[t + 2], src[t])

        loop(count, body)

    apply(f, af, 8)
    apply(af, a2f, 6)
    apply(a2f, a3f, 4)
    apply(bb.at[pl.ds(2, 10)], ab, 8)
    apply(ab.at[pl.ds(1, 6)], a2b, 4)
    apply(uu, au, 6)
    apply(au, a2u, 4)

    rows = pl.ds(HX, CX)
    lanes = pl.ds(0, CY)
    acc = [jnp.zeros((8, CY), jnp.float32)] * 40
    for t in range(CZ):
        vb, vab, va2b = bb[t + 5, rows, lanes], ab[t + 2, rows, lanes], a2b[t, rows, lanes]
        vu, vau, va2u = uu[t + 2, rows, lanes], au[t + 1, rows, lanes], a2u[t, rows, lanes]
        vf, vaf, va2f, va3f = (
            f[t + 3, rows, lanes], af[t + 2, rows, lanes], a2f[t + 1, rows, lanes], a3f[t, rows, lanes],
        )
        terms = [
            vb * vb, vb * vab, vab * vab, vab * va2b,
            vu * vu, vu * vau, vau * vau, vau * va2u,
            vu * vf, vu * vaf, vu * va2f, vau * va2f, va2u * va2f,
            vf * vf, vf * vaf, vaf * vaf, vaf * va2f, va2f * va2f, va2f * va3f,
        ]
        for k in range(3):
            wk = w[k, t]
            terms += [a * wk for a in (vu, vau, vf, vaf, va2f, vb, vab)]
        acc = [x + rows_of(a) for x, a in zip(acc, terms)]
    rows_list = [jnp.sum(a, axis=0, keepdims=True) for a in acc]
    rows_list += [jnp.sum(part[k], axis=0, keepdims=True) for k in range(5)]
    rows_list += [jnp.zeros((1, CY), jnp.float32)] * (48 - NUM_SUMS)
    table = jnp.concatenate(rows_list, axis=0)
    totals = jnp.sum(table, axis=1, keepdims=True)
    line = lax.broadcasted_iota(jnp.int32, (48, SLOTS), 1)
    which = lax.broadcasted_iota(jnp.int32, (48, SLOTS), 0)
    row = jnp.sum(jnp.where(line == which, totals, 0.0), axis=0, keepdims=True)
    out[...] = jnp.broadcast_to(row, (DEVICES, SLOTS))
    send[0:4] = edge[c]
    send[4] = a2f[3 - c, near]
    send[5] = au[3 - c, near]


def steps(m0, m1, m2, m3):
    alpha = m0 / m1
    norm = m0 * ((m0 * m2) / (m1 * m1) - 1.0)
    beta = norm / m0
    one = 1.0 + beta
    curve = one * one * m1 - 2.0 * one * alpha * m2 + alpha * alpha * m3
    second = norm / curve
    return alpha + second * one, -second * alpha


def last_kernel(
    coefs, core, gathered, bb, uu, f, af, a2f, ab, au, ri, si, e, q, adj4, pot, g,
    phase_back, velocity_back, params, phi, pr, pa, adj, qe,
):
    c = core[0]
    near = pl.ds(NEAR, ROWS - 2 * NEAR)
    for i in range(2):
        lo, hi = low_high(c, ri, si, i)
        qe[i, 0, near] = lo
        qe[i, 5, near] = hi
        qe[i, 1:5] = q[i + 1, 1:5]
        lo, hi = low_high(c, ri, si, 2 + i)
        adj[i, near] = lo
        adj[6 + i, near] = hi
    adj[2:6] = adj4[...]
    mobility = 0.1 * coefs[0]
    tension = 0.5 * coefs[1]
    viscosity = 0.1 * coefs[2]
    interface = 0.5 * coefs[3]

    total = jnp.sum(gathered[...], axis=0, keepdims=True)
    line = lax.broadcasted_iota(jnp.int32, (1, SLOTS), 1)

    def s(k):
        return jnp.sum(jnp.where(line == k, total, 0.0), axis=1, keepdims=True)

    c0, c1 = steps(s(0), s(1), s(2), s(3))
    m_uu = [s(4 + k) for k in range(4)]
    m_uf = [s(8 + k) for k in range(5)]
    m_ff = [s(13 + k) for k in range(6)]
    moments = [
        m_uu[k] - 2.0 * (c0 * m_uf[k] + c1 * m_uf[k + 1])
        + (c0 * c0) * m_ff[k] + (2.0 * c0 * c1) * m_ff[k + 1] + (c1 * c1) * m_ff[k + 2]
        for k in range(4)
    ]
    e0, e1 = steps(*moments)
    coef = (e0, e1, -e0 * c0, -(e0 * c1 + e1 * c0), -e1 * c1, -c0, -c1)

    def meet(k):
        value = coef[0] * s(19 + 7 * k)
        for j in range(1, 7):
            value = value + coef[j] * s(19 + 7 * k + j)
        return value

    scale = 1.0 / (256 * 64 * 256)
    g0 = DT * s(40)
    g1 = DT * (s(41) - meet(0))
    g2 = DT * (s(42) - meet(1))
    g3 = -((DT * mobility) * s(44) + (DT * tension) * (s(43) - meet(2)))
    place = lax.broadcasted_iota(jnp.int32, (1, CY), 1)
    packed = jnp.where(place == 0, g0, jnp.where(place == 1, g1, jnp.where(place == 2, g2, g3)))
    params[...] = packed * scale

    def combine(t):
        value = coef[0] * uu[t + 1] + coef[1] * au[t] + coef[2] * f[t + 2] + coef[3] * af[t + 1]
        phi[t + 1] = value + coef[4] * a2f[t] + coef[5] * bb[t + 4] + coef[6] * ab[t + 1]

    loop(6, combine)
    rows = near
    a_lo, a_hi = low_high(c, ri, si, 4)
    u_lo, u_hi = low_high(c, ri, si, 5)
    for t, a2, a1 in ((0, a_lo, u_lo), (7, a_hi, u_hi)):
        value = coef[0] * uu[t, rows] + coef[1] * a1 + coef[2] * f[t + 1, rows] + coef[3] * af[t, rows]
        phi[t, rows] = value + coef[4] * a2 + coef[5] * bb[t + 3, rows] + coef[6] * ab[t, rows]

    def at(field, z):
        return e[BASE[field] + HALO[field] + z]

    def project(t):
        c = phi[t + 1]
        r0 = q[0, t] + 0.5 * (phi[t + 2] - phi[t])
        r1 = qe[0, t] + dx(c)
        r2 = qe[1, t] + dy(c)
        pr[0, t] = r0
        pr[1, t] = r1
        pr[2, t] = r2
        d = adj[t + 1]
        lap = adj[t + 2] + adj[t] + (x_up(d) + x_dn(d)) + (y_up(d) + y_dn(d)) - 6.0 * d
        pa[t] = (DT * mobility) * lap + (DT * tension) * (r0 * g[0, t] + r1 * g[1, t] + r2 * g[2, t])

    loop(6, project)

    def finish(t):
        v0, v1, v2 = at(V0, t), at(V1, t), at(V2, t)
        v0u, v0d = at(V0, t + 1), at(V0, t - 1)
        c = adj[t + 2]
        here = pot[t + 2]
        ph = at(PH, t)
        lam = pa[t + 1]
        lap = pa[t + 2] + pa[t] + (x_up(lam) + x_dn(lam)) + (y_up(lam) + y_dn(lam)) - 6.0 * lam
        up = v0u * adj[t + 3] - tension * (pot[t + 3] * pr[0, t + 2])
        dn = v0d * adj[t + 1] - tension * (pot[t + 1] * pr[0, t])
        div = 0.5 * (up - dn)
        div = div + dx(v1 * c - tension * (here * pr[1, t + 1]))
        div = div + dy(v2 * c - tension * (here * pr[2, t + 1]))
        value = c + DT * div + (3.0 * ph * ph - 1.0) * lam - interface * lap
        phase_back[t] = own(value)
        r = [pr[i, t + 1] for i in range(3)]
        vel = (v0, v1, v2)
        grads = [[], [], []]
        for i, field in enumerate((V0, V1, V2)):
            grads[0].append(0.5 * (at(field, t + 1) - at(field, t - 1)))
            grads[1].append(dx(vel[i]))
            grads[2].append(dy(vel[i]))
        for k in range(3):
            mix = r[0] * grads[k][0] + r[1] * grads[k][1] + r[2] * grads[k][2]
            ru, rd = pr[k, t + 2], pr[k, t]
            moved = (viscosity + 0.5 * v0u) * ru + (viscosity - 0.5 * v0d) * rd
            moved = moved + x_up((viscosity + 0.5 * v1) * r[k]) + x_dn((viscosity - 0.5 * v1) * r[k])
            moved = moved + y_up((viscosity + 0.5 * v2) * r[k]) + y_dn((viscosity - 0.5 * v2) * r[k])
            moved = moved - (6.0 * viscosity) * r[k]
            value = r[k] + DT * (moved - mix - c * g[k, t + 1])
            velocity_back[k, t] = own(value)

    loop(4, finish)


def f32(*shape):
    return jax.ShapeDtypeStruct(shape, jnp.float32)


def layers(*lead):
    return f32(*lead, ROWS, LANES)


def scratch(*lead):
    return pltpu.VMEM((*lead, ROWS, LANES), jnp.float32)


VM = pl.BlockSpec(memory_space=pltpu.VMEM)
SM = pl.BlockSpec(memory_space=pltpu.SMEM)
PARAMS = pltpu.CompilerParams(vmem_limit_bytes=12 * 1024 * 1024)
SWAP = [(0, 1), (1, 0)]


def role_shift(value, cross):
    gx, gy, gz = (lax.axis_size(a) for a in ("gx", "gy", "gz"))
    pairs = []
    for x in range(gx):
        for y in range(gy):
            for i in range(gz):
                target = (1 - x if cross else x, y, (i + 1 - 2 * y) % gz)
                pairs.append(((x * gy + y) * gz + i, (target[0] * gy + y) * gz + target[2]))
    return lax.ppermute(value, ("gx", "gy", "gz"), pairs)


def ring(value, step):
    count = lax.axis_size("gz")
    return lax.ppermute(value, "gz", [(i, (i + step) % count) for i in range(count)])


def swap(value):
    return lax.ppermute(value, "gy", SWAP)


def call(kernel, outs, ins, scratches, name, smem):
    return pl.pallas_call(
        kernel,
        out_shape=outs,
        in_specs=[SM] * smem + [VM] * (len(ins) - smem),
        out_specs=jax.tree.map(lambda _: VM, outs),
        scratch_shapes=scratches,
        compiler_params=PARAMS,
        name=name,
    )(*ins)


def local(phase, velocity, phase_obs, velocity_obs, coefs):
    core = lax.axis_index("gy").astype(jnp.int32).reshape(1)
    mine = (velocity, phase, phase_obs, velocity_obs)
    theirs = lax.optimization_barrier(tuple(swap(a) for a in mine))
    stack, edges, coefs = pl.pallas_call(
        load_kernel,
        out_shape=(f32(8 * CZ, CX, CY), f32(6 * CZ, 2 * HX, CY), f32(4)),
        in_specs=[pl.BlockSpec(memory_space=pltpu.HBM)] * 5,
        out_specs=(VM, VM, VM),
        scratch_shapes=[pltpu.SemaphoreType.DMA((9,))],
        compiler_params=PARAMS,
        name="load",
    )(*mine, coefs)
    gxr = lax.ppermute(edges, "gx", SWAP)
    main, diag = call(
        pack_kernel,
        (f32(SENT, CX, LANES), f32(SENT, 2 * HX, LANES)),
        (core, stack, theirs[0], theirs[1], theirs[3]),
        [],
        "pack",
        1,
    )
    mr = role_shift(main, False)
    dr = role_shift(diag, True)
    gxs = swap(gxr)
    ms, ds = swap(mr), swap(dr)
    narrow = ROWS - 2 * NEAR
    e, b, u, q, pot, lph, g, lv, send = call(
        first_kernel,
        (layers(TOTAL), layers(6), layers(4), layers(3, 6), layers(8), layers(8), layers(3, 6), layers(3, 8),
         f32(6, narrow, LANES)),
        (coefs, core, stack, *theirs, gxr, gxs, mr, ms, dr, ds),
        [scratch(8), scratch(6), scratch(6)],
        "first",
        2,
    )
    r2 = role_shift(send, False)
    adj, w, part, edge = call(
        weight_kernel,
        (layers(4), f32(3, CZ, CX, CY), f32(5, 8, CY), f32(2, 4, narrow, LANES)),
        (coefs, e, q, pot, lph, g, lv),
        [],
        "weights",
        1,
    )
    r2, w, part, edge = lax.optimization_barrier((r2, w, part, edge))
    s2 = swap(r2)
    sums, bb, uu, f, af, a2f, ab, au, send = call(
        moment_kernel,
        (f32(DEVICES, SLOTS), layers(14), layers(8), layers(10), layers(8), layers(6), layers(8), layers(6),
         f32(6, narrow, LANES)),
        (core, b, u, r2, s2, w, part, edge),
        [scratch(4), scratch(4), scratch(4)],
        "moments",
        1,
    )
    ri = role_shift(send, False)
    gathered = lax.all_to_all(sums.reshape(DEVICES, 1, SLOTS), ("gx", "gy", "gz"), 0, 0).reshape(DEVICES, SLOTS)
    ri, gathered = lax.optimization_barrier((ri, gathered))
    si = swap(ri)
    phase_back, velocity_back, params = call(
        last_kernel,
        (f32(CZ, CX, CY), f32(3, CZ, CX, CY), f32(1, CY)),
        (coefs, core, gathered, bb, uu, f, af, a2f, ab, au, ri, si, e, q, adj, pot, g),
        [scratch(8), scratch(3, 6), scratch(6), scratch(8), scratch(2, 6)],
        "last",
        2,
    )
    return phase_back, velocity_back, params[0, :4]


def solution(mesh):
    return jax.shard_map(
        local,
        mesh=mesh,
        in_specs=(
            P("gz", "gx", "gy"),
            P(None, "gz", "gx", "gy"),
            P("gz", "gx", "gy"),
            P(None, "gz", "gx", "gy"),
            P(),
        ),
        out_specs=(P("gz", "gx", "gy"), P(None, "gz", "gx", "gy"), P()),
        check_vma=False,
    )
```

```python
import jax
import jax.numpy as jnp
from jax import lax
from jax.experimental import pallas as pl
from jax.experimental.pallas import tpu as pltpu
from jax.sharding import PartitionSpec as P

DT = 0.1
SHIFT = 0.01
CZ, CX, CY = 4, 32, 128
HX = 8
NEAR = 4
NARROW = (CX + 2 * HX) - 2 * NEAR
ROWS = CX + 2 * HX
LANES = 2 * CY
DEVICES = 256

V0, V1, V2, PH, PO, O0, O1, O2 = range(8)
HALO = (2, 1, 1, 2, 0, 1, 0, 0)
BASE = []
_at = 0
for _h in HALO:
    BASE.append(_at)
    _at += CZ + 2 * _h
TOTAL = _at
SENT = sum(HALO)
NUM_SUMS = 45
SLOTS = 64


def x_up(a):
    return pltpu.roll(a, a.shape[0] - 1, 0)


def x_dn(a):
    return pltpu.roll(a, 1, 0)


def y_up(a):
    return pltpu.roll(a, a.shape[1] - 1, 1)


def y_dn(a):
    return pltpu.roll(a, 1, 1)


def dx(a):
    return 0.5 * (x_up(a) - x_dn(a))


def dy(a):
    return 0.5 * (y_up(a) - y_dn(a))


def own(a):
    return a[HX : HX + CX, :CY]


def lap_of(c, zu, zd):
    return (zu + zd) + (x_up(c) + x_dn(c)) + (y_up(c) + y_dn(c)) - 6.0 * c


def other_first(a):
    return jnp.concatenate([a[:, CY:], a[:, :CY]], 1)


def loop(count, body):
    def step(t, carry):
        body(t)
        return carry

    lax.fori_loop(0, count, step, 0, unroll=2)


def low_high(core, mine, theirs, j):
    a, b = mine[j], other_first(theirs[j])
    return jnp.where(core == 0, a, b), jnp.where(core == 0, b, a)


def load_kernel(vel, ph, po, vo, coefs, stack, out, coefs_out, sems):
    copies = [
        pltpu.make_async_copy(ph, stack.at[pl.ds(CZ * PH, CZ)], sems.at[6]),
        pltpu.make_async_copy(po, stack.at[pl.ds(CZ * PO, CZ)], sems.at[7]),
        pltpu.make_async_copy(coefs, coefs_out, sems.at[8]),
    ]
    for i in range(3):
        copies.append(pltpu.make_async_copy(vel.at[i], stack.at[pl.ds(CZ * (V0 + i), CZ)], sems.at[i]))
        copies.append(pltpu.make_async_copy(vo.at[i], stack.at[pl.ds(CZ * (O0 + i), CZ)], sems.at[3 + i]))
    for copy in copies:
        copy.start()
    for copy in copies:
        copy.wait()
    wide = CZ * PO
    out[0:wide, 0:HX] = stack[0:wide, CX - HX :]
    out[0:wide, HX:] = stack[0:wide, :HX]
    for n in range(wide):
        at, row = wide + n // 2, HX * (n % 2)
        out[at, row : row + NEAR] = stack[wide + n, CX - NEAR :]
        out[at, row + NEAR : row + HX] = stack[wide + n, :NEAR]


def pack_kernel(core, stack, peer, main, diag):
    c = core[0]
    n = 0
    for f, h in enumerate(HALO):
        for j in range(h):
            z = j + (CZ - h) * (1 - c)
            for half in range(2):
                src = (stack, peer)[half][CZ * f + z]
                lanes = pl.ds(CY * half, CY)
                main[n, :, lanes] = src
                diag[n, 0:HX, lanes] = src[CX - HX :]
                diag[n, HX:, lanes] = src[:HX]
            n += 1


def inner_kernel(stack, peer, gxr, gxs, e):
    for f, h in enumerate(HALO):
        mid = BASE[f] + h
        for z in range(CZ):
            for half, x in enumerate((gxr, gxs)):
                src = (stack, peer)[half][CZ * f + z]
                lanes = pl.ds(CY * half, CY)
                e[mid + z, HX : HX + CX, lanes] = src
                if f <= PH:
                    e[mid + z, 0:HX, lanes] = x[CZ * f + z, 0:HX]
                    e[mid + z, HX + CX :, lanes] = x[CZ * f + z, HX:]
                else:
                    k = CZ * (f - PO) + z
                    pair, row = CZ * PO + k // 2, HX * (k % 2)
                    e[mid + z, HX - NEAR : HX, lanes] = x[pair, row : row + NEAR]
                    e[mid + z, HX + CX : HX + CX + NEAR, lanes] = x[pair, row + NEAR : row + HX]


def first_kernel(
    coefs, core, inner, mr, ms, dr, ds, e, b, u, q, pot, lph, g, lv, send, far, p0,
):
    tension = 0.5 * coefs[1]
    viscosity = 0.1 * coefs[2]
    interface = 0.5 * coefs[3]
    c = core[0]

    n = 0
    for f, h in enumerate(HALO):
        high = BASE[f] + h + CZ
        for j in range(h):
            lo, hi = low_high(c, mr, ms, n)
            e[BASE[f] + j, HX : HX + CX] = lo
            e[high + j, HX : HX + CX] = hi
            lo, hi = low_high(c, dr, ds, n)
            e[BASE[f] + j, 0:HX] = lo[0:HX]
            e[BASE[f] + j, HX + CX :] = lo[HX:]
            e[high + j, 0:HX] = hi[0:HX]
            e[high + j, HX + CX :] = hi[HX:]
            n += 1

    def at(field, z):
        return e[BASE[field] + HALO[field] + z]

    def potential(t):
        z = t - 1
        a = at(PH, z)
        lap = lap_of(a, at(PH, z + 1), at(PH, z - 1))
        lph[t] = lap
        pot[t] = a * a * a - a - interface * lap

    loop(6, potential)

    def provisional(field, z, grad, here):
        a = at(field, z)
        zu, zd = at(field, z + 1), at(field, z - 1)
        xu, xd, yu, yd = x_up(a), x_dn(a), y_up(a), y_dn(a)
        lap = (zu + zd) + (xu + xd) + (yu + yd) - 6.0 * a
        advect = at(V0, z) * (zu - zd) + at(V1, z) * (xu - xd) + at(V2, z) * (yu - yd)
        value = a - (0.5 * DT) * advect + (DT * viscosity) * lap + (DT * tension) * (here * grad)
        return value, lap

    def along(t):
        z = t - 1
        grad = 0.5 * (at(PH, z + 1) - at(PH, z - 1))
        p0[t], lv[0, t] = provisional(V0, z, grad, pot[t])

    loop(6, along)

    def slopes(t):
        z = t - 1
        a = at(PH, z)
        g[0, t] = 0.5 * (at(PH, z + 1) - at(PH, z - 1))
        g[1, t] = dx(a)
        g[2, t] = dy(a)
        q[0, t] = p0[t] - at(O0, z)

    loop(6, slopes)

    def across(z):
        here = pot[z + 1]
        p1, lv[1, z] = provisional(V1, z, g[1, z + 1], here)
        p2, lv[2, z] = provisional(V2, z, g[2, z + 1], here)
        b[z] = -(0.5 * (p0[z + 2] - p0[z]) + dx(p1) + dy(p2))
        q1 = p1 - at(O1, z)
        q2 = p2 - at(O2, z)
        q[1, z + 1] = q1
        q[2, z + 1] = q2
        u[z] = 0.5 * (q[0, z + 2] - q[0, z]) + dx(q1) + dy(q2)

    loop(4, across)

    inside = pl.ds(NEAR, NARROW)
    for j in range(4):
        send[NARROW * j : NARROW * (j + 1)] = b[j, inside]
    for j in range(2):
        send[NARROW * (4 + j) : NARROW * (5 + j)] = u[j + 2 * (1 - c), inside]
    edge = 3 * (1 - c)
    send[NARROW * 6 : NARROW * 6 + 1] = b[edge, NEAR - 1 : NEAR]
    send[NARROW * 6 + 1 : NARROW * 6 + 2] = b[edge, ROWS - NEAR : ROWS - NEAR + 1]
    far[...] = b[0, HX : HX + CX, :CY]


def rows_of(a):
    return (a[0:8] + a[8:16]) + (a[16:24] + a[24:32])


def weight_kernel(coefs, e, q, pot, lph, g, lv, adj, w, part, edge):
    mobility = 0.1 * coefs[0]

    def at(field, z):
        return e[BASE[field] + HALO[field] + z]

    sums = [jnp.zeros((8, CY), jnp.float32)] * 5
    for t in range(CZ):
        here = pot[t + 1]
        lap = lph[t + 1]
        gs = [g[i, t + 1] for i in range(3)]
        up, dn = pot[t + 2] * g[0, t + 2], pot[t] * g[0, t]
        w1 = 0.5 * (up - dn) + dx(here * gs[1]) + dy(here * gs[2])
        w2 = 0.5 * (lv[0, t + 2] - lv[0, t]) + dx(lv[1, t]) + dy(lv[2, t])
        up, dn = lph[t + 2] * g[0, t + 2], lph[t] * g[0, t]
        w3 = 0.5 * (up - dn) + dx(lap * gs[1]) + dy(lap * gs[2])
        w[0, t] = own(w1)
        w[1, t] = own(w2)
        w[2, t] = own(w3)
        lap_pot = lap_of(here, pot[t + 2], pot[t])
        lap_lap = lap_of(lap, lph[t + 2], lph[t])
        flow = at(V0, t) * gs[0] + at(V1, t) * gs[1] + at(V2, t) * gs[2]
        c = at(PH, t) - DT * flow + (DT * mobility) * lap_pot - at(PO, t)
        adj[t] = c
        qs = [q[i, t + 1] for i in range(3)]
        qg = qs[0] * gs[0] + qs[1] * gs[1] + qs[2] * gs[2]
        ql = qs[0] * lv[0, t + 1] + qs[1] * lv[1, t] + qs[2] * lv[2, t]
        terms = (own(c * lap_pot), own(here * qg), own(ql), own(lap * qg), own(c * lap_lap))
        sums = [s + rows_of(a) for s, a in zip(sums, terms)]
    for k in range(5):
        part[k] = sums[k]
    for k, z in ((0, CZ - 1), (1, 0)):
        edge[k, 0] = q[1, z + 1, NEAR : ROWS - NEAR]
        edge[k, 1] = q[2, z + 1, NEAR : ROWS - NEAR]
        for j in range(2):
            edge[k, 2 + j] = adj[2 * (1 - k) + j, NEAR : ROWS - NEAR]


def shifted(c, zu, zd):
    return (6.0 + SHIFT) * c - ((zu + zd) + (x_up(c) + x_dn(c)) + (y_up(c) + y_dn(c)))


def moment_kernel(core, b4, u4, r, s, far, w, part, edge, out, bb, uu, f, af, a2f, ab, au, send, a2b, a2u):
    c = core[0]
    near = pl.ds(NEAR, NARROW)

    def got(first, count):
        mine, theirs = r[first : first + count], other_first(s[first : first + count])
        return jnp.where(c == 0, mine, theirs), jnp.where(c == 0, theirs, mine)

    for j in range(4):
        lo, hi = got(NARROW * j, NARROW)
        bb[j, near] = lo
        bb[8 + j, near] = hi
    for j in range(2):
        lo, hi = got(NARROW * (4 + j), NARROW)
        uu[j, near] = lo
        uu[6 + j, near] = hi
    lo, hi = got(NARROW * 6, 8)
    for z, rim in ((3, lo), (8, hi)):
        bb[z, NEAR - 1 : NEAR] = rim[0:1]
        bb[z, ROWS - NEAR : ROWS - NEAR + 1] = rim[1:2]
    bb[12, HX : HX + CX, :CY] = far[...]
    bb[4:8] = b4[...]
    uu[2:6] = u4[...]

    def wide(t):
        a = bb[t + 2]
        across = (pltpu.roll(a, ROWS - 2, 0) + pltpu.roll(a, 2, 0)) + (
            pltpu.roll(a, LANES - 2, 1) + pltpu.roll(a, 2, 1)
        )
        f[t] = 0.25 * ((bb[t + 4] + bb[t]) + across) - 1.5 * a

    loop(9, wide)

    def apply(src, dst, count):
        def body(t):
            dst[t] = shifted(src[t + 1], src[t + 2], src[t])

        loop(count, body)

    apply(f, af, 7)
    apply(af, a2f, 5)
    apply(bb.at[pl.ds(1, 10)], ab, 8)
    apply(ab.at[pl.ds(1, 6)], a2b, 4)
    apply(uu, au, 6)
    apply(au, a2u, 4)

    rows = pl.ds(HX, CX)
    lanes = pl.ds(0, CY)
    acc = [jnp.zeros((8, CY), jnp.float32)] * 40
    for t in range(CZ):
        vb, vab, va2b = bb[t + 4, rows, lanes], ab[t + 2, rows, lanes], a2b[t, rows, lanes]
        vu, vau, va2u = uu[t + 2, rows, lanes], au[t + 1, rows, lanes], a2u[t, rows, lanes]
        vf, vaf, va2f = f[t + 2, rows, lanes], af[t + 1, rows, lanes], a2f[t, rows, lanes]
        a = a2f[t]
        across = (x_up(a) + x_dn(a)) + (y_up(a) + y_dn(a))
        va3f = (6.0 + SHIFT) * va2f - (2.0 * a2f[t + 1, rows, lanes] + own(across))
        terms = [
            vb * vb, vb * vab, vab * vab, vab * va2b,
            vu * vu, vu * vau, vau * vau, vau * va2u,
            vu * vf, vu * vaf, vu * va2f, vau * va2f, va2u * va2f,
            vf * vf, vf * vaf, vaf * vaf, vaf * va2f, va2f * va2f, va2f * va3f,
        ]
        for k in range(3):
            wk = w[k, t]
            terms += [a * wk for a in (vu, vau, vf, vaf, va2f, vb, vab)]
        acc = [x + rows_of(a) for x, a in zip(acc, terms)]
    rows_list = [jnp.sum(a, axis=0, keepdims=True) for a in acc]
    rows_list += [jnp.sum(part[k], axis=0, keepdims=True) for k in range(5)]
    rows_list += [jnp.zeros((1, CY), jnp.float32)] * (48 - NUM_SUMS)
    table = jnp.concatenate(rows_list, axis=0)
    totals = jnp.sum(table, axis=1, keepdims=True)
    line = lax.broadcasted_iota(jnp.int32, (48, SLOTS), 1)
    which = lax.broadcasted_iota(jnp.int32, (48, SLOTS), 0)
    row = jnp.sum(jnp.where(line == which, totals, 0.0), axis=0, keepdims=True)
    out[...] = jnp.broadcast_to(row, (DEVICES, SLOTS))
    send[0:4] = edge[c]
    first = 2 * (1 - c)
    send[4] = a2f[first, near]
    send[5] = a2f[first + 1, near]
    send[6] = af[3 - c, near]
    send[7] = au[3 - c, near]


def steps(m0, m1, m2, m3):
    alpha = m0 / m1
    norm = m0 * ((m0 * m2) / (m1 * m1) - 1.0)
    beta = norm / m0
    one = 1.0 + beta
    curve = one * one * m1 - 2.0 * one * alpha * m2 + alpha * alpha * m3
    second = norm / curve
    return alpha + second * one, -second * alpha


def last_kernel(
    coefs, core, gathered, bb, uu, f, af, a2f, ab, au, ri, si, e, q, adj4, pot, g,
    phase_back, velocity_back, params, phi, pr, pa, adj, qe, a2e, afe, aue,
):
    c = core[0]
    near = pl.ds(NEAR, ROWS - 2 * NEAR)
    for i in range(2):
        lo, hi = low_high(c, ri, si, i)
        qe[i, 0, near] = lo
        qe[i, 5, near] = hi
        qe[i, 1:5] = q[i + 1, 1:5]
        lo, hi = low_high(c, ri, si, 2 + i)
        adj[i, near] = lo
        adj[6 + i, near] = hi
    adj[2:6] = adj4[...]
    mobility = 0.1 * coefs[0]
    tension = 0.5 * coefs[1]
    viscosity = 0.1 * coefs[2]
    interface = 0.5 * coefs[3]

    total = jnp.sum(gathered[...], axis=0, keepdims=True)
    line = lax.broadcasted_iota(jnp.int32, (1, SLOTS), 1)

    def s(k):
        return jnp.sum(jnp.where(line == k, total, 0.0), axis=1, keepdims=True)

    c0, c1 = steps(s(0), s(1), s(2), s(3))
    m_uu = [s(4 + k) for k in range(4)]
    m_uf = [s(8 + k) for k in range(5)]
    m_ff = [s(13 + k) for k in range(6)]
    moments = [
        m_uu[k] - 2.0 * (c0 * m_uf[k] + c1 * m_uf[k + 1])
        + (c0 * c0) * m_ff[k] + (2.0 * c0 * c1) * m_ff[k + 1] + (c1 * c1) * m_ff[k + 2]
        for k in range(4)
    ]
    e0, e1 = steps(*moments)
    coef = (e0, e1, -e0 * c0, -(e0 * c1 + e1 * c0), -e1 * c1, -c0, -c1)

    def meet(k):
        value = coef[0] * s(19 + 7 * k)
        for j in range(1, 7):
            value = value + coef[j] * s(19 + 7 * k + j)
        return value

    scale = 1.0 / (256 * 64 * 256)
    g0 = DT * s(40)
    g1 = DT * (s(41) - meet(0))
    g2 = DT * (s(42) - meet(1))
    g3 = -((DT * mobility) * s(44) + (DT * tension) * (s(43) - meet(2)))
    place = lax.broadcasted_iota(jnp.int32, (1, CY), 1)
    packed = jnp.where(place == 0, g0, jnp.where(place == 1, g1, jnp.where(place == 2, g2, g3)))
    params[...] = (packed * scale)[0, 0:4]

    for j in range(2):
        lo, hi = low_high(c, ri, si, 4 + j)
        a2e[j, near] = lo
        a2e[6 + j, near] = hi
    a2e[2:6] = a2f[0:4]
    for j, (src, dst) in enumerate(((af, afe), (au, aue))):
        lo, hi = low_high(c, ri, si, 6 + j)
        dst[0, near] = lo
        dst[7, near] = hi
        dst[1:7] = src[0:6]

    def combine(t):
        value = coef[0] * uu[t] + coef[1] * aue[t] + coef[2] * f[t] + coef[3] * afe[t]
        phi[t] = value + coef[4] * a2e[t] + coef[5] * bb[t + 2] + coef[6] * ab[t]

    loop(8, combine)

    def at(field, z):
        return e[BASE[field] + HALO[field] + z]

    def project(t):
        c = phi[t + 1]
        r0 = q[0, t] + 0.5 * (phi[t + 2] - phi[t])
        r1 = qe[0, t] + dx(c)
        r2 = qe[1, t] + dy(c)
        pr[0, t] = r0
        pr[1, t] = r1
        pr[2, t] = r2
        d = adj[t + 1]
        lap = adj[t + 2] + adj[t] + (x_up(d) + x_dn(d)) + (y_up(d) + y_dn(d)) - 6.0 * d
        pa[t] = (DT * mobility) * lap + (DT * tension) * (r0 * g[0, t] + r1 * g[1, t] + r2 * g[2, t])

    loop(6, project)

    def finish(t):
        v0, v1, v2 = at(V0, t), at(V1, t), at(V2, t)
        v0u, v0d = at(V0, t + 1), at(V0, t - 1)
        c = adj[t + 2]
        here = pot[t + 1]
        ph = at(PH, t)
        lam = pa[t + 1]
        lap = pa[t + 2] + pa[t] + (x_up(lam) + x_dn(lam)) + (y_up(lam) + y_dn(lam)) - 6.0 * lam
        up = v0u * adj[t + 3] - tension * (pot[t + 2] * pr[0, t + 2])
        dn = v0d * adj[t + 1] - tension * (pot[t] * pr[0, t])
        div = 0.5 * (up - dn)
        div = div + dx(v1 * c - tension * (here * pr[1, t + 1]))
        div = div + dy(v2 * c - tension * (here * pr[2, t + 1]))
        value = c + DT * div + (3.0 * ph * ph - 1.0) * lam - interface * lap
        phase_back[t] = own(value)
        r = [pr[i, t + 1] for i in range(3)]
        vel = (v0, v1, v2)
        grads = [[], [], []]
        for i, field in enumerate((V0, V1, V2)):
            grads[0].append(0.5 * (at(field, t + 1) - at(field, t - 1)))
            grads[1].append(dx(vel[i]))
            grads[2].append(dy(vel[i]))
        for k in range(3):
            mix = r[0] * grads[k][0] + r[1] * grads[k][1] + r[2] * grads[k][2]
            ru, rd = pr[k, t + 2], pr[k, t]
            moved = (viscosity + 0.5 * v0u) * ru + (viscosity - 0.5 * v0d) * rd
            moved = moved + x_up((viscosity + 0.5 * v1) * r[k]) + x_dn((viscosity - 0.5 * v1) * r[k])
            moved = moved + y_up((viscosity + 0.5 * v2) * r[k]) + y_dn((viscosity - 0.5 * v2) * r[k])
            moved = moved - (6.0 * viscosity) * r[k]
            value = r[k] + DT * (moved - mix - c * g[k, t + 1])
            velocity_back[k, t] = own(value)

    loop(4, finish)


def f32(*shape):
    return jax.ShapeDtypeStruct(shape, jnp.float32)


def layers(*lead):
    return f32(*lead, ROWS, LANES)


def scratch(*lead):
    return pltpu.VMEM((*lead, ROWS, LANES), jnp.float32)


VM = pl.BlockSpec(memory_space=pltpu.VMEM)
SM = pl.BlockSpec(memory_space=pltpu.SMEM)
PARAMS = pltpu.CompilerParams(vmem_limit_bytes=12 * 1024 * 1024)
SWAP = [(0, 1), (1, 0)]


def role_shift(value, cross):
    gx, gy, gz = (lax.axis_size(a) for a in ("gx", "gy", "gz"))
    pairs = []
    for x in range(gx):
        for y in range(gy):
            for i in range(gz):
                target = (1 - x if cross else x, y, (i + 1 - 2 * y) % gz)
                pairs.append(((x * gy + y) * gz + i, (target[0] * gy + y) * gz + target[2]))
    return lax.ppermute(value, ("gx", "gy", "gz"), pairs)


def ring(value, step):
    count = lax.axis_size("gz")
    return lax.ppermute(value, "gz", [(i, (i + step) % count) for i in range(count)])


def swap(value):
    return lax.ppermute(value, "gy", SWAP)


def call(kernel, outs, ins, scratches, name, smem, aliases={}):
    return pl.pallas_call(
        kernel,
        out_shape=outs,
        in_specs=[SM] * smem + [VM] * (len(ins) - smem),
        out_specs=jax.tree.map(lambda _: VM, outs),
        scratch_shapes=scratches,
        input_output_aliases=aliases,
        compiler_params=PARAMS,
        name=name,
    )(*ins)


def local(phase, velocity, phase_obs, velocity_obs, coefs):
    core = lax.axis_index("gy").astype(jnp.int32).reshape(1)
    mine = (velocity, phase, phase_obs, velocity_obs)
    stack, edges, coefs = pl.pallas_call(
        load_kernel,
        out_shape=(f32(8 * CZ, CX, CY), f32(6 * CZ, 2 * HX, CY), f32(4)),
        in_specs=[pl.BlockSpec(memory_space=pltpu.HBM)] * 5,
        out_specs=(VM, VM, VM),
        scratch_shapes=[pltpu.SemaphoreType.DMA((9,))],
        compiler_params=PARAMS,
        name="load",
    )(*(pltpu.with_memory_space_constraint(a, pltpu.HBM) for a in (*mine, coefs)))
    peer = swap(stack)
    gxr = lax.ppermute(edges, "gx", SWAP)
    main, diag = call(
        pack_kernel,
        (f32(SENT, CX, LANES), f32(SENT, 2 * HX, LANES)),
        (core, stack, peer),
        [],
        "pack",
        1,
    )
    mr = role_shift(main, False)
    dr = role_shift(diag, True)
    gxs = swap(gxr)
    inner = call(inner_kernel, layers(TOTAL), (stack, peer, gxr, gxs), [], "inner", 0)
    mr, inner = lax.optimization_barrier((mr, inner))
    ms = swap(mr)
    ds = swap(dr)
    e, b, u, q, pot, lph, g, lv, send, far = call(
        first_kernel,
        (layers(TOTAL), layers(4), layers(4), layers(3, 6), layers(6), layers(6), layers(3, 6), layers(3, 6),
         f32(6 * NARROW + 8, LANES), f32(CX, CY)),
        (coefs, core, inner, mr, ms, dr, ds),
        [scratch(6)],
        "first",
        2,
        {2: 0},
    )
    r2 = role_shift(send, False)
    far = ring(far, -2)
    adj, w, part, edge = call(
        weight_kernel,
        (layers(4), f32(3, CZ, CX, CY), f32(5, 8, CY), f32(2, 4, NARROW, LANES)),
        (coefs, e, q, pot, lph, g, lv),
        [],
        "weights",
        1,
    )
    r2, far, w, part, edge = lax.optimization_barrier((r2, far, w, part, edge))
    s2 = swap(r2)
    sums, bb, uu, f, af, a2f, ab, au, send = call(
        moment_kernel,
        (f32(DEVICES, SLOTS), layers(13), layers(8), layers(9), layers(7), layers(5), layers(8), layers(6),
         f32(8, NARROW, LANES)),
        (core, b, u, r2, s2, far, w, part, edge),
        [scratch(4), scratch(4)],
        "moments",
        1,
    )
    ri = role_shift(send, False)
    gathered = lax.all_to_all(sums.reshape(DEVICES, 1, SLOTS), ("gx", "gy", "gz"), 0, 0).reshape(DEVICES, SLOTS)
    ri, gathered = lax.optimization_barrier((ri, gathered))
    si = swap(ri)
    phase_back, velocity_back, params = call(
        last_kernel,
        (f32(CZ, CX, CY), f32(3, CZ, CX, CY), f32(4)),
        (coefs, core, gathered, bb, uu, f, af, a2f, ab, au, ri, si, e, q, adj, pot, g),
        [scratch(8), scratch(3, 6), scratch(6), scratch(8), scratch(2, 6), scratch(8), scratch(8), scratch(8)],
        "last",
        2,
    )
    return phase_back, velocity_back, params


def solution(mesh):
    return jax.shard_map(
        local,
        mesh=mesh,
        in_specs=(
            P("gz", "gx", "gy"),
            P(None, "gz", "gx", "gy"),
            P("gz", "gx", "gy"),
            P(None, "gz", "gx", "gy"),
            P(),
        ),
        out_specs=(P("gz", "gx", "gy"), P(None, "gz", "gx", "gy"), P()),
        check_vma=False,
    )
```

```python
import jax
import jax.numpy as jnp
from jax import lax
from jax.experimental import pallas as pl
from jax.experimental.pallas import tpu as pltpu
from jax.sharding import PartitionSpec as P

DT = 0.1
SHIFT = 0.01
CZ, CX, CY = 4, 32, 128
HX = 8
NEAR = 4
UNROLL = 4
NARROW = (CX + 2 * HX) - 2 * NEAR
ROWS = CX + 2 * HX
LANES = 2 * CY
PARTNERS = 128

V0, V1, V2, PH, PO, O0, O1, O2 = range(8)
HALO = (2, 1, 1, 2, 0, 1, 0, 0)
BASE = []
_at = 0
for _h in HALO:
    BASE.append(_at)
    _at += CZ + 2 * _h
TOTAL = _at
SENT = [(f, k) for f, h in enumerate(HALO) for k in range(1, h + 1)]
CORNER = [3 if f == O0 else 8 - k for f, k in SENT]
CORNER_ROWS = -(-2 * sum(CORNER) // 8) * 8
AGAIN = [("b", k, 6 - k) for k in (1, 2, 3, 4)] + [("u", k, 3 - k) for k in (1, 2)]
AGAIN_ROWS = -(-sum(CX + 2 * w for _, _, w in AGAIN) // 8) * 8
NUM_SUMS = 45
SLOTS = 64


def x_up(a):
    return pltpu.roll(a, a.shape[0] - 1, 0)


def x_dn(a):
    return pltpu.roll(a, 1, 0)


def y_up(a):
    return pltpu.roll(a, a.shape[1] - 1, 1)


def y_dn(a):
    return pltpu.roll(a, 1, 1)


def dx(a):
    return 0.5 * (x_up(a) - x_dn(a))


def dy(a):
    return 0.5 * (y_up(a) - y_dn(a))


def own(a):
    return a[HX : HX + CX, :CY]


def lap_of(c, zu, zd):
    return (zu + zd) + (x_up(c) + x_dn(c)) + (y_up(c) + y_dn(c)) - 6.0 * c


def other_first(a):
    return jnp.concatenate([a[:, CY:], a[:, :CY]], 1)


def outgoing(core, k):
    return (CZ - k) * (1 - core) + (k - 1) * core


def loop(count, body):
    def step(t, carry):
        body(t)
        return carry

    lax.fori_loop(0, count, step, 0, unroll=UNROLL)


def low_high(core, mine, theirs):
    theirs = other_first(theirs)
    return jnp.where(core == 0, mine, theirs), jnp.where(core == 0, theirs, mine)


def load_kernel(vel, ph, po, vo, coefs, stack, out, coefs_out, give, sems):
    copies = [
        pltpu.make_async_copy(ph, stack.at[pl.ds(CZ * PH, CZ)], sems.at[6]),
        pltpu.make_async_copy(po, stack.at[pl.ds(CZ * PO, CZ)], sems.at[7]),
        pltpu.make_async_copy(coefs, coefs_out, sems.at[8]),
    ]
    for i in range(3):
        copies.append(pltpu.make_async_copy(vel.at[i], stack.at[pl.ds(CZ * (V0 + i), CZ)], sems.at[i]))
        copies.append(pltpu.make_async_copy(vo.at[i], stack.at[pl.ds(CZ * (O0 + i), CZ)], sems.at[3 + i]))
    for copy in copies:
        copy.start()
    for copy in copies:
        copy.wait()
    other = 1 - lax.axis_index("gy")
    for n, (f, k) in enumerate(SENT):
        give[n] = stack[CZ * f + outgoing(other, k)]
    wide = CZ * PO
    out[0:wide, 0:HX] = stack[0:wide, CX - HX :]
    out[0:wide, HX:] = stack[0:wide, :HX]
    for n in range(wide):
        at, row = wide + n // 2, HX * (n % 2)
        out[at, row : row + NEAR] = stack[wide + n, CX - NEAR :]
        out[at, row + NEAR : row + HX] = stack[wide + n, :NEAR]


def pack_kernel(stack, got, main, diag):
    c = lax.axis_index("gy")
    row = 0
    for n, (f, k) in enumerate(SENT):
        src = jnp.concatenate([stack[CZ * f + outgoing(c, k)], got[n]], 1)
        main[n] = src
        w = CORNER[n]
        diag[row : row + w] = src[CX - w :]
        diag[row + w : row + 2 * w] = src[:w]
        row += 2 * w


def inner_kernel(stack, peer, gxr, gxs, e):
    for f, h in enumerate(HALO):
        mid = BASE[f] + h
        for z in range(CZ):
            for half, x in enumerate((gxr, gxs)):
                src = (stack, peer)[half][CZ * f + z]
                lanes = pl.ds(CY * half, CY)
                e[mid + z, HX : HX + CX, lanes] = src
                if f <= PH:
                    e[mid + z, 0:HX, lanes] = x[CZ * f + z, 0:HX]
                    e[mid + z, HX + CX :, lanes] = x[CZ * f + z, HX:]
                else:
                    k = CZ * (f - PO) + z
                    pair, row = CZ * PO + k // 2, HX * (k % 2)
                    e[mid + z, HX - NEAR : HX, lanes] = x[pair, row : row + NEAR]
                    e[mid + z, HX + CX : HX + CX + NEAR, lanes] = x[pair, row + NEAR : row + HX]


def first_kernel(coefs, inner, mr, ms, dr, ds, e, b, u, q, pot, lph, g, lv, send, far, p0):
    tension = 0.5 * coefs[1]
    viscosity = 0.1 * coefs[2]
    interface = 0.5 * coefs[3]
    c = lax.axis_index("gy")

    row = 0
    for n, (f, k) in enumerate(SENT):
        below, above = BASE[f] + HALO[f] - k, BASE[f] + HALO[f] + CZ + k - 1
        lo, hi = low_high(c, mr[n], ms[n])
        e[below, HX : HX + CX] = lo
        e[above, HX : HX + CX] = hi
        w = CORNER[n]
        lo, hi = low_high(c, dr[row : row + 2 * w], ds[row : row + 2 * w])
        for layer, part in ((below, lo), (above, hi)):
            e[layer, HX - w : HX] = part[:w]
            e[layer, HX + CX : HX + CX + w] = part[w:]
        row += 2 * w

    def at(field, z):
        return e[BASE[field] + HALO[field] + z]

    def potential(t):
        z = t - 1
        a = at(PH, z)
        lap = lap_of(a, at(PH, z + 1), at(PH, z - 1))
        lph[t] = lap
        pot[t] = a * a * a - a - interface * lap

    loop(6, potential)

    def provisional(field, z, grad, here):
        a = at(field, z)
        zu, zd = at(field, z + 1), at(field, z - 1)
        xu, xd, yu, yd = x_up(a), x_dn(a), y_up(a), y_dn(a)
        lap = (zu + zd) + (xu + xd) + (yu + yd) - 6.0 * a
        advect = at(V0, z) * (zu - zd) + at(V1, z) * (xu - xd) + at(V2, z) * (yu - yd)
        value = a - (0.5 * DT) * advect + (DT * viscosity) * lap + (DT * tension) * (here * grad)
        return value, lap

    def along(t):
        z = t - 1
        grad = 0.5 * (at(PH, z + 1) - at(PH, z - 1))
        p0[t], lv[0, t] = provisional(V0, z, grad, pot[t])

    loop(6, along)

    def slopes(t):
        z = t - 1
        a = at(PH, z)
        g[0, t] = 0.5 * (at(PH, z + 1) - at(PH, z - 1))
        g[1, t] = dx(a)
        g[2, t] = dy(a)
        q[0, t] = p0[t] - at(O0, z)

    loop(6, slopes)

    def across(z):
        here = pot[z + 1]
        p1, lv[1, z] = provisional(V1, z, g[1, z + 1], here)
        p2, lv[2, z] = provisional(V2, z, g[2, z + 1], here)
        b[z] = -(0.5 * (p0[z + 2] - p0[z]) + dx(p1) + dy(p2))
        q1 = p1 - at(O1, z)
        q2 = p2 - at(O2, z)
        q[1, z + 1] = q1
        q[2, z + 1] = q2
        u[z] = 0.5 * (q[0, z + 2] - q[0, z]) + dx(q1) + dy(q2)

    loop(4, across)

    row = 0
    for name, k, w in AGAIN:
        field = b if name == "b" else u
        rows = CX + 2 * w
        send[row : row + rows] = field[outgoing(c, k), HX - w : HX + CX + w]
        row += rows
    far[...] = b[0, HX : HX + CX]


def folded(a):
    a = a[:, :CY] + a[:, CY:]
    return (a[0:8] + a[8:16]) + (a[16:24] + a[24:32])


def middle(a):
    return a[HX : HX + CX]


def weight_kernel(coefs, e, q, pot, lph, g, lv, adj, w, part, edge):
    mobility = 0.1 * coefs[0]

    def at(field, z):
        return e[BASE[field] + HALO[field] + z]

    sums = [jnp.zeros((8, CY), jnp.float32)] * 5
    for t in range(CZ):
        here = pot[t + 1]
        lap = lph[t + 1]
        gs = [g[i, t + 1] for i in range(3)]
        up, dn = pot[t + 2] * g[0, t + 2], pot[t] * g[0, t]
        w1 = 0.5 * (up - dn) + dx(here * gs[1]) + dy(here * gs[2])
        w2 = 0.5 * (lv[0, t + 2] - lv[0, t]) + dx(lv[1, t]) + dy(lv[2, t])
        up, dn = lph[t + 2] * g[0, t + 2], lph[t] * g[0, t]
        w3 = 0.5 * (up - dn) + dx(lap * gs[1]) + dy(lap * gs[2])
        w[0, t] = middle(w1)
        w[1, t] = middle(w2)
        w[2, t] = middle(w3)
        lap_pot = lap_of(here, pot[t + 2], pot[t])
        lap_lap = lap_of(lap, lph[t + 2], lph[t])
        flow = at(V0, t) * gs[0] + at(V1, t) * gs[1] + at(V2, t) * gs[2]
        c = at(PH, t) - DT * flow + (DT * mobility) * lap_pot - at(PO, t)
        adj[t] = c
        qs = [q[i, t + 1] for i in range(3)]
        qg = qs[0] * gs[0] + qs[1] * gs[1] + qs[2] * gs[2]
        ql = qs[0] * lv[0, t + 1] + qs[1] * lv[1, t] + qs[2] * lv[2, t]
        terms = (middle(c * lap_pot), middle(here * qg), middle(ql), middle(lap * qg), middle(c * lap_lap))
        sums = [s + folded(a) for s, a in zip(sums, terms)]
    for k in range(5):
        part[k] = sums[k]
    for k, z in ((0, CZ - 1), (1, 0)):
        edge[k, 0] = q[1, z + 1, NEAR : ROWS - NEAR]
        edge[k, 1] = q[2, z + 1, NEAR : ROWS - NEAR]
        for j in range(2):
            edge[k, 2 + j] = adj[2 * (1 - k) + j, NEAR : ROWS - NEAR]


def shifted(c, zu, zd):
    return (6.0 + SHIFT) * c - ((zu + zd) + (x_up(c) + x_dn(c)) + (y_up(c) + y_dn(c)))


def moment_kernel(b4, u4, r, s, far, w, part, edge, out, bb, uu, f, af, a2f, ab, au, send, a2b, a2u):
    c = lax.axis_index("gy")
    near = pl.ds(NEAR, NARROW)
    row = 0
    for name, k, width in AGAIN:
        rows = CX + 2 * width
        lo, hi = low_high(c, r[row : row + rows], s[row : row + rows])
        dst, below = (bb, 4 - k) if name == "b" else (uu, 2 - k)
        above = 7 + k if name == "b" else 5 + k
        dst[below, HX - width : HX + CX + width] = lo
        dst[above, HX - width : HX + CX + width] = hi
        row += rows
    bb[12, HX : HX + CX] = far[...]
    bb[4:8] = b4[...]
    uu[2:6] = u4[...]

    def wide(t):
        a = bb[t + 2]
        across = (pltpu.roll(a, ROWS - 2, 0) + pltpu.roll(a, 2, 0)) + (
            pltpu.roll(a, LANES - 2, 1) + pltpu.roll(a, 2, 1)
        )
        f[t] = 0.25 * ((bb[t + 4] + bb[t]) + across) - 1.5 * a

    loop(9, wide)

    def apply(src, dst, count):
        def body(t):
            dst[t] = shifted(src[t + 1], src[t + 2], src[t])

        loop(count, body)

    apply(f, af, 7)
    apply(af, a2f, 5)
    apply(bb.at[pl.ds(1, 10)], ab, 8)
    apply(ab.at[pl.ds(1, 6)], a2b, 4)
    apply(uu, au, 6)
    apply(au, a2u, 4)

    rows = pl.ds(HX, CX)
    acc = [jnp.zeros((8, CY), jnp.float32)] * 40
    for t in range(CZ):
        vb, vab, va2b = bb[t + 4, rows], ab[t + 2, rows], a2b[t, rows]
        vu, vau, va2u = uu[t + 2, rows], au[t + 1, rows], a2u[t, rows]
        vf, vaf, va2f = f[t + 2, rows], af[t + 1, rows], a2f[t, rows]
        a = a2f[t]
        across = (x_up(a) + x_dn(a)) + (y_up(a) + y_dn(a))
        va3f = (6.0 + SHIFT) * va2f - (2.0 * a2f[t + 1, rows] + middle(across))
        terms = [
            vb * vb, vb * vab, vab * vab, vab * va2b,
            vu * vu, vu * vau, vau * vau, vau * va2u,
            vu * vf, vu * vaf, vu * va2f, vau * va2f, va2u * va2f,
            vf * vf, vf * vaf, vaf * vaf, vaf * va2f, va2f * va2f, va2f * va3f,
        ]
        for k in range(3):
            wk = w[k, t]
            terms += [a * wk for a in (vu, vau, vf, vaf, va2f, vb, vab)]
        acc = [x + folded(a) for x, a in zip(acc, terms)]
    rows_list = [jnp.sum(a, axis=0, keepdims=True) for a in acc]
    rows_list += [jnp.sum(part[k], axis=0, keepdims=True) for k in range(5)]
    rows_list += [jnp.zeros((1, CY), jnp.float32)] * (48 - NUM_SUMS)
    table = jnp.concatenate(rows_list, axis=0)
    totals = jnp.sum(table, axis=1, keepdims=True)
    line = lax.broadcasted_iota(jnp.int32, (48, SLOTS), 1)
    which = lax.broadcasted_iota(jnp.int32, (48, SLOTS), 0)
    row = jnp.sum(jnp.where(line == which, totals, 0.0), axis=0, keepdims=True)
    out[...] = jnp.broadcast_to(row, (PARTNERS, SLOTS))
    send[0:4] = edge[c]
    first = 2 * (1 - c)
    send[4] = a2f[first, near]
    send[5] = a2f[first + 1, near]
    send[6] = af[3 - c, near]
    send[7] = au[3 - c, near]


def steps(m0, m1, m2, m3):
    alpha = m0 / m1
    norm = m0 * ((m0 * m2) / (m1 * m1) - 1.0)
    beta = norm / m0
    one = 1.0 + beta
    curve = one * one * m1 - 2.0 * one * alpha * m2 + alpha * alpha * m3
    second = norm / curve
    return alpha + second * one, -second * alpha


def last_kernel(
    coefs, gathered, bb, uu, f, af, a2f, ab, au, ri, si, e, q, adj4, pot, g,
    phase_back, velocity_back, params, phi, pr, pa, adj, qe, a2e, afe, aue,
):
    c = lax.axis_index("gy")
    near = pl.ds(NEAR, NARROW)
    for i in range(2):
        lo, hi = low_high(c, ri[i], si[i])
        qe[i, 0, near] = lo
        qe[i, 5, near] = hi
        qe[i, 1:5] = q[i + 1, 1:5]
        lo, hi = low_high(c, ri[2 + i], si[2 + i])
        adj[i, near] = lo
        adj[6 + i, near] = hi
    adj[2:6] = adj4[...]
    mobility = 0.1 * coefs[0]
    tension = 0.5 * coefs[1]
    viscosity = 0.1 * coefs[2]
    interface = 0.5 * coefs[3]

    total = jnp.sum(gathered[...], axis=0, keepdims=True)
    line = lax.broadcasted_iota(jnp.int32, (1, SLOTS), 1)

    def s(k):
        return jnp.sum(jnp.where(line == k, total, 0.0), axis=1, keepdims=True)

    c0, c1 = steps(s(0), s(1), s(2), s(3))
    m_uu = [s(4 + k) for k in range(4)]
    m_uf = [s(8 + k) for k in range(5)]
    m_ff = [s(13 + k) for k in range(6)]
    moments = [
        m_uu[k] - 2.0 * (c0 * m_uf[k] + c1 * m_uf[k + 1])
        + (c0 * c0) * m_ff[k] + (2.0 * c0 * c1) * m_ff[k + 1] + (c1 * c1) * m_ff[k + 2]
        for k in range(4)
    ]
    e0, e1 = steps(*moments)
    coef = (e0, e1, -e0 * c0, -(e0 * c1 + e1 * c0), -e1 * c1, -c0, -c1)

    def meet(k):
        value = coef[0] * s(19 + 7 * k)
        for j in range(1, 7):
            value = value + coef[j] * s(19 + 7 * k + j)
        return value

    scale = 1.0 / (256 * 64 * 256)
    g0 = DT * s(40)
    g1 = DT * (s(41) - meet(0))
    g2 = DT * (s(42) - meet(1))
    g3 = -((DT * mobility) * s(44) + (DT * tension) * (s(43) - meet(2)))
    place = lax.broadcasted_iota(jnp.int32, (1, CY), 1)
    packed = jnp.where(place == 0, g0, jnp.where(place == 1, g1, jnp.where(place == 2, g2, g3)))
    params[...] = (packed * scale)[0, 0:4]

    for j in range(2):
        lo, hi = low_high(c, ri[4 + j], si[4 + j])
        a2e[j, near] = lo
        a2e[6 + j, near] = hi
    a2e[2:6] = a2f[0:4]
    for j, (src, dst) in enumerate(((af, afe), (au, aue))):
        lo, hi = low_high(c, ri[6 + j], si[6 + j])
        dst[0, near] = lo
        dst[7, near] = hi
        dst[1:7] = src[0:6]

    def combine(t):
        value = coef[0] * uu[t] + coef[1] * aue[t] + coef[2] * f[t] + coef[3] * afe[t]
        phi[t] = value + coef[4] * a2e[t] + coef[5] * bb[t + 2] + coef[6] * ab[t]

    loop(8, combine)

    def at(field, z):
        return e[BASE[field] + HALO[field] + z]

    def project(t):
        c = phi[t + 1]
        r0 = q[0, t] + 0.5 * (phi[t + 2] - phi[t])
        r1 = qe[0, t] + dx(c)
        r2 = qe[1, t] + dy(c)
        pr[0, t] = r0
        pr[1, t] = r1
        pr[2, t] = r2
        d = adj[t + 1]
        lap = adj[t + 2] + adj[t] + (x_up(d) + x_dn(d)) + (y_up(d) + y_dn(d)) - 6.0 * d
        pa[t] = (DT * mobility) * lap + (DT * tension) * (r0 * g[0, t] + r1 * g[1, t] + r2 * g[2, t])

    loop(6, project)

    def finish(t):
        v0, v1, v2 = at(V0, t), at(V1, t), at(V2, t)
        v0u, v0d = at(V0, t + 1), at(V0, t - 1)
        c = adj[t + 2]
        here = pot[t + 1]
        ph = at(PH, t)
        lam = pa[t + 1]
        lap = pa[t + 2] + pa[t] + (x_up(lam) + x_dn(lam)) + (y_up(lam) + y_dn(lam)) - 6.0 * lam
        up = v0u * adj[t + 3] - tension * (pot[t + 2] * pr[0, t + 2])
        dn = v0d * adj[t + 1] - tension * (pot[t] * pr[0, t])
        div = 0.5 * (up - dn)
        div = div + dx(v1 * c - tension * (here * pr[1, t + 1]))
        div = div + dy(v2 * c - tension * (here * pr[2, t + 1]))
        value = c + DT * div + (3.0 * ph * ph - 1.0) * lam - interface * lap
        phase_back[t] = own(value)
        r = [pr[i, t + 1] for i in range(3)]
        vel = (v0, v1, v2)
        grads = [[], [], []]
        for i, field in enumerate((V0, V1, V2)):
            grads[0].append(0.5 * (at(field, t + 1) - at(field, t - 1)))
            grads[1].append(dx(vel[i]))
            grads[2].append(dy(vel[i]))
        for k in range(3):
            mix = r[0] * grads[k][0] + r[1] * grads[k][1] + r[2] * grads[k][2]
            ru, rd = pr[k, t + 2], pr[k, t]
            moved = (viscosity + 0.5 * v0u) * ru + (viscosity - 0.5 * v0d) * rd
            moved = moved + x_up((viscosity + 0.5 * v1) * r[k]) + x_dn((viscosity - 0.5 * v1) * r[k])
            moved = moved + y_up((viscosity + 0.5 * v2) * r[k]) + y_dn((viscosity - 0.5 * v2) * r[k])
            moved = moved - (6.0 * viscosity) * r[k]
            value = r[k] + DT * (moved - mix - c * g[k, t + 1])
            velocity_back[k, t] = own(value)

    loop(4, finish)


def f32(*shape):
    return jax.ShapeDtypeStruct(shape, jnp.float32)


def layers(*lead):
    return f32(*lead, ROWS, LANES)


def scratch(*lead):
    return pltpu.VMEM((*lead, ROWS, LANES), jnp.float32)


VM = pl.BlockSpec(memory_space=pltpu.VMEM)
SM = pl.BlockSpec(memory_space=pltpu.SMEM)
PARAMS = pltpu.CompilerParams(vmem_limit_bytes=12 * 1024 * 1024)
SWAP = [(0, 1), (1, 0)]


def role_shift(value, cross):
    gx, gy, gz = (lax.axis_size(a) for a in ("gx", "gy", "gz"))
    pairs = []
    for x in range(gx):
        for y in range(gy):
            for i in range(gz):
                target = (1 - x if cross else x, y, (i + 1 - 2 * y) % gz)
                pairs.append(((x * gy + y) * gz + i, (target[0] * gy + y) * gz + target[2]))
    return lax.ppermute(value, ("gx", "gy", "gz"), pairs)


def ring(value, step):
    count = lax.axis_size("gz")
    return lax.ppermute(value, "gz", [(i, (i + step) % count) for i in range(count)])


def swap(value):
    return lax.ppermute(value, "gy", SWAP)


def call(kernel, outs, ins, scratches, name, smem, aliases={}):
    return pl.pallas_call(
        kernel,
        out_shape=outs,
        in_specs=[SM] * smem + [VM] * (len(ins) - smem),
        out_specs=jax.tree.map(lambda _: VM, outs),
        scratch_shapes=scratches,
        input_output_aliases=aliases,
        compiler_params=PARAMS,
        name=name,
    )(*ins)


def local(phase, velocity, phase_obs, velocity_obs, coefs):
    mine = (velocity, phase, phase_obs, velocity_obs)
    stack, edges, coefs, give = pl.pallas_call(
        load_kernel,
        out_shape=(f32(8 * CZ, CX, CY), f32(6 * CZ, 2 * HX, CY), f32(4), f32(len(SENT), CX, CY)),
        in_specs=[pl.BlockSpec(memory_space=pltpu.HBM)] * 5,
        out_specs=(VM,) * 4,
        scratch_shapes=[pltpu.SemaphoreType.DMA((9,))],
        compiler_params=PARAMS,
        name="load",
    )(*(pltpu.with_memory_space_constraint(a, pltpu.HBM) for a in (*mine, coefs)))
    peer = swap(stack)
    gxr = lax.ppermute(edges, "gx", SWAP)
    main, diag = call(
        pack_kernel,
        (f32(len(SENT), CX, LANES), f32(CORNER_ROWS, LANES)),
        (stack, swap(give)),
        [],
        "pack",
        0,
    )
    mr = role_shift(main, False)
    dr = role_shift(diag, True)
    gxr, mr, dr = lax.optimization_barrier((gxr, mr, dr))
    gxs = swap(gxr)
    inner = call(inner_kernel, layers(TOTAL), (stack, peer, gxr, gxs), [], "inner", 0)
    ms = swap(mr)
    ds = swap(dr)
    e, b, u, q, pot, lph, g, lv, send, far = call(
        first_kernel,
        (layers(TOTAL), layers(4), layers(4), layers(3, 6), layers(6), layers(6), layers(3, 6), layers(3, 6),
         f32(AGAIN_ROWS, LANES), f32(CX, LANES)),
        (coefs, inner, mr, ms, dr, ds),
        [scratch(6)],
        "first",
        1,
        {1: 0},
    )
    r2 = role_shift(send, False)
    far = ring(far, -2)
    adj, w, part, edge = call(
        weight_kernel,
        (layers(4), f32(3, CZ, CX, LANES), f32(5, 8, CY), f32(2, 4, NARROW, LANES)),
        (coefs, e, q, pot, lph, g, lv),
        [],
        "weights",
        1,
    )
    r2, far, w, part, edge = lax.optimization_barrier((r2, far, w, part, edge))
    s2 = swap(r2)
    sums, bb, uu, f, af, a2f, ab, au, send = call(
        moment_kernel,
        (f32(PARTNERS, SLOTS), layers(13), layers(8), layers(9), layers(7), layers(5), layers(8), layers(6),
         f32(8, NARROW, LANES)),
        (b, u, r2, s2, far, w, part, edge),
        [scratch(4), scratch(4)],
        "moments",
        0,
    )
    ri = role_shift(send, False)
    gathered = lax.all_to_all(sums.reshape(PARTNERS, 1, SLOTS), ("gx", "gz"), 0, 0).reshape(PARTNERS, SLOTS)
    ri, gathered = lax.optimization_barrier((ri, gathered))
    si = swap(ri)
    phase_back, velocity_back, params = call(
        last_kernel,
        (f32(CZ, CX, CY), f32(3, CZ, CX, CY), f32(4)),
        (coefs, gathered, bb, uu, f, af, a2f, ab, au, ri, si, e, q, adj, pot, g),
        [scratch(8), scratch(3, 6), scratch(6), scratch(8), scratch(2, 6), scratch(8), scratch(8), scratch(8)],
        "last",
        1,
    )
    return phase_back, velocity_back, params


def solution(mesh):
    return jax.shard_map(
        local,
        mesh=mesh,
        in_specs=(
            P("gz", "gx", "gy"),
            P(None, "gz", "gx", "gy"),
            P("gz", "gx", "gy"),
            P(None, "gz", "gx", "gy"),
            P(),
        ),
        out_specs=(P("gz", "gx", "gy"), P(None, "gz", "gx", "gy"), P()),
        check_vma=False,
    )
```

```python
import jax
import jax.numpy as jnp
from jax import lax
from jax.experimental import pallas as pl
from jax.experimental.pallas import tpu as pltpu
from jax.sharding import PartitionSpec as P

DT = 0.1
SHIFT = 0.01
CZ, CX, CY = 4, 32, 128
HX = 8
NEAR = 4
NARROW = (CX + 2 * HX) - 2 * NEAR
ROWS = CX + 2 * HX
LANES = 2 * CY
PARTNERS = 128

V0, V1, V2, PH, PO, O0, O1, O2 = range(8)
HALO = (2, 1, 1, 2, 0, 1, 0, 0)
BASE = []
_at = 0
for _h in HALO:
    BASE.append(_at)
    _at += CZ + 2 * _h
TOTAL = _at
SENT = [(f, k) for f, h in enumerate(HALO) for k in range(1, h + 1)]
CORNER = [3 if f == O0 else 8 - k for f, k in SENT]
CORNER_ROWS = -(-2 * sum(CORNER) // 8) * 8
AGAIN = [("b", k, 6 - k) for k in (1, 2, 3, 4)] + [("u", k, 3 - k) for k in (1, 2)]
AGAIN_ROWS = -(-sum(CX + 2 * w for _, _, w in AGAIN) // 8) * 8
NUM_SUMS = 45
SLOTS = 64


def x_up(a):
    return pltpu.roll(a, a.shape[0] - 1, 0)


def x_dn(a):
    return pltpu.roll(a, 1, 0)


def y_up(a):
    return pltpu.roll(a, a.shape[1] - 1, 1)


def y_dn(a):
    return pltpu.roll(a, 1, 1)


def dx(a):
    return 0.5 * (x_up(a) - x_dn(a))


def dy(a):
    return 0.5 * (y_up(a) - y_dn(a))


def own(a):
    return a[HX : HX + CX, :CY]


def lap_of(c, zu, zd):
    return (zu + zd) + (x_up(c) + x_dn(c)) + (y_up(c) + y_dn(c)) - 6.0 * c


def other_first(a):
    return jnp.concatenate([a[:, CY:], a[:, :CY]], 1)


def outgoing(core, k):
    return (CZ - k) * (1 - core) + (k - 1) * core


def loop(count, body):
    def step(t, carry):
        body(t)
        return carry

    lax.fori_loop(0, count, step, 0, unroll=count)


def low_high(core, mine, theirs):
    theirs = other_first(theirs)
    return jnp.where(core == 0, mine, theirs), jnp.where(core == 0, theirs, mine)


def load_kernel(vel, ph, po, vo, coefs, stack, out, coefs_out, give, sems):
    copies = [
        pltpu.make_async_copy(ph, stack.at[pl.ds(CZ * PH, CZ)], sems.at[6]),
        pltpu.make_async_copy(po, stack.at[pl.ds(CZ * PO, CZ)], sems.at[7]),
        pltpu.make_async_copy(coefs, coefs_out, sems.at[8]),
    ]
    for i in range(3):
        copies.append(pltpu.make_async_copy(vel.at[i], stack.at[pl.ds(CZ * (V0 + i), CZ)], sems.at[i]))
        copies.append(pltpu.make_async_copy(vo.at[i], stack.at[pl.ds(CZ * (O0 + i), CZ)], sems.at[3 + i]))
    for copy in copies:
        copy.start()
    for copy in copies:
        copy.wait()
    other = 1 - lax.axis_index("gy")
    for n, (f, k) in enumerate(SENT):
        give[n] = stack[CZ * f + outgoing(other, k)]
    wide = CZ * PO
    out[0:wide, 0:HX] = stack[0:wide, CX - HX :]
    out[0:wide, HX:] = stack[0:wide, :HX]
    for n in range(wide):
        at, row = wide + n // 2, HX * (n % 2)
        out[at, row : row + NEAR] = stack[wide + n, CX - NEAR :]
        out[at, row + NEAR : row + HX] = stack[wide + n, :NEAR]


def pack_kernel(stack, got, main, diag):
    c = lax.axis_index("gy")
    row = 0
    for n, (f, k) in enumerate(SENT):
        src = jnp.concatenate([stack[CZ * f + outgoing(c, k)], got[n]], 1)
        main[n] = src
        w = CORNER[n]
        diag[row : row + w] = src[CX - w :]
        diag[row + w : row + 2 * w] = src[:w]
        row += 2 * w


def inner_kernel(stack, peer, gxr, gxs, e):
    for f, h in enumerate(HALO):
        mid = BASE[f] + h
        for z in range(CZ):
            for half, x in enumerate((gxr, gxs)):
                src = (stack, peer)[half][CZ * f + z]
                lanes = pl.ds(CY * half, CY)
                e[mid + z, HX : HX + CX, lanes] = src
                if f <= PH:
                    e[mid + z, 0:HX, lanes] = x[CZ * f + z, 0:HX]
                    e[mid + z, HX + CX :, lanes] = x[CZ * f + z, HX:]
                else:
                    k = CZ * (f - PO) + z
                    pair, row = CZ * PO + k // 2, HX * (k % 2)
                    e[mid + z, HX - NEAR : HX, lanes] = x[pair, row : row + NEAR]
                    e[mid + z, HX + CX : HX + CX + NEAR, lanes] = x[pair, row + NEAR : row + HX]


def first_kernel(coefs, inner, mr, ms, dr, ds, e, b, u, q, pot, lph, g, lv, send, far, p0):
    tension = 0.5 * coefs[1]
    viscosity = 0.1 * coefs[2]
    interface = 0.5 * coefs[3]
    c = lax.axis_index("gy")

    row = 0
    for n, (f, k) in enumerate(SENT):
        below, above = BASE[f] + HALO[f] - k, BASE[f] + HALO[f] + CZ + k - 1
        lo, hi = low_high(c, mr[n], ms[n])
        e[below, HX : HX + CX] = lo
        e[above, HX : HX + CX] = hi
        w = CORNER[n]
        lo, hi = low_high(c, dr[row : row + 2 * w], ds[row : row + 2 * w])
        for layer, part in ((below, lo), (above, hi)):
            e[layer, HX - w : HX] = part[:w]
            e[layer, HX + CX : HX + CX + w] = part[w:]
        row += 2 * w

    def at(field, z):
        return e[BASE[field] + HALO[field] + z]

    def potential(t):
        z = t - 1
        a = at(PH, z)
        lap = lap_of(a, at(PH, z + 1), at(PH, z - 1))
        lph[t] = lap
        pot[t] = a * a * a - a - interface * lap

    loop(6, potential)

    def provisional(field, z, grad, here):
        a = at(field, z)
        zu, zd = at(field, z + 1), at(field, z - 1)
        xu, xd, yu, yd = x_up(a), x_dn(a), y_up(a), y_dn(a)
        lap = (zu + zd) + (xu + xd) + (yu + yd) - 6.0 * a
        advect = at(V0, z) * (zu - zd) + at(V1, z) * (xu - xd) + at(V2, z) * (yu - yd)
        value = a - (0.5 * DT) * advect + (DT * viscosity) * lap + (DT * tension) * (here * grad)
        return value, lap

    def along(t):
        z = t - 1
        grad = 0.5 * (at(PH, z + 1) - at(PH, z - 1))
        p0[t], lv[0, t] = provisional(V0, z, grad, pot[t])

    loop(6, along)

    def slopes(t):
        z = t - 1
        a = at(PH, z)
        g[0, t] = 0.5 * (at(PH, z + 1) - at(PH, z - 1))
        g[1, t] = dx(a)
        g[2, t] = dy(a)
        q[0, t] = p0[t] - at(O0, z)

    loop(6, slopes)

    def across(z):
        here = pot[z + 1]
        p1, lv[1, z] = provisional(V1, z, g[1, z + 1], here)
        p2, lv[2, z] = provisional(V2, z, g[2, z + 1], here)
        b[z] = -(0.5 * (p0[z + 2] - p0[z]) + dx(p1) + dy(p2))
        q1 = p1 - at(O1, z)
        q2 = p2 - at(O2, z)
        q[1, z + 1] = q1
        q[2, z + 1] = q2
        u[z] = 0.5 * (q[0, z + 2] - q[0, z]) + dx(q1) + dy(q2)

    loop(4, across)

    row = 0
    for name, k, w in AGAIN:
        field = b if name == "b" else u
        rows = CX + 2 * w
        send[row : row + rows] = field[outgoing(c, k), HX - w : HX + CX + w]
        row += rows
    far[...] = b[0, HX : HX + CX]


def folded(a):
    a = a[:, :CY] + a[:, CY:]
    return (a[0:8] + a[8:16]) + (a[16:24] + a[24:32])


def middle(a):
    return a[HX : HX + CX]


def weight_kernel(coefs, e, q, pot, lph, g, lv, adj, w, part, edge, gv, base):
    mobility = 0.1 * coefs[0]

    def at(field, z):
        return e[BASE[field] + HALO[field] + z]

    sums = [jnp.zeros((8, CY), jnp.float32)] * 5
    for t in range(CZ):
        here = pot[t + 1]
        lap = lph[t + 1]
        gs = [g[i, t + 1] for i in range(3)]
        up, dn = pot[t + 2] * g[0, t + 2], pot[t] * g[0, t]
        w1 = 0.5 * (up - dn) + dx(here * gs[1]) + dy(here * gs[2])
        w2 = 0.5 * (lv[0, t + 2] - lv[0, t]) + dx(lv[1, t]) + dy(lv[2, t])
        up, dn = lph[t + 2] * g[0, t + 2], lph[t] * g[0, t]
        w3 = 0.5 * (up - dn) + dx(lap * gs[1]) + dy(lap * gs[2])
        w[0, t] = middle(w1)
        w[1, t] = middle(w2)
        w[2, t] = middle(w3)
        lap_pot = lap_of(here, pot[t + 2], pot[t])
        lap_lap = lap_of(lap, lph[t + 2], lph[t])
        flow = at(V0, t) * gs[0] + at(V1, t) * gs[1] + at(V2, t) * gs[2]
        c = at(PH, t) - DT * flow + (DT * mobility) * lap_pot - at(PO, t)
        adj[t] = c
        v1, v2 = at(V1, t), at(V2, t)
        base[t] = own(c + DT * (dx(v1 * c) + dy(v2 * c)))
        for i, field in enumerate((V0, V1, V2)):
            a = at(field, t)
            gv[0, i, t] = own(0.5 * (at(field, t + 1) - at(field, t - 1)))
            gv[1, i, t] = own(dx(a))
            gv[2, i, t] = own(dy(a))
        qs = [q[i, t + 1] for i in range(3)]
        qg = qs[0] * gs[0] + qs[1] * gs[1] + qs[2] * gs[2]
        ql = qs[0] * lv[0, t + 1] + qs[1] * lv[1, t] + qs[2] * lv[2, t]
        terms = (middle(c * lap_pot), middle(here * qg), middle(ql), middle(lap * qg), middle(c * lap_lap))
        sums = [s + folded(a) for s, a in zip(sums, terms)]
    for k in range(5):
        part[k] = sums[k]
    for k, z in ((0, CZ - 1), (1, 0)):
        edge[k, 0] = q[1, z + 1, NEAR : ROWS - NEAR]
        edge[k, 1] = q[2, z + 1, NEAR : ROWS - NEAR]
        for j in range(2):
            edge[k, 2 + j] = adj[2 * (1 - k) + j, NEAR : ROWS - NEAR]


def shifted(c, zu, zd):
    return (6.0 + SHIFT) * c - ((zu + zd) + (x_up(c) + x_dn(c)) + (y_up(c) + y_dn(c)))


def moment_kernel(b4, u4, r, s, far, w, part, edge, out, bb, uu, f, af, a2f, ab, au, send, a2b, a2u):
    c = lax.axis_index("gy")
    near = pl.ds(NEAR, NARROW)
    row = 0
    for name, k, width in AGAIN:
        rows = CX + 2 * width
        lo, hi = low_high(c, r[row : row + rows], s[row : row + rows])
        dst, below = (bb, 4 - k) if name == "b" else (uu, 2 - k)
        above = 7 + k if name == "b" else 5 + k
        dst[below, HX - width : HX + CX + width] = lo
        dst[above, HX - width : HX + CX + width] = hi
        row += rows
    bb[12, HX : HX + CX] = far[...]
    bb[4:8] = b4[...]
    uu[2:6] = u4[...]

    def wide(t):
        a = bb[t + 2]
        across = (pltpu.roll(a, ROWS - 2, 0) + pltpu.roll(a, 2, 0)) + (
            pltpu.roll(a, LANES - 2, 1) + pltpu.roll(a, 2, 1)
        )
        f[t] = 0.25 * ((bb[t + 4] + bb[t]) + across) - 1.5 * a

    loop(9, wide)

    def apply(src, dst, count):
        def body(t):
            dst[t] = shifted(src[t + 1], src[t + 2], src[t])

        loop(count, body)

    apply(f, af, 7)
    apply(af, a2f, 5)
    apply(bb.at[pl.ds(1, 10)], ab, 8)
    apply(ab.at[pl.ds(1, 6)], a2b, 4)
    apply(uu, au, 6)
    apply(au, a2u, 4)

    rows = pl.ds(HX, CX)
    acc = [jnp.zeros((8, CY), jnp.float32)] * 40
    for t in range(CZ):
        vb, vab, va2b = bb[t + 4, rows], ab[t + 2, rows], a2b[t, rows]
        vu, vau, va2u = uu[t + 2, rows], au[t + 1, rows], a2u[t, rows]
        vf, vaf, va2f = f[t + 2, rows], af[t + 1, rows], a2f[t, rows]
        a = a2f[t]
        across = (x_up(a) + x_dn(a)) + (y_up(a) + y_dn(a))
        va3f = (6.0 + SHIFT) * va2f - (2.0 * a2f[t + 1, rows] + middle(across))
        terms = [
            vb * vb, vb * vab, vab * vab, vab * va2b,
            vu * vu, vu * vau, vau * vau, vau * va2u,
            vu * vf, vu * vaf, vu * va2f, vau * va2f, va2u * va2f,
            vf * vf, vf * vaf, vaf * vaf, vaf * va2f, va2f * va2f, va2f * va3f,
        ]
        for k in range(3):
            wk = w[k, t]
            terms += [a * wk for a in (vu, vau, vf, vaf, va2f, vb, vab)]
        acc = [x + folded(a) for x, a in zip(acc, terms)]
    rows_list = [jnp.sum(a, axis=0, keepdims=True) for a in acc]
    rows_list += [jnp.sum(part[k], axis=0, keepdims=True) for k in range(5)]
    rows_list += [jnp.zeros((1, CY), jnp.float32)] * (48 - NUM_SUMS)
    table = jnp.concatenate(rows_list, axis=0)
    totals = jnp.sum(table, axis=1, keepdims=True)
    line = lax.broadcasted_iota(jnp.int32, (48, SLOTS), 1)
    which = lax.broadcasted_iota(jnp.int32, (48, SLOTS), 0)
    row = jnp.sum(jnp.where(line == which, totals, 0.0), axis=0, keepdims=True)
    out[...] = jnp.broadcast_to(row, (PARTNERS, SLOTS))
    send[0:4] = edge[c]
    first = 2 * (1 - c)
    send[4] = a2f[first, near]
    send[5] = a2f[first + 1, near]
    send[6] = af[3 - c, near]
    send[7] = au[3 - c, near]


def steps(m0, m1, m2, m3):
    alpha = m0 / m1
    second = (m1 / m0) * ((m0 * m2 - m1 * m1) / (m1 * m3 - m2 * m2))
    second = jnp.clip(second, 1.0 / (12.0 + SHIFT), 1.0 / SHIFT)
    return alpha + second * ((m0 * m2) / (m1 * m1)), -second * alpha


def solve_kernel(gathered, mobility, tension, coef_out, params):
    total = jnp.sum(gathered[...], axis=0, keepdims=True)
    line = lax.broadcasted_iota(jnp.int32, (1, SLOTS), 1)

    def s(k):
        return jnp.sum(jnp.where(line == k, total, 0.0), axis=1, keepdims=True)

    c0, c1 = steps(s(0), s(1), s(2), s(3))
    uu = [s(4 + k) for k in range(4)]
    uf = [s(8 + k) for k in range(5)]
    ff = [s(13 + k) for k in range(6)]
    moments = [
        uu[k] - 2.0 * (c0 * uf[k] + c1 * uf[k + 1])
        + (c0 * c0) * ff[k] + (2.0 * c0 * c1) * ff[k + 1] + (c1 * c1) * ff[k + 2]
        for k in range(4)
    ]
    e0, e1 = steps(*moments)
    coef = (e0, e1, -e0 * c0, -(e0 * c1 + e1 * c0), -e1 * c1, -c0, -c1)
    for j in range(7):
        coef_out[j : j + 1] = jnp.broadcast_to(coef[j], (1, CY))

    def meet(k):
        value = coef[0] * s(19 + 7 * k)
        for j in range(1, 7):
            value = value + coef[j] * s(19 + 7 * k + j)
        return value

    scale = 1.0 / (256 * 64 * 256)
    g0 = DT * s(40)
    g1 = DT * (s(41) - meet(0))
    g2 = DT * (s(42) - meet(1))
    g3 = -((DT * mobility) * s(44) + (DT * tension) * (s(43) - meet(2)))
    place = lax.broadcasted_iota(jnp.int32, (1, CY), 1)
    packed = jnp.where(place == 0, g0, jnp.where(place == 1, g1, jnp.where(place == 2, g2, g3)))
    params[...] = (packed * scale)[0, 0:4]
    return coef


def half_step(side, halo, coef, consts, basis, state, work, write):
    mobility, tension, viscosity, interface = consts
    uu, f, af, a2f, bb, ab, au = basis
    e, q, adj4, pot, g, gv, base = state
    phi, pr, pa, adj, qe, new = work
    near = pl.ds(NEAR, NARROW)
    for i in range(2):
        qe[i, 5 * side, near] = halo(i)
        adj[6 * side + i, near] = halo(2 + i)

    def mixed(terms):
        value = coef[0] * terms[0]
        for a, t in zip(coef[1:], terms[1:]):
            value = value + a * t
        return value

    i = 1 + 5 * side
    phi[i, near] = mixed([
        uu[i, near], au[i - 1, near], f[i, near], af[i - 1, near], halo(5 - side), bb[i + 2, near], ab[i, near],
    ])
    i = 7 * side
    phi[i, near] = mixed([uu[i, near], halo(7), f[i, near], halo(6), halo(4 + side), bb[i + 2, near], ab[i, near]])

    def project(t):
        c = phi[t + 1]
        r0 = q[0, t] + 0.5 * (phi[t + 2] - phi[t])
        r1 = qe[0, t] + dx(c)
        r2 = qe[1, t] + dy(c)
        pr[0, t] = r0
        pr[1, t] = r1
        pr[2, t] = r2
        lap = lap_of(adj[t + 1], adj[t + 2], adj[t])
        pa[t] = (DT * mobility) * lap + (DT * tension) * (r0 * g[0, t] + r1 * g[1, t] + r2 * g[2, t])

    for t in new:
        project(t)

    def at(field, z):
        return e[BASE[field] + HALO[field] + z]

    for n in range(2):
        t = 2 * side + n
        v1, v2 = at(V1, t), at(V2, t)
        v0u, v0d = at(V0, t + 1), at(V0, t - 1)
        here = pot[t + 1]
        ph = own(at(PH, t))
        lam = pa[t + 1]
        up = v0u * adj[t + 3] - tension * (pot[t + 2] * pr[0, t + 2])
        dn = v0d * adj[t + 1] - tension * (pot[t] * pr[0, t])
        div = 0.5 * (up - dn) - tension * (dx(here * pr[1, t + 1]) + dy(here * pr[2, t + 1]))
        value = base[t] + DT * own(div) + (3.0 * ph * ph - 1.0) * own(lam)
        write(n, 0, value - interface * own(lap_of(lam, pa[t + 2], pa[t])))
        r = [pr[i, t + 1] for i in range(3)]
        mine = [own(a) for a in r]
        c = own(adj[t + 2])
        for k in range(3):
            mix = mine[0] * gv[k, 0, t] + mine[1] * gv[k, 1, t] + mine[2] * gv[k, 2, t]
            moved = (viscosity + 0.5 * v0u) * pr[k, t + 2] + (viscosity - 0.5 * v0d) * pr[k, t]
            moved = moved + x_up((viscosity + 0.5 * v1) * r[k]) + x_dn((viscosity - 0.5 * v1) * r[k])
            moved = moved + y_up((viscosity + 0.5 * v2) * r[k]) + y_dn((viscosity - 0.5 * v2) * r[k])
            moved = own(moved) - (6.0 * viscosity) * mine[k]
            write(n, 1 + k, mine[k] + DT * (moved - mix - c * own(g[k, t + 1])))


def constants(coefs):
    return 0.1 * coefs[0], 0.5 * coefs[1], 0.1 * coefs[2], 0.5 * coefs[3]


def near_kernel(
    coefs, gathered, uu, f, af, a2f, bb, ab, au, ri, e, q, adj4, pot, g, gv, base,
    params, table, phi_own, shared, result, phi, pr, pa, adj, qe,
):
    consts = constants(coefs)
    coef = solve_kernel(gathered, consts[0], consts[1], table, params)
    side = lax.axis_index("gy")
    adj[2:6] = adj4[...]
    for i in range(2):
        qe[i, 1:5] = q[i + 1, 1:5]
    for z in range(CZ):
        value = coef[0] * uu[z + 2] + coef[1] * au[z + 1] + coef[2] * f[z + 2] + coef[3] * af[z + 1]
        value = value + coef[4] * a2f[z] + coef[5] * bb[z + 4] + coef[6] * ab[z + 2]
        phi[z + 2] = value
        phi_own[z] = value

    def write(n, k, value):
        result[k, n] = value

    new = [2 * side + n for n in range(4)]
    half_step(
        side, lambda j: ri[j], coef, consts, (uu, f, af, a2f, bb, ab, au), (e, q, adj4, pot, g, gv, base),
        (phi, pr, pa, adj, qe, new), write,
    )
    for n in range(2):
        for i in range(3):
            shared[i, n] = pr[i, 2 + n]
        shared[3, n] = pa[2 + n]


def far_kernel(
    coefs, table, uu, f, af, a2f, bb, ab, au, si, e, q, adj4, pot, g, gv, base, phi_own, shared, result,
    phase_back, velocity_back, phi, pr, pa, adj, qe,
):
    consts = constants(coefs)
    coef = [table[j : j + 1, 0:1] for j in range(7)]
    mine = lax.axis_index("gy")
    side = 1 - mine
    adj[2:6] = adj4[...]
    for i in range(2):
        qe[i, 1:5] = q[i + 1, 1:5]
    phi[2:6] = phi_own[...]
    for n in range(2):
        for i in range(3):
            pr[i, 2 + n] = shared[i, n]
        pa[2 + n] = shared[3, n]

    def write(n, k, value):
        if k == 0:
            phase_back[2 * side + n] = value
        else:
            velocity_back[k - 1, 2 * side + n] = value

    new = [4 * side + n for n in range(2)]
    half_step(
        side, lambda j: other_first(si[j]), coef, consts, (uu, f, af, a2f, bb, ab, au),
        (e, q, adj4, pot, g, gv, base), (phi, pr, pa, adj, qe, new), write,
    )
    for n in range(2):
        phase_back[2 * mine + n] = result[0, n]
        for k in range(3):
            velocity_back[k, 2 * mine + n] = result[1 + k, n]


def f32(*shape):
    return jax.ShapeDtypeStruct(shape, jnp.float32)


def layers(*lead):
    return f32(*lead, ROWS, LANES)


def scratch(*lead):
    return pltpu.VMEM((*lead, ROWS, LANES), jnp.float32)


VM = pl.BlockSpec(memory_space=pltpu.VMEM)
SM = pl.BlockSpec(memory_space=pltpu.SMEM)
PARAMS = pltpu.CompilerParams(vmem_limit_bytes=12 * 1024 * 1024)
SWAP = [(0, 1), (1, 0)]


def role_shift(value, cross):
    gx, gy, gz = (lax.axis_size(a) for a in ("gx", "gy", "gz"))
    pairs = []
    for x in range(gx):
        for y in range(gy):
            for i in range(gz):
                target = (1 - x if cross else x, y, (i + 1 - 2 * y) % gz)
                pairs.append(((x * gy + y) * gz + i, (target[0] * gy + y) * gz + target[2]))
    return lax.ppermute(value, ("gx", "gy", "gz"), pairs)


def ring(value, step):
    count = lax.axis_size("gz")
    return lax.ppermute(value, "gz", [(i, (i + step) % count) for i in range(count)])


def swap(value):
    return lax.ppermute(value, "gy", SWAP)


def call(kernel, outs, ins, scratches, name, smem, aliases={}):
    return pl.pallas_call(
        kernel,
        out_shape=outs,
        in_specs=[SM] * smem + [VM] * (len(ins) - smem),
        out_specs=jax.tree.map(lambda _: VM, outs),
        scratch_shapes=scratches,
        input_output_aliases=aliases,
        compiler_params=PARAMS,
        name=name,
    )(*ins)


def local(phase, velocity, phase_obs, velocity_obs, coefs):
    mine = (velocity, phase, phase_obs, velocity_obs)
    stack, edges, coefs, give = pl.pallas_call(
        load_kernel,
        out_shape=(f32(8 * CZ, CX, CY), f32(6 * CZ, 2 * HX, CY), f32(4), f32(len(SENT), CX, CY)),
        in_specs=[pl.BlockSpec(memory_space=pltpu.HBM)] * 5,
        out_specs=(VM,) * 4,
        scratch_shapes=[pltpu.SemaphoreType.DMA((9,))],
        compiler_params=PARAMS,
        name="load",
    )(*(pltpu.with_memory_space_constraint(a, pltpu.HBM) for a in (*mine, coefs)))
    peer = swap(stack)
    gxr = lax.ppermute(edges, "gx", SWAP)
    main, diag = call(
        pack_kernel,
        (f32(len(SENT), CX, LANES), f32(CORNER_ROWS, LANES)),
        (stack, swap(give)),
        [],
        "pack",
        0,
    )
    mr = role_shift(main, False)
    dr = role_shift(diag, True)
    gxr, mr, dr = lax.optimization_barrier((gxr, mr, dr))
    gxs = swap(gxr)
    inner = call(inner_kernel, layers(TOTAL), (stack, peer, gxr, gxs), [], "inner", 0)
    ms = swap(mr)
    ds = swap(dr)
    e, b, u, q, pot, lph, g, lv, send, far = call(
        first_kernel,
        (layers(TOTAL), layers(4), layers(4), layers(3, 6), layers(6), layers(6), layers(3, 6), layers(3, 6),
         f32(AGAIN_ROWS, LANES), f32(CX, LANES)),
        (coefs, inner, mr, ms, dr, ds),
        [scratch(6)],
        "first",
        1,
        {1: 0},
    )
    r2 = role_shift(send, False)
    far = ring(far, -2)
    adj, w, part, edge, gv, base = call(
        weight_kernel,
        (layers(4), f32(3, CZ, CX, LANES), f32(5, 8, CY), f32(2, 4, NARROW, LANES), f32(3, 3, CZ, CX, CY), f32(CZ, CX, CY)),
        (coefs, e, q, pot, lph, g, lv),
        [],
        "weights",
        1,
    )
    r2, far, w, part, edge = lax.optimization_barrier((r2, far, w, part, edge))
    s2 = swap(r2)
    sums, bb, uu, f, af, a2f, ab, au, send = call(
        moment_kernel,
        (f32(PARTNERS, SLOTS), layers(13), layers(8), layers(9), layers(7), layers(5), layers(8), layers(6),
         f32(8, NARROW, LANES)),
        (b, u, r2, s2, far, w, part, edge),
        [scratch(4), scratch(4)],
        "moments",
        0,
    )
    ri = role_shift(send, False)
    gathered = lax.all_to_all(sums.reshape(PARTNERS, 1, SLOTS), ("gx", "gz"), 0, 0).reshape(PARTNERS, SLOTS)
    ri, gathered = lax.optimization_barrier((ri, gathered))
    si = swap(ri)
    basis = (uu, f, af, a2f, bb, ab, au)
    state = (e, q, adj, pot, g, gv, base)
    room = [scratch(8), scratch(3, 6), scratch(6), scratch(8), scratch(2, 6)]
    params, table, phi, shared, result = call(
        near_kernel,
        (f32(4), f32(8, CY), layers(4), layers(4, 2), f32(4, 2, CX, CY)),
        (coefs, gathered, *basis, ri, *state),
        room,
        "near",
        1,
    )
    phase_back, velocity_back = call(
        far_kernel,
        (f32(CZ, CX, CY), f32(3, CZ, CX, CY)),
        (coefs, table, *basis, si, *state, phi, shared, result),
        room,
        "far",
        1,
    )
    return phase_back, velocity_back, params


def solution(mesh):
    return jax.shard_map(
        local,
        mesh=mesh,
        in_specs=(
            P("gz", "gx", "gy"),
            P(None, "gz", "gx", "gy"),
            P("gz", "gx", "gy"),
            P(None, "gz", "gx", "gy"),
            P(),
        ),
        out_specs=(P("gz", "gx", "gy"), P(None, "gz", "gx", "gy"), P()),
        check_vma=False,
    )
```

```python
import jax
import jax.numpy as jnp
from jax import lax
from jax.experimental import pallas as pl
from jax.experimental.pallas import tpu as pltpu
from jax.sharding import PartitionSpec as P

DT = 0.1
SHIFT = 0.01
CZ, CX, CY = 4, 32, 128
HX = 8
NEAR = 4
NARROW = (CX + 2 * HX) - 2 * NEAR
ROWS = CX + 2 * HX
LANES = 2 * CY
PARTNERS = 128

V0, V1, V2, PH, PO, O0, O1, O2 = range(8)
HALO = (2, 1, 1, 2, 0, 1, 0, 0)
BASE = []
_at = 0
for _h in HALO:
    BASE.append(_at)
    _at += CZ + 2 * _h
TOTAL = _at
SENT = [(f, k) for f, h in enumerate(HALO) for k in range(1, h + 1)]
CORNER = [{(V0, 1): 1, (V1, 1): 1, (V2, 1): 1, (PH, 1): 3, (PH, 2): 2}.get(entry, 0) for entry in SENT]
CORNER_ROWS = 2 * sum(CORNER)
EDGE = (2, 2, 2, 4, 2, 1, 1, 1)
EDGE_ROWS = 2 * CZ * sum(EDGE)
AGAIN = [("b", k, 6 - k) for k in (1, 2, 3, 4)] + [("u", k, 3 - k) for k in (1, 2)]
AGAIN_ROWS = 2 * sum(w for _, _, w in AGAIN)
RIM = [("b", z, 6) for z in range(CZ)] + [("u", z, 3) for z in range(CZ)]
RIM_ROWS = 2 * sum(w for _, _, w in RIM)
NUM_SUMS = 45
SLOTS = 64


def x_up(a):
    return pltpu.roll(a, a.shape[0] - 1, 0)


def x_dn(a):
    return pltpu.roll(a, 1, 0)


def y_up(a):
    return pltpu.roll(a, a.shape[1] - 1, 1)


def y_dn(a):
    return pltpu.roll(a, 1, 1)


def dx(a):
    return 0.5 * (x_up(a) - x_dn(a))


def dy(a):
    return 0.5 * (y_up(a) - y_dn(a))


def own(a):
    return a[HX : HX + CX, :CY]


def lap_of(c, zu, zd):
    return (zu + zd) + (x_up(c) + x_dn(c)) + (y_up(c) + y_dn(c)) - 6.0 * c


def other_first(a):
    return jnp.concatenate([a[:, CY:], a[:, :CY]], 1)


def outgoing(core, k):
    return (CZ - k) * (1 - core) + (k - 1) * core


def loop(count, body):
    def step(t, carry):
        body(t)
        return carry

    lax.fori_loop(0, count, step, 0, unroll=count)


def low_high(core, mine, theirs):
    theirs = other_first(theirs)
    return jnp.where(core == 0, mine, theirs), jnp.where(core == 0, theirs, mine)


def load_kernel(vel, ph, po, vo, coefs, stack, out, coefs_out, give, sems):
    copies = [
        pltpu.make_async_copy(ph, stack.at[pl.ds(CZ * PH, CZ)], sems.at[6]),
        pltpu.make_async_copy(po, stack.at[pl.ds(CZ * PO, CZ)], sems.at[7]),
        pltpu.make_async_copy(coefs, coefs_out, sems.at[8]),
    ]
    for i in range(3):
        copies.append(pltpu.make_async_copy(vel.at[i], stack.at[pl.ds(CZ * (V0 + i), CZ)], sems.at[i]))
        copies.append(pltpu.make_async_copy(vo.at[i], stack.at[pl.ds(CZ * (O0 + i), CZ)], sems.at[3 + i]))
    for copy in copies:
        copy.start()
    for copy in copies:
        copy.wait()
    other = 1 - lax.axis_index("gy")
    for n, (f, k) in enumerate(SENT):
        give[n] = stack[CZ * f + outgoing(other, k)]
    row = 0
    for f, w in enumerate(EDGE):
        for z in range(CZ):
            out[row : row + w] = stack[CZ * f + z, CX - w :]
            out[row + w : row + 2 * w] = stack[CZ * f + z, :w]
            row += 2 * w


def pack_kernel(stack, got, main, diag):
    c = lax.axis_index("gy")
    row = 0
    for n, (f, k) in enumerate(SENT):
        src = jnp.concatenate([stack[CZ * f + outgoing(c, k)], got[n]], 1)
        main[n] = src
        w = CORNER[n]
        if w:
            diag[row : row + w] = src[CX - w :]
            diag[row + w : row + 2 * w] = src[:w]
        row += 2 * w


def inner_kernel(stack, peer, gxr, gxs, e):
    row = 0
    for f, w in enumerate(EDGE):
        mid = BASE[f] + HALO[f]
        for z in range(CZ):
            for half, x in enumerate((gxr, gxs)):
                lanes = pl.ds(CY * half, CY)
                e[mid + z, HX : HX + CX, lanes] = (stack, peer)[half][CZ * f + z]
                e[mid + z, HX - w : HX, lanes] = x[row : row + w]
                e[mid + z, HX + CX : HX + CX + w, lanes] = x[row + w : row + 2 * w]
            row += 2 * w


def first_kernel(coefs, inner, mr, ms, dr, ds, e, b, u, q, pot, lph, g, lv, send, corner, rim, far, p0):
    tension = 0.5 * coefs[1]
    viscosity = 0.1 * coefs[2]
    interface = 0.5 * coefs[3]
    c = lax.axis_index("gy")

    row = 0
    for n, (f, k) in enumerate(SENT):
        below, above = BASE[f] + HALO[f] - k, BASE[f] + HALO[f] + CZ + k - 1
        lo, hi = low_high(c, mr[n], ms[n])
        e[below, HX : HX + CX] = lo
        e[above, HX : HX + CX] = hi
        w = CORNER[n]
        if w == 0:
            continue
        lo, hi = low_high(c, dr[row : row + 2 * w], ds[row : row + 2 * w])
        for layer, part in ((below, lo), (above, hi)):
            e[layer, HX - w : HX] = part[:w]
            e[layer, HX + CX : HX + CX + w] = part[w:]
        row += 2 * w

    def at(field, z):
        return e[BASE[field] + HALO[field] + z]

    def potential(t):
        z = t - 1
        a = at(PH, z)
        lap = lap_of(a, at(PH, z + 1), at(PH, z - 1))
        lph[t] = lap
        pot[t] = a * a * a - a - interface * lap

    loop(6, potential)

    def provisional(field, z, grad, here):
        a = at(field, z)
        zu, zd = at(field, z + 1), at(field, z - 1)
        xu, xd, yu, yd = x_up(a), x_dn(a), y_up(a), y_dn(a)
        lap = (zu + zd) + (xu + xd) + (yu + yd) - 6.0 * a
        advect = at(V0, z) * (zu - zd) + at(V1, z) * (xu - xd) + at(V2, z) * (yu - yd)
        value = a - (0.5 * DT) * advect + (DT * viscosity) * lap + (DT * tension) * (here * grad)
        return value, lap

    def along(t):
        z = t - 1
        grad = 0.5 * (at(PH, z + 1) - at(PH, z - 1))
        p0[t], lv[0, t] = provisional(V0, z, grad, pot[t])

    loop(6, along)

    def slopes(t):
        z = t - 1
        a = at(PH, z)
        g[0, t] = 0.5 * (at(PH, z + 1) - at(PH, z - 1))
        g[1, t] = dx(a)
        g[2, t] = dy(a)
        q[0, t] = p0[t] - at(O0, z)

    loop(6, slopes)

    def across(z):
        here = pot[z + 1]
        p1, lv[1, z] = provisional(V1, z, g[1, z + 1], here)
        p2, lv[2, z] = provisional(V2, z, g[2, z + 1], here)
        b[z] = -(0.5 * (p0[z + 2] - p0[z]) + dx(p1) + dy(p2))
        q1 = p1 - at(O1, z)
        q2 = p2 - at(O2, z)
        q[1, z + 1] = q1
        q[2, z + 1] = q2
        u[z] = 0.5 * (q[0, z + 2] - q[0, z]) + dx(q1) + dy(q2)

    loop(4, across)

    row = 0
    for n, (name, k, w) in enumerate(AGAIN):
        src = (b if name == "b" else u)[outgoing(c, k)]
        send[CX * n : CX * (n + 1)] = src[HX : HX + CX]
        corner[row : row + w] = src[HX + CX - w : HX + CX]
        corner[row + w : row + 2 * w] = src[HX : HX + w]
        row += 2 * w
    row = 0
    for name, z, w in RIM:
        field = b if name == "b" else u
        rim[row : row + w] = field[z, HX + CX - w : HX + CX, :CY]
        rim[row + w : row + 2 * w] = field[z, HX : HX + w, :CY]
        row += 2 * w
    far[...] = b[0, HX : HX + CX]


def folded(a):
    a = a[:, :CY] + a[:, CY:]
    return (a[0:8] + a[8:16]) + (a[16:24] + a[24:32])


def middle(a):
    return a[HX : HX + CX]


def weight_kernel(coefs, e, q, pot, lph, g, lv, adj, w, part, edge, gv, base):
    mobility = 0.1 * coefs[0]

    def at(field, z):
        return e[BASE[field] + HALO[field] + z]

    sums = [jnp.zeros((8, CY), jnp.float32)] * 5
    for t in range(CZ):
        here = pot[t + 1]
        lap = lph[t + 1]
        gs = [g[i, t + 1] for i in range(3)]
        up, dn = pot[t + 2] * g[0, t + 2], pot[t] * g[0, t]
        w1 = 0.5 * (up - dn) + dx(here * gs[1]) + dy(here * gs[2])
        w2 = 0.5 * (lv[0, t + 2] - lv[0, t]) + dx(lv[1, t]) + dy(lv[2, t])
        up, dn = lph[t + 2] * g[0, t + 2], lph[t] * g[0, t]
        w3 = 0.5 * (up - dn) + dx(lap * gs[1]) + dy(lap * gs[2])
        w[0, t] = middle(w1)
        w[1, t] = middle(w2)
        w[2, t] = middle(w3)
        lap_pot = lap_of(here, pot[t + 2], pot[t])
        lap_lap = lap_of(lap, lph[t + 2], lph[t])
        flow = at(V0, t) * gs[0] + at(V1, t) * gs[1] + at(V2, t) * gs[2]
        c = at(PH, t) - DT * flow + (DT * mobility) * lap_pot - at(PO, t)
        adj[t] = c
        v1, v2 = at(V1, t), at(V2, t)
        base[t] = own(c + DT * (dx(v1 * c) + dy(v2 * c)))
        for i, field in enumerate((V0, V1, V2)):
            a = at(field, t)
            gv[0, i, t] = own(0.5 * (at(field, t + 1) - at(field, t - 1)))
            gv[1, i, t] = own(dx(a))
            gv[2, i, t] = own(dy(a))
        qs = [q[i, t + 1] for i in range(3)]
        qg = qs[0] * gs[0] + qs[1] * gs[1] + qs[2] * gs[2]
        ql = qs[0] * lv[0, t + 1] + qs[1] * lv[1, t] + qs[2] * lv[2, t]
        terms = (middle(c * lap_pot), middle(here * qg), middle(ql), middle(lap * qg), middle(c * lap_lap))
        sums = [s + folded(a) for s, a in zip(sums, terms)]
    for k in range(5):
        part[k] = sums[k]
    for k, z in ((0, CZ - 1), (1, 0)):
        edge[k, 0] = q[1, z + 1, NEAR : ROWS - NEAR]
        edge[k, 1] = q[2, z + 1, NEAR : ROWS - NEAR]
        for j in range(2):
            edge[k, 2 + j] = adj[2 * (1 - k) + j, NEAR : ROWS - NEAR]


def shifted(c, zu, zd):
    return (6.0 + SHIFT) * c - ((zu + zd) + (x_up(c) + x_dn(c)) + (y_up(c) + y_dn(c)))


def moment_kernel(b4, u4, r, s, d, ds, x, xs, far, w, part, edge, out, bb, uu, f, af, a2f, ab, au, send, a2b, a2u):
    c = lax.axis_index("gy")
    near = pl.ds(NEAR, NARROW)
    bb[4:8] = b4[...]
    uu[2:6] = u4[...]
    row = 0
    for n, (name, k, width) in enumerate(AGAIN):
        dst, below = (bb, 4 - k) if name == "b" else (uu, 2 - k)
        above = 7 + k if name == "b" else 5 + k
        lo, hi = low_high(c, r[CX * n : CX * (n + 1)], s[CX * n : CX * (n + 1)])
        dst[below, HX : HX + CX] = lo
        dst[above, HX : HX + CX] = hi
        lo, hi = low_high(c, d[row : row + 2 * width], ds[row : row + 2 * width])
        for layer, part_rows in ((below, lo), (above, hi)):
            dst[layer, HX - width : HX] = part_rows[:width]
            dst[layer, HX + CX : HX + CX + width] = part_rows[width:]
        row += 2 * width
    row = 0
    for name, z, width in RIM:
        dst, layer = (bb, 4 + z) if name == "b" else (uu, 2 + z)
        for half, src in enumerate((x, xs)):
            lanes = pl.ds(CY * half, CY)
            dst[layer, HX - width : HX, lanes] = src[row : row + width]
            dst[layer, HX + CX : HX + CX + width, lanes] = src[row + width : row + 2 * width]
        row += 2 * width
    bb[12, HX : HX + CX] = far[...]

    def wide(t):
        a = bb[t + 2]
        across = (pltpu.roll(a, ROWS - 2, 0) + pltpu.roll(a, 2, 0)) + (
            pltpu.roll(a, LANES - 2, 1) + pltpu.roll(a, 2, 1)
        )
        f[t] = 0.25 * ((bb[t + 4] + bb[t]) + across) - 1.5 * a

    loop(9, wide)

    def apply(src, dst, count):
        def body(t):
            dst[t] = shifted(src[t + 1], src[t + 2], src[t])

        loop(count, body)

    apply(f, af, 7)
    apply(af, a2f, 5)
    apply(bb.at[pl.ds(1, 10)], ab, 8)
    apply(ab.at[pl.ds(1, 6)], a2b, 4)
    apply(uu, au, 6)
    apply(au, a2u, 4)

    rows = pl.ds(HX, CX)
    acc = [jnp.zeros((8, CY), jnp.float32)] * 40
    for t in range(CZ):
        vb, vab, va2b = bb[t + 4, rows], ab[t + 2, rows], a2b[t, rows]
        vu, vau, va2u = uu[t + 2, rows], au[t + 1, rows], a2u[t, rows]
        vf, vaf, va2f = f[t + 2, rows], af[t + 1, rows], a2f[t, rows]
        a = a2f[t]
        across = (x_up(a) + x_dn(a)) + (y_up(a) + y_dn(a))
        va3f = (6.0 + SHIFT) * va2f - (2.0 * a2f[t + 1, rows] + middle(across))
        terms = [
            vb * vb, vb * vab, vab * vab, vab * va2b,
            vu * vu, vu * vau, vau * vau, vau * va2u,
            vu * vf, vu * vaf, vu * va2f, vau * va2f, va2u * va2f,
            vf * vf, vf * vaf, vaf * vaf, vaf * va2f, va2f * va2f, va2f * va3f,
        ]
        for k in range(3):
            wk = w[k, t]
            terms += [a * wk for a in (vu, vau, vf, vaf, va2f, vb, vab)]
        acc = [x + folded(a) for x, a in zip(acc, terms)]
    rows_list = [jnp.sum(a, axis=0, keepdims=True) for a in acc]
    rows_list += [jnp.sum(part[k], axis=0, keepdims=True) for k in range(5)]
    rows_list += [jnp.zeros((1, CY), jnp.float32)] * (48 - NUM_SUMS)
    table = jnp.concatenate(rows_list, axis=0)
    totals = jnp.sum(table, axis=1, keepdims=True)
    line = lax.broadcasted_iota(jnp.int32, (48, SLOTS), 1)
    which = lax.broadcasted_iota(jnp.int32, (48, SLOTS), 0)
    row = jnp.sum(jnp.where(line == which, totals, 0.0), axis=0, keepdims=True)
    out[...] = jnp.broadcast_to(row, (PARTNERS, SLOTS))
    send[0:4] = edge[c]
    first = 2 * (1 - c)
    send[4] = a2f[first, near]
    send[5] = a2f[first + 1, near]
    send[6] = af[3 - c, near]
    send[7] = au[3 - c, near]


def steps(m0, m1, m2, m3):
    alpha = m0 / m1
    second = (m1 / m0) * ((m0 * m2 - m1 * m1) / (m1 * m3 - m2 * m2))
    second = jnp.clip(second, 1.0 / (12.0 + SHIFT), 1.0 / SHIFT)
    return alpha + second * ((m0 * m2) / (m1 * m1)), -second * alpha


def solve_kernel(gathered, mobility, tension, coef_out, params):
    total = jnp.sum(gathered[...], axis=0, keepdims=True)
    line = lax.broadcasted_iota(jnp.int32, (1, SLOTS), 1)

    def s(k):
        return jnp.sum(jnp.where(line == k, total, 0.0), axis=1, keepdims=True)

    c0, c1 = steps(s(0), s(1), s(2), s(3))
    uu = [s(4 + k) for k in range(4)]
    uf = [s(8 + k) for k in range(5)]
    ff = [s(13 + k) for k in range(6)]
    moments = [
        uu[k] - 2.0 * (c0 * uf[k] + c1 * uf[k + 1])
        + (c0 * c0) * ff[k] + (2.0 * c0 * c1) * ff[k + 1] + (c1 * c1) * ff[k + 2]
        for k in range(4)
    ]
    e0, e1 = steps(*moments)
    coef = (e0, e1, -e0 * c0, -(e0 * c1 + e1 * c0), -e1 * c1, -c0, -c1)
    for j in range(7):
        coef_out[j : j + 1] = jnp.broadcast_to(coef[j], (1, CY))

    def meet(k):
        value = coef[0] * s(19 + 7 * k)
        for j in range(1, 7):
            value = value + coef[j] * s(19 + 7 * k + j)
        return value

    scale = 1.0 / (256 * 64 * 256)
    g0 = DT * s(40)
    g1 = DT * (s(41) - meet(0))
    g2 = DT * (s(42) - meet(1))
    g3 = -((DT * mobility) * s(44) + (DT * tension) * (s(43) - meet(2)))
    place = lax.broadcasted_iota(jnp.int32, (1, CY), 1)
    packed = jnp.where(place == 0, g0, jnp.where(place == 1, g1, jnp.where(place == 2, g2, g3)))
    params[...] = (packed * scale)[0, 0:4]
    return coef


def half_step(side, halo, coef, consts, basis, state, work, write):
    mobility, tension, viscosity, interface = consts
    uu, f, af, a2f, bb, ab, au = basis
    e, q, adj4, pot, g, gv, base = state
    phi, pr, pa, adj, qe, new = work
    near = pl.ds(NEAR, NARROW)
    for i in range(2):
        qe[i, 5 * side, near] = halo(i)
        adj[6 * side + i, near] = halo(2 + i)

    def mixed(terms):
        value = coef[0] * terms[0]
        for a, t in zip(coef[1:], terms[1:]):
            value = value + a * t
        return value

    i = 1 + 5 * side
    phi[i, near] = mixed([
        uu[i, near], au[i - 1, near], f[i, near], af[i - 1, near], halo(5 - side), bb[i + 2, near], ab[i, near],
    ])
    i = 7 * side
    phi[i, near] = mixed([uu[i, near], halo(7), f[i, near], halo(6), halo(4 + side), bb[i + 2, near], ab[i, near]])

    def project(t):
        c = phi[t + 1]
        r0 = q[0, t] + 0.5 * (phi[t + 2] - phi[t])
        r1 = qe[0, t] + dx(c)
        r2 = qe[1, t] + dy(c)
        pr[0, t] = r0
        pr[1, t] = r1
        pr[2, t] = r2
        lap = lap_of(adj[t + 1], adj[t + 2], adj[t])
        pa[t] = (DT * mobility) * lap + (DT * tension) * (r0 * g[0, t] + r1 * g[1, t] + r2 * g[2, t])

    for t in new:
        project(t)

    def at(field, z):
        return e[BASE[field] + HALO[field] + z]

    for n in range(2):
        t = 2 * side + n
        v1, v2 = at(V1, t), at(V2, t)
        v0u, v0d = at(V0, t + 1), at(V0, t - 1)
        here = pot[t + 1]
        ph = own(at(PH, t))
        lam = pa[t + 1]
        up = v0u * adj[t + 3] - tension * (pot[t + 2] * pr[0, t + 2])
        dn = v0d * adj[t + 1] - tension * (pot[t] * pr[0, t])
        div = 0.5 * (up - dn) - tension * (dx(here * pr[1, t + 1]) + dy(here * pr[2, t + 1]))
        value = base[t] + DT * own(div) + (3.0 * ph * ph - 1.0) * own(lam)
        write(n, 0, value - interface * own(lap_of(lam, pa[t + 2], pa[t])))
        r = [pr[i, t + 1] for i in range(3)]
        mine = [own(a) for a in r]
        c = own(adj[t + 2])
        for k in range(3):
            mix = mine[0] * gv[k, 0, t] + mine[1] * gv[k, 1, t] + mine[2] * gv[k, 2, t]
            moved = (viscosity + 0.5 * v0u) * pr[k, t + 2] + (viscosity - 0.5 * v0d) * pr[k, t]
            moved = moved + x_up((viscosity + 0.5 * v1) * r[k]) + x_dn((viscosity - 0.5 * v1) * r[k])
            moved = moved + y_up((viscosity + 0.5 * v2) * r[k]) + y_dn((viscosity - 0.5 * v2) * r[k])
            moved = own(moved) - (6.0 * viscosity) * mine[k]
            write(n, 1 + k, mine[k] + DT * (moved - mix - c * own(g[k, t + 1])))


def constants(coefs):
    return 0.1 * coefs[0], 0.5 * coefs[1], 0.1 * coefs[2], 0.5 * coefs[3]


def near_kernel(
    coefs, gathered, uu, f, af, a2f, bb, ab, au, ri, e, q, adj4, pot, g, gv, base,
    params, table, phi_own, shared, result, phi, pr, pa, adj, qe,
):
    consts = constants(coefs)
    coef = solve_kernel(gathered, consts[0], consts[1], table, params)
    side = lax.axis_index("gy")
    adj[2:6] = adj4[...]
    for i in range(2):
        qe[i, 1:5] = q[i + 1, 1:5]
    for z in range(CZ):
        value = coef[0] * uu[z + 2] + coef[1] * au[z + 1] + coef[2] * f[z + 2] + coef[3] * af[z + 1]
        value = value + coef[4] * a2f[z] + coef[5] * bb[z + 4] + coef[6] * ab[z + 2]
        phi[z + 2] = value
        phi_own[z] = value

    def write(n, k, value):
        result[k, n] = value

    new = [2 * side + n for n in range(4)]
    half_step(
        side, lambda j: ri[j], coef, consts, (uu, f, af, a2f, bb, ab, au), (e, q, adj4, pot, g, gv, base),
        (phi, pr, pa, adj, qe, new), write,
    )
    for n in range(2):
        for i in range(3):
            shared[i, n] = pr[i, 2 + n]
        shared[3, n] = pa[2 + n]


def far_kernel(
    coefs, table, uu, f, af, a2f, bb, ab, au, si, e, q, adj4, pot, g, gv, base, phi_own, shared, result,
    phase_back, velocity_back, phi, pr, pa, adj, qe,
):
    consts = constants(coefs)
    coef = [table[j : j + 1, 0:1] for j in range(7)]
    mine = lax.axis_index("gy")
    side = 1 - mine
    adj[2:6] = adj4[...]
    for i in range(2):
        qe[i, 1:5] = q[i + 1, 1:5]
    phi[2:6] = phi_own[...]
    for n in range(2):
        for i in range(3):
            pr[i, 2 + n] = shared[i, n]
        pa[2 + n] = shared[3, n]

    def write(n, k, value):
        if k == 0:
            phase_back[2 * side + n] = value
        else:
            velocity_back[k - 1, 2 * side + n] = value

    new = [4 * side + n for n in range(2)]
    half_step(
        side, lambda j: other_first(si[j]), coef, consts, (uu, f, af, a2f, bb, ab, au),
        (e, q, adj4, pot, g, gv, base), (phi, pr, pa, adj, qe, new), write,
    )
    for n in range(2):
        phase_back[2 * mine + n] = result[0, n]
        for k in range(3):
            velocity_back[k, 2 * mine + n] = result[1 + k, n]


def f32(*shape):
    return jax.ShapeDtypeStruct(shape, jnp.float32)


def layers(*lead):
    return f32(*lead, ROWS, LANES)


def scratch(*lead):
    return pltpu.VMEM((*lead, ROWS, LANES), jnp.float32)


VM = pl.BlockSpec(memory_space=pltpu.VMEM)
SM = pl.BlockSpec(memory_space=pltpu.SMEM)
PARAMS = pltpu.CompilerParams(vmem_limit_bytes=12 * 1024 * 1024)
SWAP = [(0, 1), (1, 0)]


def role_shift(value, cross):
    gx, gy, gz = (lax.axis_size(a) for a in ("gx", "gy", "gz"))
    pairs = []
    for x in range(gx):
        for y in range(gy):
            for i in range(gz):
                target = (1 - x if cross else x, y, (i + 1 - 2 * y) % gz)
                pairs.append(((x * gy + y) * gz + i, (target[0] * gy + y) * gz + target[2]))
    return lax.ppermute(value, ("gx", "gy", "gz"), pairs)


def ring(value, step):
    count = lax.axis_size("gz")
    return lax.ppermute(value, "gz", [(i, (i + step) % count) for i in range(count)])


def swap(value):
    return lax.ppermute(value, "gy", SWAP)


def call(kernel, outs, ins, scratches, name, smem, aliases={}):
    return pl.pallas_call(
        kernel,
        out_shape=outs,
        in_specs=[SM] * smem + [VM] * (len(ins) - smem),
        out_specs=jax.tree.map(lambda _: VM, outs),
        scratch_shapes=scratches,
        input_output_aliases=aliases,
        compiler_params=PARAMS,
        name=name,
    )(*ins)


def local(phase, velocity, phase_obs, velocity_obs, coefs):
    mine = (velocity, phase, phase_obs, velocity_obs)
    stack, edges, coefs, give = pl.pallas_call(
        load_kernel,
        out_shape=(f32(8 * CZ, CX, CY), f32(EDGE_ROWS, CY), f32(4), f32(len(SENT), CX, CY)),
        in_specs=[pl.BlockSpec(memory_space=pltpu.HBM)] * 5,
        out_specs=(VM,) * 4,
        scratch_shapes=[pltpu.SemaphoreType.DMA((9,))],
        compiler_params=PARAMS,
        name="load",
    )(*(pltpu.with_memory_space_constraint(a, pltpu.HBM) for a in (*mine, coefs)))
    peer = swap(stack)
    gxr = lax.ppermute(edges, "gx", SWAP)
    main, diag = call(
        pack_kernel,
        (f32(len(SENT), CX, LANES), f32(CORNER_ROWS, LANES)),
        (stack, swap(give)),
        [],
        "pack",
        0,
    )
    mr = role_shift(main, False)
    dr = role_shift(diag, True)
    gxr, mr, dr = lax.optimization_barrier((gxr, mr, dr))
    gxs = swap(gxr)
    inner = call(inner_kernel, layers(TOTAL), (stack, peer, gxr, gxs), [], "inner", 0)
    ms = swap(mr)
    ds = swap(dr)
    e, b, u, q, pot, lph, g, lv, send, corner, rim, far = call(
        first_kernel,
        (layers(TOTAL), layers(4), layers(4), layers(3, 6), layers(6), layers(6), layers(3, 6), layers(3, 6),
         f32(CX * len(AGAIN), LANES), f32(AGAIN_ROWS, LANES), f32(RIM_ROWS, CY), f32(CX, LANES)),
        (coefs, inner, mr, ms, dr, ds),
        [scratch(6)],
        "first",
        1,
        {1: 0},
    )
    r2 = role_shift(send, False)
    d2 = role_shift(corner, True)
    x2 = lax.ppermute(rim, "gx", SWAP)
    far = ring(far, -2)
    adj, w, part, edge, gv, base = call(
        weight_kernel,
        (layers(4), f32(3, CZ, CX, LANES), f32(5, 8, CY), f32(2, 4, NARROW, LANES), f32(3, 3, CZ, CX, CY), f32(CZ, CX, CY)),
        (coefs, e, q, pot, lph, g, lv),
        [],
        "weights",
        1,
    )
    r2, d2, x2, far, w, part, edge = lax.optimization_barrier((r2, d2, x2, far, w, part, edge))
    s2, ds2, xs2 = swap(r2), swap(d2), swap(x2)
    sums, bb, uu, f, af, a2f, ab, au, send = call(
        moment_kernel,
        (f32(PARTNERS, SLOTS), layers(13), layers(8), layers(9), layers(7), layers(5), layers(8), layers(6),
         f32(8, NARROW, LANES)),
        (b, u, r2, s2, d2, ds2, x2, xs2, far, w, part, edge),
        [scratch(4), scratch(4)],
        "moments",
        0,
    )
    ri = role_shift(send, False)
    gathered = lax.all_to_all(sums.reshape(PARTNERS, 1, SLOTS), ("gx", "gz"), 0, 0).reshape(PARTNERS, SLOTS)
    ri, gathered = lax.optimization_barrier((ri, gathered))
    si = swap(ri)
    basis = (uu, f, af, a2f, bb, ab, au)
    state = (e, q, adj, pot, g, gv, base)
    room = [scratch(8), scratch(3, 6), scratch(6), scratch(8), scratch(2, 6)]
    params, table, phi, shared, result = call(
        near_kernel,
        (f32(4), f32(8, CY), layers(4), layers(4, 2), f32(4, 2, CX, CY)),
        (coefs, gathered, *basis, ri, *state),
        room,
        "near",
        1,
    )
    phase_back, velocity_back = call(
        far_kernel,
        (f32(CZ, CX, CY), f32(3, CZ, CX, CY)),
        (coefs, table, *basis, si, *state, phi, shared, result),
        room,
        "far",
        1,
    )
    return phase_back, velocity_back, params


def solution(mesh):
    return jax.shard_map(
        local,
        mesh=mesh,
        in_specs=(
            P("gz", "gx", "gy"),
            P(None, "gz", "gx", "gy"),
            P("gz", "gx", "gy"),
            P(None, "gz", "gx", "gy"),
            P(),
        ),
        out_specs=(P("gz", "gx", "gy"), P(None, "gz", "gx", "gy"), P()),
        check_vma=False,
    )
```

```python
import jax
import jax.numpy as jnp
from jax import lax
from jax.experimental import pallas as pl
from jax.experimental.pallas import tpu as pltpu
from jax.sharding import PartitionSpec as P

DT = 0.1
SHIFT = 0.01
CZ, CX, CY = 4, 32, 128
HX = 8
NEAR = 4
NARROW = (CX + 2 * HX) - 2 * NEAR
ROWS = CX + 2 * HX
LANES = 2 * CY
PARTNERS = 128

V0, V1, V2, PH, PO, O0, O1, O2 = range(8)
HALO = (2, 1, 1, 2, 0, 1, 0, 0)
BASE = []
_at = 0
for _h in HALO:
    BASE.append(_at)
    _at += CZ + 2 * _h
TOTAL = _at
SENT = [(f, k) for f, h in enumerate(HALO) for k in range(1, h + 1)]
CORNER = [{(V0, 1): 1, (V1, 1): 1, (V2, 1): 1, (PH, 1): 3, (PH, 2): 2}.get(entry, 0) for entry in SENT]
CORNER_ROWS = 2 * sum(CORNER)
EDGE = (2, 2, 2, 4, 2, 1, 1, 1)
EDGE_ROWS = 2 * CZ * sum(EDGE)
AGAIN = [("b", k, 6 - k) for k in (1, 2, 3, 4)] + [("u", k, 3 - k) for k in (1, 2)]
AGAIN_ROWS = 2 * sum(w for _, _, w in AGAIN)
RIM = [("b", z, 6) for z in range(CZ)] + [("u", z, 3) for z in range(CZ)]
RIM_ROWS = 2 * sum(w for _, _, w in RIM)
THIRD = (CX, CX, CX + 2, CX, CX + 2, CX, CX, CX)
THIRD_AT = [sum(THIRD[:n]) for n in range(8)]
THIRD_ROWS = -(-sum(THIRD) // 8) * 8
NUM_SUMS = 45
SLOTS = 64


def x_up(a):
    return pltpu.roll(a, a.shape[0] - 1, 0)


def x_dn(a):
    return pltpu.roll(a, 1, 0)


def y_up(a):
    return pltpu.roll(a, a.shape[1] - 1, 1)


def y_dn(a):
    return pltpu.roll(a, 1, 1)


def dx(a):
    return 0.5 * (x_up(a) - x_dn(a))


def dy(a):
    return 0.5 * (y_up(a) - y_dn(a))


def own(a):
    return a[HX : HX + CX, :CY]


def lap_of(c, zu, zd):
    return (zu + zd) + (x_up(c) + x_dn(c)) + (y_up(c) + y_dn(c)) - 6.0 * c


def other_first(a):
    return jnp.concatenate([a[:, CY:], a[:, :CY]], 1)


def outgoing(core, k):
    return (CZ - k) * (1 - core) + (k - 1) * core


def loop(count, body):
    def step(t, carry):
        body(t)
        return carry

    lax.fori_loop(0, count, step, 0, unroll=count)


def low_high(core, mine, theirs):
    theirs = other_first(theirs)
    return jnp.where(core == 0, mine, theirs), jnp.where(core == 0, theirs, mine)


def load_kernel(vel, ph, po, vo, coefs, stack, out, coefs_out, give, sems):
    copies = [
        pltpu.make_async_copy(ph, stack.at[pl.ds(CZ * PH, CZ)], sems.at[6]),
        pltpu.make_async_copy(po, stack.at[pl.ds(CZ * PO, CZ)], sems.at[7]),
        pltpu.make_async_copy(coefs, coefs_out, sems.at[8]),
    ]
    for i in range(3):
        copies.append(pltpu.make_async_copy(vel.at[i], stack.at[pl.ds(CZ * (V0 + i), CZ)], sems.at[i]))
        copies.append(pltpu.make_async_copy(vo.at[i], stack.at[pl.ds(CZ * (O0 + i), CZ)], sems.at[3 + i]))
    for copy in copies:
        copy.start()
    for copy in copies:
        copy.wait()
    other = 1 - lax.axis_index("gy")
    for n, (f, k) in enumerate(SENT):
        give[n] = stack[CZ * f + outgoing(other, k)]
    row = 0
    for f, w in enumerate(EDGE):
        for z in range(CZ):
            out[row : row + w] = stack[CZ * f + z, CX - w :]
            out[row + w : row + 2 * w] = stack[CZ * f + z, :w]
            row += 2 * w


def pack_kernel(stack, got, main, diag):
    c = lax.axis_index("gy")
    row = 0
    for n, (f, k) in enumerate(SENT):
        src = jnp.concatenate([stack[CZ * f + outgoing(c, k)], got[n]], 1)
        main[n] = src
        w = CORNER[n]
        if w:
            diag[row : row + w] = src[CX - w :]
            diag[row + w : row + 2 * w] = src[:w]
        row += 2 * w


def inner_kernel(stack, peer, gxr, gxs, e):
    row = 0
    for f, w in enumerate(EDGE):
        mid = BASE[f] + HALO[f]
        for z in range(CZ):
            for half, x in enumerate((gxr, gxs)):
                lanes = pl.ds(CY * half, CY)
                e[mid + z, HX : HX + CX, lanes] = (stack, peer)[half][CZ * f + z]
                e[mid + z, HX - w : HX, lanes] = x[row : row + w]
                e[mid + z, HX + CX : HX + CX + w, lanes] = x[row + w : row + 2 * w]
            row += 2 * w


def at(e, field, z):
    return e[BASE[field] + HALO[field] + z]


def middle(a):
    return a[HX : HX + CX]


def provisional(e, field, z, grad, here, tension, viscosity):
    a = at(e, field, z)
    zu, zd = at(e, field, z + 1), at(e, field, z - 1)
    xu, xd, yu, yd = x_up(a), x_dn(a), y_up(a), y_dn(a)
    lap = (zu + zd) + (xu + xd) + (yu + yd) - 6.0 * a
    advect = at(e, V0, z) * (zu - zd) + at(e, V1, z) * (xu - xd) + at(e, V2, z) * (yu - yd)
    value = a - (0.5 * DT) * advect + (DT * viscosity) * lap + (DT * tension) * (here * grad)
    return value, lap


def first_kernel(coefs, inner, mr, ms, dr, ds, e, b, u, send, corner, rim, far, pot, p0):
    tension = 0.5 * coefs[1]
    viscosity = 0.1 * coefs[2]
    interface = 0.5 * coefs[3]
    c = lax.axis_index("gy")

    row = 0
    for n, (f, k) in enumerate(SENT):
        below, above = BASE[f] + HALO[f] - k, BASE[f] + HALO[f] + CZ + k - 1
        lo, hi = low_high(c, mr[n], ms[n])
        e[below, HX : HX + CX] = lo
        e[above, HX : HX + CX] = hi
        w = CORNER[n]
        if w == 0:
            continue
        lo, hi = low_high(c, dr[row : row + 2 * w], ds[row : row + 2 * w])
        for layer, part in ((below, lo), (above, hi)):
            e[layer, HX - w : HX] = part[:w]
            e[layer, HX + CX : HX + CX + w] = part[w:]
        row += 2 * w

    def potential(t):
        z = t - 1
        a = at(e, PH, z)
        pot[t] = a * a * a - a - interface * lap_of(a, at(e, PH, z + 1), at(e, PH, z - 1))

    loop(6, potential)

    def along(t):
        z = t - 1
        grad = 0.5 * (at(e, PH, z + 1) - at(e, PH, z - 1))
        value, _ = provisional(e, V0, z, grad, pot[t], tension, viscosity)
        p0[t] = middle(value)

    loop(6, along)

    def across(z):
        phase = at(e, PH, z)
        p1, _ = provisional(e, V1, z, dx(phase), pot[z + 1], tension, viscosity)
        p2, _ = provisional(e, V2, z, dy(phase), pot[z + 1], tension, viscosity)
        div = 0.5 * (p0[z + 2] - p0[z]) + middle(dx(p1) + dy(p2))
        b[z] = -div
        seen = 0.5 * middle(at(e, O0, z + 1) - at(e, O0, z - 1)) + middle(dx(at(e, O1, z)) + dy(at(e, O2, z)))
        u[z] = div - seen

    loop(4, across)

    row = 0
    for n, (name, k, w) in enumerate(AGAIN):
        src = (b if name == "b" else u)[outgoing(c, k)]
        send[CX * n : CX * (n + 1)] = src
        corner[row : row + w] = src[CX - w :]
        corner[row + w : row + 2 * w] = src[:w]
        row += 2 * w
    row = 0
    for name, z, w in RIM:
        field = b if name == "b" else u
        rim[row : row + w] = field[z, CX - w :, :CY]
        rim[row + w : row + 2 * w] = field[z, :w, :CY]
        row += 2 * w
    far[...] = b[0]


def folded(a):
    a = a[:, :CY] + a[:, CY:]
    return (a[0:8] + a[8:16]) + (a[16:24] + a[24:32])


def weight_kernel(coefs, e, adj, w, part, edge, gv, base, pot, g, q, lph, lv, p0):
    mobility, tension, viscosity, interface = constants(coefs)

    def forward(t):
        z = t - 1
        a = at(e, PH, z)
        lap = lap_of(a, at(e, PH, z + 1), at(e, PH, z - 1))
        lph[t] = lap
        here = a * a * a - a - interface * lap
        pot[t] = here
        g[0, t] = 0.5 * (at(e, PH, z + 1) - at(e, PH, z - 1))
        g[1, t] = dx(a)
        g[2, t] = dy(a)
        value, lv[0, t] = provisional(e, V0, z, g[0, t], here, tension, viscosity)
        q[0, t] = value - at(e, O0, z)

    loop(6, forward)

    def across(z):
        here = pot[z + 1]
        p1, lv[1, z] = provisional(e, V1, z, g[1, z + 1], here, tension, viscosity)
        p2, lv[2, z] = provisional(e, V2, z, g[2, z + 1], here, tension, viscosity)
        q[1, z + 1] = p1 - at(e, O1, z)
        q[2, z + 1] = p2 - at(e, O2, z)

    loop(4, across)
    sums = [jnp.zeros((8, CY), jnp.float32)] * 5
    for t in range(CZ):
        here = pot[t + 1]
        lap = lph[t + 1]
        gs = [g[i, t + 1] for i in range(3)]
        up, dn = pot[t + 2] * g[0, t + 2], pot[t] * g[0, t]
        w1 = 0.5 * (up - dn) + dx(here * gs[1]) + dy(here * gs[2])
        w2 = 0.5 * (lv[0, t + 2] - lv[0, t]) + dx(lv[1, t]) + dy(lv[2, t])
        up, dn = lph[t + 2] * g[0, t + 2], lph[t] * g[0, t]
        w3 = 0.5 * (up - dn) + dx(lap * gs[1]) + dy(lap * gs[2])
        w[0, t] = middle(w1)
        w[1, t] = middle(w2)
        w[2, t] = middle(w3)
        lap_pot = lap_of(here, pot[t + 2], pot[t])
        lap_lap = lap_of(lap, lph[t + 2], lph[t])
        flow = at(e, V0, t) * gs[0] + at(e, V1, t) * gs[1] + at(e, V2, t) * gs[2]
        c = at(e, PH, t) - DT * flow + (DT * mobility) * lap_pot - at(e, PO, t)
        adj[t] = c
        v1, v2 = at(e, V1, t), at(e, V2, t)
        base[t] = own(c + DT * (dx(v1 * c) + dy(v2 * c)))
        for i, field in enumerate((V0, V1, V2)):
            a = at(e, field, t)
            gv[0, i, t] = own(0.5 * (at(e, field, t + 1) - at(e, field, t - 1)))
            gv[1, i, t] = own(dx(a))
            gv[2, i, t] = own(dy(a))
        qs = [q[i, t + 1] for i in range(3)]
        qg = qs[0] * gs[0] + qs[1] * gs[1] + qs[2] * gs[2]
        ql = qs[0] * lv[0, t + 1] + qs[1] * lv[1, t] + qs[2] * lv[2, t]
        terms = (middle(c * lap_pot), middle(here * qg), middle(ql), middle(lap * qg), middle(c * lap_lap))
        sums = [s + folded(a) for s, a in zip(sums, terms)]
    for k in range(5):
        part[k] = sums[k]
    c = lax.axis_index("gy")
    pieces = (q[1, 1 + outgoing(c, 1)], q[2, 1 + outgoing(c, 1)], adj[outgoing(c, 1)], adj[outgoing(c, 2)])
    for n, src in enumerate(pieces):
        w = (THIRD[n] - CX) // 2
        edge[THIRD_AT[n] : THIRD_AT[n] + THIRD[n]] = src[HX - w : HX + CX + w]


def shifted(c, zu, zd):
    return (6.0 + SHIFT) * c - ((zu + zd) + (x_up(c) + x_dn(c)) + (y_up(c) + y_dn(c)))


def moment_kernel(b4, u4, r, s, d, ds, x, xs, far, fars, w, part, edge, out, bb, uu, f, af, a2f, ab, au, send, a2b, a2u):
    c = lax.axis_index("gy")
    near = pl.ds(NEAR, NARROW)
    bb[4:8, HX : HX + CX] = b4[...]
    uu[2:6, HX : HX + CX] = u4[...]
    row = 0
    for n, (name, k, width) in enumerate(AGAIN):
        dst, below = (bb, 4 - k) if name == "b" else (uu, 2 - k)
        above = 7 + k if name == "b" else 5 + k
        lo, hi = low_high(c, r[CX * n : CX * (n + 1)], s[CX * n : CX * (n + 1)])
        dst[below, HX : HX + CX] = lo
        dst[above, HX : HX + CX] = hi
        lo, hi = low_high(c, d[row : row + 2 * width], ds[row : row + 2 * width])
        for layer, part_rows in ((below, lo), (above, hi)):
            dst[layer, HX - width : HX] = part_rows[:width]
            dst[layer, HX + CX : HX + CX + width] = part_rows[width:]
        row += 2 * width
    row = 0
    for name, z, width in RIM:
        dst, layer = (bb, 4 + z) if name == "b" else (uu, 2 + z)
        for half, src in enumerate((x, xs)):
            lanes = pl.ds(CY * half, CY)
            dst[layer, HX - width : HX, lanes] = src[row : row + width]
            dst[layer, HX + CX : HX + CX + width, lanes] = src[row + width : row + 2 * width]
        row += 2 * width
    bb[12, HX : HX + CX] = jnp.where(c == 1, far[...], other_first(fars[...]))

    def wide(t):
        a = bb[t + 2]
        across = (pltpu.roll(a, ROWS - 2, 0) + pltpu.roll(a, 2, 0)) + (
            pltpu.roll(a, LANES - 2, 1) + pltpu.roll(a, 2, 1)
        )
        f[t] = 0.25 * ((bb[t + 4] + bb[t]) + across) - 1.5 * a

    loop(9, wide)

    def apply(src, dst, count):
        def body(t):
            dst[t] = shifted(src[t + 1], src[t + 2], src[t])

        loop(count, body)

    apply(f, af, 7)
    apply(af, a2f, 5)
    apply(bb.at[pl.ds(1, 10)], ab, 8)
    apply(ab.at[pl.ds(1, 6)], a2b, 4)
    apply(uu, au, 6)
    apply(au, a2u, 4)

    rows = pl.ds(HX, CX)
    acc = [jnp.zeros((8, CY), jnp.float32)] * 40
    for t in range(CZ):
        vb, vab, va2b = bb[t + 4, rows], ab[t + 2, rows], a2b[t, rows]
        vu, vau, va2u = uu[t + 2, rows], au[t + 1, rows], a2u[t, rows]
        vf, vaf, va2f = f[t + 2, rows], af[t + 1, rows], a2f[t, rows]
        a = a2f[t]
        across = (x_up(a) + x_dn(a)) + (y_up(a) + y_dn(a))
        va3f = (6.0 + SHIFT) * va2f - (2.0 * a2f[t + 1, rows] + middle(across))
        terms = [
            vb * vb, vb * vab, vab * vab, vab * va2b,
            vu * vu, vu * vau, vau * vau, vau * va2u,
            vu * vf, vu * vaf, vu * va2f, vau * va2f, va2u * va2f,
            vf * vf, vf * vaf, vaf * vaf, vaf * va2f, va2f * va2f, va2f * va3f,
        ]
        for k in range(3):
            wk = w[k, t]
            terms += [a * wk for a in (vu, vau, vf, vaf, va2f, vb, vab)]
        acc = [x + folded(a) for x, a in zip(acc, terms)]
    rows_list = [jnp.sum(a, axis=0, keepdims=True) for a in acc]
    rows_list += [jnp.sum(part[k], axis=0, keepdims=True) for k in range(5)]
    rows_list += [jnp.zeros((1, CY), jnp.float32)] * (48 - NUM_SUMS)
    table = jnp.concatenate(rows_list, axis=0)
    totals = jnp.sum(table, axis=1, keepdims=True)
    line = lax.broadcasted_iota(jnp.int32, (48, SLOTS), 1)
    which = lax.broadcasted_iota(jnp.int32, (48, SLOTS), 0)
    row = jnp.sum(jnp.where(line == which, totals, 0.0), axis=0, keepdims=True)
    out[...] = jnp.broadcast_to(row, (PARTNERS, SLOTS))
    send[0 : THIRD_AT[4]] = edge[...]
    pieces = (a2f[outgoing(c, 1)], a2f[outgoing(c, 2)], af[1 + outgoing(c, 2)], au[1 + outgoing(c, 2)])
    for n, src in enumerate(pieces, 4):
        w = (THIRD[n] - CX) // 2
        send[THIRD_AT[n] : THIRD_AT[n] + THIRD[n]] = src[HX - w : HX + CX + w]


def steps(m0, m1, m2, m3):
    alpha = m0 / m1
    second = (m1 / m0) * ((m0 * m2 - m1 * m1) / (m1 * m3 - m2 * m2))
    second = jnp.clip(second, 1.0 / (12.0 + SHIFT), 1.0 / SHIFT)
    return alpha + second * ((m0 * m2) / (m1 * m1)), -second * alpha


def solve_kernel(gathered, mobility, tension, coef_out, params):
    total = jnp.sum(gathered[...], axis=0, keepdims=True)
    line = lax.broadcasted_iota(jnp.int32, (1, SLOTS), 1)

    def s(k):
        return jnp.sum(jnp.where(line == k, total, 0.0), axis=1, keepdims=True)

    c0, c1 = steps(s(0), s(1), s(2), s(3))
    uu = [s(4 + k) for k in range(4)]
    uf = [s(8 + k) for k in range(5)]
    ff = [s(13 + k) for k in range(6)]
    moments = [
        uu[k] - 2.0 * (c0 * uf[k] + c1 * uf[k + 1])
        + (c0 * c0) * ff[k] + (2.0 * c0 * c1) * ff[k + 1] + (c1 * c1) * ff[k + 2]
        for k in range(4)
    ]
    e0, e1 = steps(*moments)
    coef = (e0, e1, -e0 * c0, -(e0 * c1 + e1 * c0), -e1 * c1, -c0, -c1)
    for j in range(7):
        coef_out[j : j + 1] = jnp.broadcast_to(coef[j], (1, CY))

    def meet(k):
        value = coef[0] * s(19 + 7 * k)
        for j in range(1, 7):
            value = value + coef[j] * s(19 + 7 * k + j)
        return value

    scale = 1.0 / (256 * 64 * 256)
    g0 = DT * s(40)
    g1 = DT * (s(41) - meet(0))
    g2 = DT * (s(42) - meet(1))
    g3 = -((DT * mobility) * s(44) + (DT * tension) * (s(43) - meet(2)))
    place = lax.broadcasted_iota(jnp.int32, (1, CY), 1)
    packed = jnp.where(place == 0, g0, jnp.where(place == 1, g1, jnp.where(place == 2, g2, g3)))
    params[...] = (packed * scale)[0, 0:4]
    return coef


def half_step(side, halo, coef, consts, basis, state, work, write):
    mobility, tension, viscosity, interface = consts
    uu, f, af, a2f, bb, ab, au = basis
    e, q, adj4, pot, g, gv, base = state
    phi, pr, pa, adj, qe, new = work
    inside, wider = pl.ds(HX, CX), pl.ds(HX - 1, CX + 2)
    for i in range(2):
        qe[i, 5 * side, inside] = halo(i)
    adj[1 + 5 * side, wider] = halo(2)
    adj[7 * side, inside] = halo(3)

    def mixed(terms):
        value = coef[0] * terms[0]
        for a, t in zip(coef[1:], terms[1:]):
            value = value + a * t
        return value

    i = 1 + 5 * side
    phi[i, wider] = mixed([
        uu[i, wider], au[i - 1, wider], f[i, wider], af[i - 1, wider], halo(4), bb[i + 2, wider], ab[i, wider],
    ])
    i = 7 * side
    phi[i, inside] = mixed([
        uu[i, inside], halo(7), f[i, inside], halo(6), halo(5), bb[i + 2, inside], ab[i, inside],
    ])

    def project(t):
        c = phi[t + 1]
        r0 = q[0, t] + 0.5 * (phi[t + 2] - phi[t])
        r1 = qe[0, t] + dx(c)
        r2 = qe[1, t] + dy(c)
        pr[0, t] = r0
        pr[1, t] = r1
        pr[2, t] = r2
        lap = lap_of(adj[t + 1], adj[t + 2], adj[t])
        pa[t] = (DT * mobility) * lap + (DT * tension) * (r0 * g[0, t] + r1 * g[1, t] + r2 * g[2, t])

    for t in new:
        project(t)

    for n in range(2):
        t = 2 * side + n
        v1, v2 = at(e, V1, t), at(e, V2, t)
        v0u, v0d = at(e, V0, t + 1), at(e, V0, t - 1)
        here = pot[t + 1]
        ph = own(at(e, PH, t))
        lam = pa[t + 1]
        up = v0u * adj[t + 3] - tension * (pot[t + 2] * pr[0, t + 2])
        dn = v0d * adj[t + 1] - tension * (pot[t] * pr[0, t])
        div = 0.5 * (up - dn) - tension * (dx(here * pr[1, t + 1]) + dy(here * pr[2, t + 1]))
        value = base[t] + DT * own(div) + (3.0 * ph * ph - 1.0) * own(lam)
        write(n, 0, value - interface * own(lap_of(lam, pa[t + 2], pa[t])))
        r = [pr[i, t + 1] for i in range(3)]
        mine = [own(a) for a in r]
        c = own(adj[t + 2])
        for k in range(3):
            mix = mine[0] * gv[k, 0, t] + mine[1] * gv[k, 1, t] + mine[2] * gv[k, 2, t]
            moved = (viscosity + 0.5 * v0u) * pr[k, t + 2] + (viscosity - 0.5 * v0d) * pr[k, t]
            moved = moved + x_up((viscosity + 0.5 * v1) * r[k]) + x_dn((viscosity - 0.5 * v1) * r[k])
            moved = moved + y_up((viscosity + 0.5 * v2) * r[k]) + y_dn((viscosity - 0.5 * v2) * r[k])
            moved = own(moved) - (6.0 * viscosity) * mine[k]
            write(n, 1 + k, mine[k] + DT * (moved - mix - c * own(g[k, t + 1])))


def constants(coefs):
    return 0.1 * coefs[0], 0.5 * coefs[1], 0.1 * coefs[2], 0.5 * coefs[3]


def near_kernel(
    coefs, gathered, uu, f, af, a2f, bb, ab, au, ri, e, q, adj4, pot, g, gv, base,
    params, table, phi_own, shared, result, phi, pr, pa, adj, qe,
):
    consts = constants(coefs)
    coef = solve_kernel(gathered, consts[0], consts[1], table, params)
    side = lax.axis_index("gy")
    adj[2:6] = adj4[...]
    for i in range(2):
        qe[i, 1:5] = q[i + 1, 1:5]
    for z in range(CZ):
        value = coef[0] * uu[z + 2] + coef[1] * au[z + 1] + coef[2] * f[z + 2] + coef[3] * af[z + 1]
        value = value + coef[4] * a2f[z] + coef[5] * bb[z + 4] + coef[6] * ab[z + 2]
        phi[z + 2] = value
        phi_own[z] = value

    def write(n, k, value):
        result[k, n] = value

    new = [2 * side + n for n in range(4)]
    half_step(
        side, lambda n: ri[THIRD_AT[n] : THIRD_AT[n] + THIRD[n]], coef, consts, (uu, f, af, a2f, bb, ab, au), (e, q, adj4, pot, g, gv, base),
        (phi, pr, pa, adj, qe, new), write,
    )
    for n in range(2):
        for i in range(3):
            shared[i, n] = pr[i, 2 + n]
        shared[3, n] = pa[2 + n]


def far_kernel(
    coefs, table, uu, f, af, a2f, bb, ab, au, si, e, q, adj4, pot, g, gv, base, phi_own, shared, result,
    phase_back, velocity_back, phi, pr, pa, adj, qe,
):
    consts = constants(coefs)
    coef = [table[j : j + 1, 0:1] for j in range(7)]
    mine = lax.axis_index("gy")
    side = 1 - mine
    adj[2:6] = adj4[...]
    for i in range(2):
        qe[i, 1:5] = q[i + 1, 1:5]
    phi[2:6] = phi_own[...]
    for n in range(2):
        for i in range(3):
            pr[i, 2 + n] = shared[i, n]
        pa[2 + n] = shared[3, n]

    def write(n, k, value):
        if k == 0:
            phase_back[2 * side + n] = value
        else:
            velocity_back[k - 1, 2 * side + n] = value

    new = [4 * side + n for n in range(2)]
    half_step(
        side, lambda n: other_first(si[THIRD_AT[n] : THIRD_AT[n] + THIRD[n]]), coef, consts, (uu, f, af, a2f, bb, ab, au),
        (e, q, adj4, pot, g, gv, base), (phi, pr, pa, adj, qe, new), write,
    )
    for n in range(2):
        phase_back[2 * mine + n] = result[0, n]
        for k in range(3):
            velocity_back[k, 2 * mine + n] = result[1 + k, n]


def f32(*shape):
    return jax.ShapeDtypeStruct(shape, jnp.float32)


def layers(*lead):
    return f32(*lead, ROWS, LANES)


def scratch(*lead):
    return pltpu.VMEM((*lead, ROWS, LANES), jnp.float32)


VM = pl.BlockSpec(memory_space=pltpu.VMEM)
SM = pl.BlockSpec(memory_space=pltpu.SMEM)
PARAMS = pltpu.CompilerParams(vmem_limit_bytes=12 * 1024 * 1024)
SWAP = [(0, 1), (1, 0)]


def role_shift(value, cross):
    gx, gy, gz = (lax.axis_size(a) for a in ("gx", "gy", "gz"))
    pairs = []
    for x in range(gx):
        for y in range(gy):
            for i in range(gz):
                target = (1 - x if cross else x, y, (i + 1 - 2 * y) % gz)
                pairs.append(((x * gy + y) * gz + i, (target[0] * gy + y) * gz + target[2]))
    return lax.ppermute(value, ("gx", "gy", "gz"), pairs)


def second_down(value):
    gx, gz = lax.axis_size("gx"), lax.axis_size("gz")
    pairs = [((2 * x + y) * gz + i, (2 * x + y) * gz + (i - 2 * y) % gz) for x in range(gx) for y in range(2) for i in range(gz)]
    return lax.ppermute(value, ("gx", "gy", "gz"), pairs)


def swap(value):
    return lax.ppermute(value, "gy", SWAP)


def call(kernel, outs, ins, scratches, name, smem, aliases={}):
    return pl.pallas_call(
        kernel,
        out_shape=outs,
        in_specs=[SM] * smem + [VM] * (len(ins) - smem),
        out_specs=jax.tree.map(lambda _: VM, outs),
        scratch_shapes=scratches,
        input_output_aliases=aliases,
        compiler_params=PARAMS,
        name=name,
    )(*ins)


def local(phase, velocity, phase_obs, velocity_obs, coefs):
    mine = (velocity, phase, phase_obs, velocity_obs)
    stack, edges, coefs, give = pl.pallas_call(
        load_kernel,
        out_shape=(f32(8 * CZ, CX, CY), f32(EDGE_ROWS, CY), f32(4), f32(len(SENT), CX, CY)),
        in_specs=[pl.BlockSpec(memory_space=pltpu.HBM)] * 5,
        out_specs=(VM,) * 4,
        scratch_shapes=[pltpu.SemaphoreType.DMA((9,))],
        compiler_params=PARAMS,
        name="load",
    )(*(pltpu.with_memory_space_constraint(a, pltpu.HBM) for a in (*mine, coefs)))
    peer = swap(stack)
    gxr = lax.ppermute(edges, "gx", SWAP)
    main, diag = call(
        pack_kernel,
        (f32(len(SENT), CX, LANES), f32(CORNER_ROWS, LANES)),
        (stack, swap(give)),
        [],
        "pack",
        0,
    )
    mr = role_shift(main, False)
    dr = role_shift(diag, True)
    gxr, mr, dr = lax.optimization_barrier((gxr, mr, dr))
    gxs = swap(gxr)
    inner = call(inner_kernel, layers(TOTAL), (stack, peer, gxr, gxs), [], "inner", 0)
    ms = swap(mr)
    ds = swap(dr)
    e, b, u, send, corner, rim, far = call(
        first_kernel,
        (layers(TOTAL), f32(CZ, CX, LANES), f32(CZ, CX, LANES), f32(CX * len(AGAIN), LANES),
         f32(AGAIN_ROWS, LANES), f32(RIM_ROWS, CY), f32(CX, LANES)),
        (coefs, inner, mr, ms, dr, ds),
        [scratch(6), pltpu.VMEM((6, CX, LANES), jnp.float32)],
        "first",
        1,
        {1: 0},
    )
    r2 = role_shift(send, False)
    d2 = role_shift(corner, True)
    x2 = lax.ppermute(rim, "gx", SWAP)
    far = second_down(far)
    adj, w, part, edge, gv, base, pot, g, q = call(
        weight_kernel,
        (layers(4), f32(3, CZ, CX, LANES), f32(5, 8, CY), f32(THIRD_AT[4], LANES), f32(3, 3, CZ, CX, CY),
         f32(CZ, CX, CY), layers(6), layers(3, 6), layers(3, 6)),
        (coefs, e),
        [scratch(6), scratch(3, 6), scratch(6)],
        "weights",
        1,
    )
    r2, d2, x2, far, w, part, edge = lax.optimization_barrier((r2, d2, x2, far, w, part, edge))
    s2, ds2, xs2 = swap(r2), swap(d2), swap(x2)
    fars = swap(far)
    sums, bb, uu, f, af, a2f, ab, au, send = call(
        moment_kernel,
        (f32(PARTNERS, SLOTS), layers(13), layers(8), layers(9), layers(7), layers(5), layers(8), layers(6),
         f32(THIRD_ROWS, LANES)),
        (b, u, r2, s2, d2, ds2, x2, xs2, far, fars, w, part, edge),
        [scratch(4), scratch(4)],
        "moments",
        0,
    )
    ri = role_shift(send, False)
    gathered = lax.all_to_all(sums.reshape(PARTNERS, 1, SLOTS), ("gx", "gz"), 0, 0).reshape(PARTNERS, SLOTS)
    ri, gathered = lax.optimization_barrier((ri, gathered))
    si = swap(ri)
    basis = (uu, f, af, a2f, bb, ab, au)
    state = (e, q, adj, pot, g, gv, base)
    room = [scratch(8), scratch(3, 6), scratch(6), scratch(8), scratch(2, 6)]
    params, table, phi, shared, result = call(
        near_kernel,
        (f32(4), f32(8, CY), layers(4), layers(4, 2), f32(4, 2, CX, CY)),
        (coefs, gathered, *basis, ri, *state),
        room,
        "near",
        1,
    )
    phase_back, velocity_back = call(
        far_kernel,
        (f32(CZ, CX, CY), f32(3, CZ, CX, CY)),
        (coefs, table, *basis, si, *state, phi, shared, result),
        room,
        "far",
        1,
    )
    return phase_back, velocity_back, params


def solution(mesh):
    return jax.shard_map(
        local,
        mesh=mesh,
        in_specs=(
            P("gz", "gx", "gy"),
            P(None, "gz", "gx", "gy"),
            P("gz", "gx", "gy"),
            P(None, "gz", "gx", "gy"),
            P(),
        ),
        out_specs=(P("gz", "gx", "gy"), P(None, "gz", "gx", "gy"), P()),
        check_vma=False,
    )
```

```python
import jax
import jax.numpy as jnp
from jax import lax
from jax.experimental import pallas as pl
from jax.experimental.pallas import tpu as pltpu
from jax.sharding import PartitionSpec as P

DT = 0.1
SHIFT = 0.01
CZ, CX, CY = 4, 32, 128
HX = 8
NEAR = 4
NARROW = (CX + 2 * HX) - 2 * NEAR
ROWS = CX + 2 * HX
LANES = 2 * CY
PARTNERS = 128

V0, V1, V2, PH, PO, O0, O1, O2 = range(8)
HALO = (2, 1, 1, 2, 0, 1, 0, 0)
BASE = []
_at = 0
for _h in HALO:
    BASE.append(_at)
    _at += CZ + 2 * _h
TOTAL = _at
SENT = [(f, k) for f, h in enumerate(HALO) for k in range(1, h + 1)]
CORNER = [{(V0, 1): 1, (V1, 1): 1, (V2, 1): 1, (PH, 1): 3, (PH, 2): 2}.get(entry, 0) for entry in SENT]
CORNER_ROWS = 2 * sum(CORNER)
EDGE = (2, 2, 2, 4, 2, 1, 1, 1)
EDGE_ROWS = 2 * CZ * sum(EDGE)
AGAIN = [("b", k, 6 - k) for k in (1, 2, 3, 4)] + [("u", k, 3 - k) for k in (1, 2)]
AGAIN_ROWS = 2 * sum(w for _, _, w in AGAIN)
RIM = [("b", z, 6) for z in range(CZ)] + [("u", z, 3) for z in range(CZ)]
RIM_ROWS = 2 * sum(w for _, _, w in RIM)
THIRD = (CX, CX, CX + 2, CX, CX + 2, CX, CX, CX)
THIRD_AT = [sum(THIRD[:n]) for n in range(8)]
THIRD_ROWS = -(-sum(THIRD) // 8) * 8
NUM_SUMS = 45
SLOTS = 64


def x_up(a):
    return pltpu.roll(a, a.shape[0] - 1, 0)


def x_dn(a):
    return pltpu.roll(a, 1, 0)


def y_up(a):
    return pltpu.roll(a, a.shape[1] - 1, 1)


def y_dn(a):
    return pltpu.roll(a, 1, 1)


def dx(a):
    return 0.5 * (x_up(a) - x_dn(a))


def dy(a):
    return 0.5 * (y_up(a) - y_dn(a))


def own(a):
    return a[HX : HX + CX, :CY]


def lap_of(c, zu, zd):
    return (zu + zd) + (x_up(c) + x_dn(c)) + (y_up(c) + y_dn(c)) - 6.0 * c


def other_first(a):
    return jnp.concatenate([a[:, CY:], a[:, :CY]], 1)


def outgoing(core, k):
    return (CZ - k) * (1 - core) + (k - 1) * core


def loop(count, body):
    def step(t, carry):
        body(t)
        return carry

    lax.fori_loop(0, count, step, 0, unroll=count)


def low_high(core, mine, theirs):
    theirs = other_first(theirs)
    return jnp.where(core == 0, mine, theirs), jnp.where(core == 0, theirs, mine)


def load_kernel(vel, ph, po, vo, coefs, stack, out, coefs_out, give, sems):
    copies = [
        pltpu.make_async_copy(ph, stack.at[pl.ds(CZ * PH, CZ)], sems.at[6]),
        pltpu.make_async_copy(po, stack.at[pl.ds(CZ * PO, CZ)], sems.at[7]),
        pltpu.make_async_copy(coefs, coefs_out, sems.at[8]),
    ]
    for i in range(3):
        copies.append(pltpu.make_async_copy(vel.at[i], stack.at[pl.ds(CZ * (V0 + i), CZ)], sems.at[i]))
        copies.append(pltpu.make_async_copy(vo.at[i], stack.at[pl.ds(CZ * (O0 + i), CZ)], sems.at[3 + i]))
    for copy in copies:
        copy.start()
    for copy in copies:
        copy.wait()
    other = 1 - lax.axis_index("gy")
    for n, (f, k) in enumerate(SENT):
        give[n] = stack[CZ * f + outgoing(other, k)]
    row = 0
    for f, w in enumerate(EDGE):
        for z in range(CZ):
            out[row : row + w] = stack[CZ * f + z, CX - w :]
            out[row + w : row + 2 * w] = stack[CZ * f + z, :w]
            row += 2 * w


def pack_kernel(stack, got, main, diag):
    c = lax.axis_index("gy")
    row = 0
    for n, (f, k) in enumerate(SENT):
        src = jnp.concatenate([stack[CZ * f + outgoing(c, k)], got[n]], 1)
        main[n] = src
        w = CORNER[n]
        if w:
            diag[row : row + w] = src[CX - w :]
            diag[row + w : row + 2 * w] = src[:w]
        row += 2 * w


def inner_kernel(stack, peer, gxr, gxs, e):
    row = 0
    for f, w in enumerate(EDGE):
        mid = BASE[f] + HALO[f]
        for z in range(CZ):
            for half, x in enumerate((gxr, gxs)):
                lanes = pl.ds(CY * half, CY)
                e[mid + z, HX : HX + CX, lanes] = (stack, peer)[half][CZ * f + z]
                e[mid + z, HX - w : HX, lanes] = x[row : row + w]
                e[mid + z, HX + CX : HX + CX + w, lanes] = x[row + w : row + 2 * w]
            row += 2 * w


def at(e, field, z):
    return e[BASE[field] + HALO[field] + z]


def middle(a):
    return a[HX : HX + CX]


def provisional(e, field, z, grad, here, tension, viscosity):
    a = at(e, field, z)
    zu, zd = at(e, field, z + 1), at(e, field, z - 1)
    xu, xd, yu, yd = x_up(a), x_dn(a), y_up(a), y_dn(a)
    lap = (zu + zd) + (xu + xd) + (yu + yd) - 6.0 * a
    advect = at(e, V0, z) * (zu - zd) + at(e, V1, z) * (xu - xd) + at(e, V2, z) * (yu - yd)
    value = a - (0.5 * DT) * advect + (DT * viscosity) * lap + (DT * tension) * (here * grad)
    return value, lap


def first_kernel(coefs, inner, mr, ms, dr, ds, e, b, u, send, corner, rim, far, pot, p0):
    tension = 0.5 * coefs[1]
    viscosity = 0.1 * coefs[2]
    interface = 0.5 * coefs[3]
    c = lax.axis_index("gy")

    row = 0
    for n, (f, k) in enumerate(SENT):
        below, above = BASE[f] + HALO[f] - k, BASE[f] + HALO[f] + CZ + k - 1
        lo, hi = low_high(c, mr[n], ms[n])
        e[below, HX : HX + CX] = lo
        e[above, HX : HX + CX] = hi
        w = CORNER[n]
        if w == 0:
            continue
        lo, hi = low_high(c, dr[row : row + 2 * w], ds[row : row + 2 * w])
        for layer, part in ((below, lo), (above, hi)):
            e[layer, HX - w : HX] = part[:w]
            e[layer, HX + CX : HX + CX + w] = part[w:]
        row += 2 * w

    def potential(t):
        z = t - 1
        a = at(e, PH, z)
        pot[t] = a * a * a - a - interface * lap_of(a, at(e, PH, z + 1), at(e, PH, z - 1))

    loop(6, potential)

    def along(t):
        z = t - 1
        grad = 0.5 * (at(e, PH, z + 1) - at(e, PH, z - 1))
        value, _ = provisional(e, V0, z, grad, pot[t], tension, viscosity)
        p0[t] = middle(value)

    loop(6, along)

    def across(z):
        phase = at(e, PH, z)
        p1, _ = provisional(e, V1, z, dx(phase), pot[z + 1], tension, viscosity)
        p2, _ = provisional(e, V2, z, dy(phase), pot[z + 1], tension, viscosity)
        div = 0.5 * (p0[z + 2] - p0[z]) + middle(dx(p1) + dy(p2))
        b[z] = -div
        seen = 0.5 * middle(at(e, O0, z + 1) - at(e, O0, z - 1)) + middle(dx(at(e, O1, z)) + dy(at(e, O2, z)))
        u[z] = div - seen

    loop(4, across)

    row = 0
    for n, (name, k, w) in enumerate(AGAIN):
        src = (b if name == "b" else u)[outgoing(c, k)]
        send[CX * n : CX * (n + 1)] = src
        corner[row : row + w] = src[CX - w :]
        corner[row + w : row + 2 * w] = src[:w]
        row += 2 * w
    row = 0
    for name, z, w in RIM:
        field = b if name == "b" else u
        rim[row : row + w] = field[z, CX - w :, :CY]
        rim[row + w : row + 2 * w] = field[z, :w, :CY]
        row += 2 * w
    far[...] = b[0]


def folded(a):
    a = a[:, :CY] + a[:, CY:]
    return (a[0:8] + a[8:16]) + (a[16:24] + a[24:32])


def weight_kernel(coefs, e, adj, w, part, edge, gv, base, pot, g, q, lph, lv, p0):
    mobility, tension, viscosity, interface = constants(coefs)

    def forward(t):
        z = t - 1
        a = at(e, PH, z)
        lap = lap_of(a, at(e, PH, z + 1), at(e, PH, z - 1))
        lph[t] = lap
        here = a * a * a - a - interface * lap
        pot[t] = here
        g[0, t] = 0.5 * (at(e, PH, z + 1) - at(e, PH, z - 1))
        g[1, t] = dx(a)
        g[2, t] = dy(a)
        value, lv[0, t] = provisional(e, V0, z, g[0, t], here, tension, viscosity)
        q[0, t] = value - at(e, O0, z)

    loop(6, forward)

    def across(z):
        here = pot[z + 1]
        p1, lv[1, z] = provisional(e, V1, z, g[1, z + 1], here, tension, viscosity)
        p2, lv[2, z] = provisional(e, V2, z, g[2, z + 1], here, tension, viscosity)
        q[1, z + 1] = p1 - at(e, O1, z)
        q[2, z + 1] = p2 - at(e, O2, z)

    loop(4, across)
    sums = [jnp.zeros((8, CY), jnp.float32)] * 5
    for t in range(CZ):
        here = pot[t + 1]
        lap = lph[t + 1]
        gs = [g[i, t + 1] for i in range(3)]
        up, dn = pot[t + 2] * g[0, t + 2], pot[t] * g[0, t]
        w1 = 0.5 * (up - dn) + dx(here * gs[1]) + dy(here * gs[2])
        w2 = 0.5 * (lv[0, t + 2] - lv[0, t]) + dx(lv[1, t]) + dy(lv[2, t])
        up, dn = lph[t + 2] * g[0, t + 2], lph[t] * g[0, t]
        w3 = 0.5 * (up - dn) + dx(lap * gs[1]) + dy(lap * gs[2])
        w[0, t] = middle(w1)
        w[1, t] = middle(w2)
        w[2, t] = middle(w3)
        lap_pot = lap_of(here, pot[t + 2], pot[t])
        lap_lap = lap_of(lap, lph[t + 2], lph[t])
        flow = at(e, V0, t) * gs[0] + at(e, V1, t) * gs[1] + at(e, V2, t) * gs[2]
        c = at(e, PH, t) - DT * flow + (DT * mobility) * lap_pot - at(e, PO, t)
        adj[t] = c
        v1, v2 = at(e, V1, t), at(e, V2, t)
        base[t] = own(c + DT * (dx(v1 * c) + dy(v2 * c)))
        for i, field in enumerate((V0, V1, V2)):
            a = at(e, field, t)
            gv[0, i, t] = own(0.5 * (at(e, field, t + 1) - at(e, field, t - 1)))
            gv[1, i, t] = own(dx(a))
            gv[2, i, t] = own(dy(a))
        qs = [q[i, t + 1] for i in range(3)]
        qg = qs[0] * gs[0] + qs[1] * gs[1] + qs[2] * gs[2]
        ql = qs[0] * lv[0, t + 1] + qs[1] * lv[1, t] + qs[2] * lv[2, t]
        terms = (middle(c * lap_pot), middle(here * qg), middle(ql), middle(lap * qg), middle(c * lap_lap))
        sums = [s + folded(a) for s, a in zip(sums, terms)]
    for k in range(5):
        part[k] = sums[k]
    c = lax.axis_index("gy")
    pieces = (q[1, 1 + outgoing(c, 1)], q[2, 1 + outgoing(c, 1)], adj[outgoing(c, 1)], adj[outgoing(c, 2)])
    for n, src in enumerate(pieces):
        w = (THIRD[n] - CX) // 2
        edge[THIRD_AT[n] : THIRD_AT[n] + THIRD[n]] = src[HX - w : HX + CX + w]


def shifted(c, zu, zd):
    return (6.0 + SHIFT) * c - ((zu + zd) + (x_up(c) + x_dn(c)) + (y_up(c) + y_dn(c)))


def gather_kernel(d, x, far, out):
    out[0:CX] = far[...]
    half = RIM_ROWS // 2
    out[CX : CX + half, :CY] = x[:half]
    out[CX : CX + half, CY:] = x[half:]
    out[CX + half : CX + half + AGAIN_ROWS] = d[...]


def moment_kernel(b4, u4, r, s, d, x, far, swapped, w, part, edge, out, bb, uu, f, af, a2f, ab, au, send, a2b, a2u):
    corner = CX + RIM_ROWS // 2
    c = lax.axis_index("gy")
    near = pl.ds(NEAR, NARROW)
    bb[4:8, HX : HX + CX] = b4[...]
    uu[2:6, HX : HX + CX] = u4[...]
    row = 0
    for n, (name, k, width) in enumerate(AGAIN):
        dst, below = (bb, 4 - k) if name == "b" else (uu, 2 - k)
        above = 7 + k if name == "b" else 5 + k
        lo, hi = low_high(c, r[CX * n : CX * (n + 1)], s[CX * n : CX * (n + 1)])
        dst[below, HX : HX + CX] = lo
        dst[above, HX : HX + CX] = hi
        lo, hi = low_high(c, d[row : row + 2 * width], swapped[corner + row : corner + row + 2 * width])
        for layer, part_rows in ((below, lo), (above, hi)):
            dst[layer, HX - width : HX] = part_rows[:width]
            dst[layer, HX + CX : HX + CX + width] = part_rows[width:]
        row += 2 * width
    row = 0
    for name, z, width in RIM:
        dst, layer = (bb, 4 + z) if name == "b" else (uu, 2 + z)
        place, side = CX + row % (RIM_ROWS // 2), pl.ds(CY * (row // (RIM_ROWS // 2)), CY)
        dst[layer, HX - width : HX, :CY] = x[row : row + width]
        dst[layer, HX + CX : HX + CX + width, :CY] = x[row + width : row + 2 * width]
        dst[layer, HX - width : HX, CY:] = swapped[place : place + width, side]
        dst[layer, HX + CX : HX + CX + width, CY:] = swapped[place + width : place + 2 * width, side]
        row += 2 * width
    bb[12, HX : HX + CX] = jnp.where(c == 1, far[...], other_first(swapped[0:CX]))

    def wide(t):
        a = bb[t + 2]
        across = (pltpu.roll(a, ROWS - 2, 0) + pltpu.roll(a, 2, 0)) + (
            pltpu.roll(a, LANES - 2, 1) + pltpu.roll(a, 2, 1)
        )
        f[t] = 0.25 * ((bb[t + 4] + bb[t]) + across) - 1.5 * a

    loop(9, wide)

    def apply(src, dst, count):
        def body(t):
            dst[t] = shifted(src[t + 1], src[t + 2], src[t])

        loop(count, body)

    apply(f, af, 7)
    apply(af, a2f, 5)
    apply(bb.at[pl.ds(1, 10)], ab, 8)
    apply(ab.at[pl.ds(1, 6)], a2b, 4)
    apply(uu, au, 6)
    apply(au, a2u, 4)

    rows = pl.ds(HX, CX)
    acc = [jnp.zeros((8, CY), jnp.float32)] * 40
    for t in range(CZ):
        vb, vab, va2b = bb[t + 4, rows], ab[t + 2, rows], a2b[t, rows]
        vu, vau, va2u = uu[t + 2, rows], au[t + 1, rows], a2u[t, rows]
        vf, vaf, va2f = f[t + 2, rows], af[t + 1, rows], a2f[t, rows]
        a = a2f[t]
        across = (x_up(a) + x_dn(a)) + (y_up(a) + y_dn(a))
        va3f = (6.0 + SHIFT) * va2f - (2.0 * a2f[t + 1, rows] + middle(across))
        terms = [
            vb * vb, vb * vab, vab * vab, vab * va2b,
            vu * vu, vu * vau, vau * vau, vau * va2u,
            vu * vf, vu * vaf, vu * va2f, vau * va2f, va2u * va2f,
            vf * vf, vf * vaf, vaf * vaf, vaf * va2f, va2f * va2f, va2f * va3f,
        ]
        for k in range(3):
            wk = w[k, t]
            terms += [a * wk for a in (vu, vau, vf, vaf, va2f, vb, vab)]
        acc = [x + folded(a) for x, a in zip(acc, terms)]
    rows_list = [jnp.sum(a, axis=0, keepdims=True) for a in acc]
    rows_list += [jnp.sum(part[k], axis=0, keepdims=True) for k in range(5)]
    rows_list += [jnp.zeros((1, CY), jnp.float32)] * (48 - NUM_SUMS)
    table = jnp.concatenate(rows_list, axis=0)
    totals = jnp.sum(table, axis=1, keepdims=True)
    line = lax.broadcasted_iota(jnp.int32, (48, SLOTS), 1)
    which = lax.broadcasted_iota(jnp.int32, (48, SLOTS), 0)
    row = jnp.sum(jnp.where(line == which, totals, 0.0), axis=0, keepdims=True)
    out[...] = jnp.broadcast_to(row, (PARTNERS, SLOTS))
    send[0 : THIRD_AT[4]] = edge[...]
    pieces = (a2f[outgoing(c, 1)], a2f[outgoing(c, 2)], af[1 + outgoing(c, 2)], au[1 + outgoing(c, 2)])
    for n, src in enumerate(pieces, 4):
        w = (THIRD[n] - CX) // 2
        send[THIRD_AT[n] : THIRD_AT[n] + THIRD[n]] = src[HX - w : HX + CX + w]


def steps(m0, m1, m2, m3):
    alpha = m0 / m1
    second = (m1 / m0) * ((m0 * m2 - m1 * m1) / (m1 * m3 - m2 * m2))
    second = jnp.clip(second, 1.0 / (12.0 + SHIFT), 1.0 / SHIFT)
    return alpha + second * ((m0 * m2) / (m1 * m1)), -second * alpha


def solve_kernel(gathered, mobility, tension, coef_out, params):
    total = jnp.sum(gathered[...], axis=0, keepdims=True)
    line = lax.broadcasted_iota(jnp.int32, (1, SLOTS), 1)

    def s(k):
        return jnp.sum(jnp.where(line == k, total, 0.0), axis=1, keepdims=True)

    c0, c1 = steps(s(0), s(1), s(2), s(3))
    uu = [s(4 + k) for k in range(4)]
    uf = [s(8 + k) for k in range(5)]
    ff = [s(13 + k) for k in range(6)]
    moments = [
        uu[k] - 2.0 * (c0 * uf[k] + c1 * uf[k + 1])
        + (c0 * c0) * ff[k] + (2.0 * c0 * c1) * ff[k + 1] + (c1 * c1) * ff[k + 2]
        for k in range(4)
    ]
    e0, e1 = steps(*moments)
    coef = (e0, e1, -e0 * c0, -(e0 * c1 + e1 * c0), -e1 * c1, -c0, -c1)
    for j in range(7):
        coef_out[j : j + 1] = jnp.broadcast_to(coef[j], (1, CY))

    def meet(k):
        value = coef[0] * s(19 + 7 * k)
        for j in range(1, 7):
            value = value + coef[j] * s(19 + 7 * k + j)
        return value

    scale = 1.0 / (256 * 64 * 256)
    g0 = DT * s(40)
    g1 = DT * (s(41) - meet(0))
    g2 = DT * (s(42) - meet(1))
    g3 = -((DT * mobility) * s(44) + (DT * tension) * (s(43) - meet(2)))
    place = lax.broadcasted_iota(jnp.int32, (1, CY), 1)
    packed = jnp.where(place == 0, g0, jnp.where(place == 1, g1, jnp.where(place == 2, g2, g3)))
    params[...] = (packed * scale)[0, 0:4]
    return coef


def half_step(side, halo, coef, consts, basis, state, work, write):
    mobility, tension, viscosity, interface = consts
    uu, f, af, a2f, bb, ab, au = basis
    e, q, adj4, pot, g, gv, base = state
    phi, pr, pa, adj, qe, new = work
    inside, wider = pl.ds(HX, CX), pl.ds(HX - 1, CX + 2)
    for i in range(2):
        qe[i, 5 * side, inside] = halo(i)
    adj[1 + 5 * side, wider] = halo(2)
    adj[7 * side, inside] = halo(3)

    def mixed(terms):
        value = coef[0] * terms[0]
        for a, t in zip(coef[1:], terms[1:]):
            value = value + a * t
        return value

    i = 1 + 5 * side
    phi[i, wider] = mixed([
        uu[i, wider], au[i - 1, wider], f[i, wider], af[i - 1, wider], halo(4), bb[i + 2, wider], ab[i, wider],
    ])
    i = 7 * side
    phi[i, inside] = mixed([
        uu[i, inside], halo(7), f[i, inside], halo(6), halo(5), bb[i + 2, inside], ab[i, inside],
    ])

    def project(t):
        c = phi[t + 1]
        r0 = q[0, t] + 0.5 * (phi[t + 2] - phi[t])
        r1 = qe[0, t] + dx(c)
        r2 = qe[1, t] + dy(c)
        pr[0, t] = r0
        pr[1, t] = r1
        pr[2, t] = r2
        lap = lap_of(adj[t + 1], adj[t + 2], adj[t])
        pa[t] = (DT * mobility) * lap + (DT * tension) * (r0 * g[0, t] + r1 * g[1, t] + r2 * g[2, t])

    for t in new:
        project(t)

    for n in range(2):
        t = 2 * side + n
        v1, v2 = at(e, V1, t), at(e, V2, t)
        v0u, v0d = at(e, V0, t + 1), at(e, V0, t - 1)
        here = pot[t + 1]
        ph = own(at(e, PH, t))
        lam = pa[t + 1]
        up = v0u * adj[t + 3] - tension * (pot[t + 2] * pr[0, t + 2])
        dn = v0d * adj[t + 1] - tension * (pot[t] * pr[0, t])
        div = 0.5 * (up - dn) - tension * (dx(here * pr[1, t + 1]) + dy(here * pr[2, t + 1]))
        value = base[t] + DT * own(div) + (3.0 * ph * ph - 1.0) * own(lam)
        write(n, 0, value - interface * own(lap_of(lam, pa[t + 2], pa[t])))
        r = [pr[i, t + 1] for i in range(3)]
        mine = [own(a) for a in r]
        c = own(adj[t + 2])
        for k in range(3):
            mix = mine[0] * gv[k, 0, t] + mine[1] * gv[k, 1, t] + mine[2] * gv[k, 2, t]
            moved = (viscosity + 0.5 * v0u) * pr[k, t + 2] + (viscosity - 0.5 * v0d) * pr[k, t]
            moved = moved + x_up((viscosity + 0.5 * v1) * r[k]) + x_dn((viscosity - 0.5 * v1) * r[k])
            moved = moved + y_up((viscosity + 0.5 * v2) * r[k]) + y_dn((viscosity - 0.5 * v2) * r[k])
            moved = own(moved) - (6.0 * viscosity) * mine[k]
            write(n, 1 + k, mine[k] + DT * (moved - mix - c * own(g[k, t + 1])))


def constants(coefs):
    return 0.1 * coefs[0], 0.5 * coefs[1], 0.1 * coefs[2], 0.5 * coefs[3]


def near_kernel(
    coefs, gathered, uu, f, af, a2f, bb, ab, au, ri, e, q, adj4, pot, g, gv, base,
    params, table, phi_own, shared, result, phi, pr, pa, adj, qe,
):
    consts = constants(coefs)
    coef = solve_kernel(gathered, consts[0], consts[1], table, params)
    side = lax.axis_index("gy")
    adj[2:6] = adj4[...]
    for i in range(2):
        qe[i, 1:5] = q[i + 1, 1:5]
    for z in range(CZ):
        value = coef[0] * uu[z + 2] + coef[1] * au[z + 1] + coef[2] * f[z + 2] + coef[3] * af[z + 1]
        value = value + coef[4] * a2f[z] + coef[5] * bb[z + 4] + coef[6] * ab[z + 2]
        phi[z + 2] = value
        phi_own[z] = value

    def write(n, k, value):
        result[k, n] = value

    new = [2 * side + n for n in range(4)]
    half_step(
        side, lambda n: ri[THIRD_AT[n] : THIRD_AT[n] + THIRD[n]], coef, consts, (uu, f, af, a2f, bb, ab, au), (e, q, adj4, pot, g, gv, base),
        (phi, pr, pa, adj, qe, new), write,
    )
    for n in range(2):
        for i in range(3):
            shared[i, n] = pr[i, 2 + n]
        shared[3, n] = pa[2 + n]


def far_kernel(
    coefs, table, uu, f, af, a2f, bb, ab, au, si, e, q, adj4, pot, g, gv, base, phi_own, shared, result,
    phase_back, velocity_back, phi, pr, pa, adj, qe,
):
    consts = constants(coefs)
    coef = [table[j : j + 1, 0:1] for j in range(7)]
    mine = lax.axis_index("gy")
    side = 1 - mine
    adj[2:6] = adj4[...]
    for i in range(2):
        qe[i, 1:5] = q[i + 1, 1:5]
    phi[2:6] = phi_own[...]
    for n in range(2):
        for i in range(3):
            pr[i, 2 + n] = shared[i, n]
        pa[2 + n] = shared[3, n]

    def write(n, k, value):
        if k == 0:
            phase_back[2 * side + n] = value
        else:
            velocity_back[k - 1, 2 * side + n] = value

    new = [4 * side + n for n in range(2)]
    half_step(
        side, lambda n: other_first(si[THIRD_AT[n] : THIRD_AT[n] + THIRD[n]]), coef, consts, (uu, f, af, a2f, bb, ab, au),
        (e, q, adj4, pot, g, gv, base), (phi, pr, pa, adj, qe, new), write,
    )
    for n in range(2):
        phase_back[2 * mine + n] = result[0, n]
        for k in range(3):
            velocity_back[k, 2 * mine + n] = result[1 + k, n]


def f32(*shape):
    return jax.ShapeDtypeStruct(shape, jnp.float32)


def layers(*lead):
    return f32(*lead, ROWS, LANES)


def scratch(*lead):
    return pltpu.VMEM((*lead, ROWS, LANES), jnp.float32)


VM = pl.BlockSpec(memory_space=pltpu.VMEM)
SM = pl.BlockSpec(memory_space=pltpu.SMEM)
PARAMS = pltpu.CompilerParams(vmem_limit_bytes=12 * 1024 * 1024)
SWAP = [(0, 1), (1, 0)]


def role_shift(value, cross):
    gx, gy, gz = (lax.axis_size(a) for a in ("gx", "gy", "gz"))
    pairs = []
    for x in range(gx):
        for y in range(gy):
            for i in range(gz):
                target = (1 - x if cross else x, y, (i + 1 - 2 * y) % gz)
                pairs.append(((x * gy + y) * gz + i, (target[0] * gy + y) * gz + target[2]))
    return lax.ppermute(value, ("gx", "gy", "gz"), pairs)


def second_down(value):
    gx, gz = lax.axis_size("gx"), lax.axis_size("gz")
    pairs = [((2 * x + y) * gz + i, (2 * x + y) * gz + (i - 2 * y) % gz) for x in range(gx) for y in range(2) for i in range(gz)]
    return lax.ppermute(value, ("gx", "gy", "gz"), pairs)


def swap(value):
    return lax.ppermute(value, "gy", SWAP)


def call(kernel, outs, ins, scratches, name, smem, aliases={}):
    return pl.pallas_call(
        kernel,
        out_shape=outs,
        in_specs=[SM] * smem + [VM] * (len(ins) - smem),
        out_specs=jax.tree.map(lambda _: VM, outs),
        scratch_shapes=scratches,
        input_output_aliases=aliases,
        compiler_params=PARAMS,
        name=name,
    )(*ins)


def local(phase, velocity, phase_obs, velocity_obs, coefs):
    mine = (velocity, phase, phase_obs, velocity_obs)
    stack, edges, coefs, give = pl.pallas_call(
        load_kernel,
        out_shape=(f32(8 * CZ, CX, CY), f32(EDGE_ROWS, CY), f32(4), f32(len(SENT), CX, CY)),
        in_specs=[pl.BlockSpec(memory_space=pltpu.HBM)] * 5,
        out_specs=(VM,) * 4,
        scratch_shapes=[pltpu.SemaphoreType.DMA((9,))],
        compiler_params=PARAMS,
        name="load",
    )(*(pltpu.with_memory_space_constraint(a, pltpu.HBM) for a in (*mine, coefs)))
    peer = swap(stack)
    gxr = lax.ppermute(edges, "gx", SWAP)
    main, diag = call(
        pack_kernel,
        (f32(len(SENT), CX, LANES), f32(CORNER_ROWS, LANES)),
        (stack, swap(give)),
        [],
        "pack",
        0,
    )
    mr = role_shift(main, False)
    dr = role_shift(diag, True)
    gxr, mr, dr = lax.optimization_barrier((gxr, mr, dr))
    gxs = swap(gxr)
    inner = call(inner_kernel, layers(TOTAL), (stack, peer, gxr, gxs), [], "inner", 0)
    ms = swap(mr)
    ds = swap(dr)
    e, b, u, send, corner, rim, far = call(
        first_kernel,
        (layers(TOTAL), f32(CZ, CX, LANES), f32(CZ, CX, LANES), f32(CX * len(AGAIN), LANES),
         f32(AGAIN_ROWS, LANES), f32(RIM_ROWS, CY), f32(CX, LANES)),
        (coefs, inner, mr, ms, dr, ds),
        [scratch(6), pltpu.VMEM((6, CX, LANES), jnp.float32)],
        "first",
        1,
        {1: 0},
    )
    r2 = role_shift(send, False)
    d2 = role_shift(corner, True)
    x2 = lax.ppermute(rim, "gx", SWAP)
    far = second_down(far)
    adj, w, part, edge, gv, base, pot, g, q = call(
        weight_kernel,
        (layers(4), f32(3, CZ, CX, LANES), f32(5, 8, CY), f32(THIRD_AT[4], LANES), f32(3, 3, CZ, CX, CY),
         f32(CZ, CX, CY), layers(6), layers(3, 6), layers(3, 6)),
        (coefs, e),
        [scratch(6), scratch(3, 6), scratch(6)],
        "weights",
        1,
    )
    r2, d2, x2, far, w, part, edge = lax.optimization_barrier((r2, d2, x2, far, w, part, edge))
    small = call(gather_kernel, f32(CX + RIM_ROWS // 2 + AGAIN_ROWS, LANES), (d2, x2, far), [], "gather", 0)
    s2, swapped = swap(r2), swap(small)
    sums, bb, uu, f, af, a2f, ab, au, send = call(
        moment_kernel,
        (f32(PARTNERS, SLOTS), layers(13), layers(8), layers(9), layers(7), layers(5), layers(8), layers(6),
         f32(THIRD_ROWS, LANES)),
        (b, u, r2, s2, d2, x2, far, swapped, w, part, edge),
        [scratch(4), scratch(4)],
        "moments",
        0,
    )
    ri = role_shift(send, False)
    gathered = lax.all_to_all(sums.reshape(PARTNERS, 1, SLOTS), ("gx", "gz"), 0, 0).reshape(PARTNERS, SLOTS)
    ri, gathered = lax.optimization_barrier((ri, gathered))
    si = swap(ri)
    basis = (uu, f, af, a2f, bb, ab, au)
    state = (e, q, adj, pot, g, gv, base)
    room = [scratch(8), scratch(3, 6), scratch(6), scratch(8), scratch(2, 6)]
    params, table, phi, shared, result = call(
        near_kernel,
        (f32(4), f32(8, CY), layers(4), layers(4, 2), f32(4, 2, CX, CY)),
        (coefs, gathered, *basis, ri, *state),
        room,
        "near",
        1,
    )
    phase_back, velocity_back = call(
        far_kernel,
        (f32(CZ, CX, CY), f32(3, CZ, CX, CY)),
        (coefs, table, *basis, si, *state, phi, shared, result),
        room,
        "far",
        1,
    )
    return phase_back, velocity_back, params


def solution(mesh):
    return jax.shard_map(
        local,
        mesh=mesh,
        in_specs=(
            P("gz", "gx", "gy"),
            P(None, "gz", "gx", "gy"),
            P("gz", "gx", "gy"),
            P(None, "gz", "gx", "gy"),
            P(),
        ),
        out_specs=(P("gz", "gx", "gy"), P(None, "gz", "gx", "gy"), P()),
        check_vma=False,
    )
```

```python
import jax
import jax.numpy as jnp
from jax import lax
from jax.experimental import pallas as pl
from jax.experimental.pallas import tpu as pltpu
from jax.sharding import PartitionSpec as P

DT = 0.1
SHIFT = 0.01
CZ, CX, CY = 4, 32, 128
HX = 8
NEAR = 4
NARROW = (CX + 2 * HX) - 2 * NEAR
ROWS = CX + 2 * HX
LANES = 2 * CY
PARTNERS = 128

V0, V1, V2, PH, PO, O0, O1, O2 = range(8)
HALO = (2, 1, 1, 2, 0, 1, 0, 0)
BASE = []
_at = 0
for _h in HALO:
    BASE.append(_at)
    _at += CZ + 2 * _h
TOTAL = _at
SENT = [(f, k) for f, h in enumerate(HALO) for k in range(1, h + 1)]
CORNER = [{(V0, 1): 1, (V1, 1): 1, (V2, 1): 1, (PH, 1): 3, (PH, 2): 2}.get(entry, 0) for entry in SENT]
CORNER_ROWS = 2 * sum(CORNER)
EDGE = (2, 2, 2, 4, 2, 1, 1, 1)
EDGE_ROWS = 2 * CZ * sum(EDGE)
AGAIN = [("b", k, 6 - k) for k in (1, 2, 3, 4)] + [("u", k, 3 - k) for k in (1, 2)]
AGAIN_ROWS = 2 * sum(w for _, _, w in AGAIN)
RIM = [("b", z, 6) for z in range(CZ)] + [("u", z, 3) for z in range(CZ)]
RIM_ROWS = 2 * sum(w for _, _, w in RIM)
THIRD = (CX, CX, CX + 2, CX, CX + 2, CX, CX, CX)
THIRD_AT = [sum(THIRD[:n]) for n in range(8)]
THIRD_ROWS = -(-sum(THIRD) // 8) * 8
NUM_SUMS = 45
SLOTS = 64


def x_up(a):
    return pltpu.roll(a, a.shape[0] - 1, 0)


def x_dn(a):
    return pltpu.roll(a, 1, 0)


def y_up(a):
    return pltpu.roll(a, a.shape[1] - 1, 1)


def y_dn(a):
    return pltpu.roll(a, 1, 1)


def dx(a):
    return 0.5 * (x_up(a) - x_dn(a))


def dy(a):
    return 0.5 * (y_up(a) - y_dn(a))


def own(a):
    return a[HX : HX + CX, :CY]


def lap_of(c, zu, zd):
    return (zu + zd) + (x_up(c) + x_dn(c)) + (y_up(c) + y_dn(c)) - 6.0 * c


def other_first(a):
    return jnp.concatenate([a[:, CY:], a[:, :CY]], 1)


def outgoing(core, k):
    return (CZ - k) * (1 - core) + (k - 1) * core


def loop(count, body):
    def step(t, carry):
        body(t)
        return carry

    lax.fori_loop(0, count, step, 0, unroll=count)


def low_high(core, mine, theirs):
    theirs = other_first(theirs)
    return jnp.where(core == 0, mine, theirs), jnp.where(core == 0, theirs, mine)


def load_kernel(vel, ph, po, vo, coefs, stack, out, coefs_out, give, sems):
    copies = [
        pltpu.make_async_copy(vel, stack.at[pl.ds(V0, 3)], sems.at[0]),
        pltpu.make_async_copy(ph, stack.at[PH], sems.at[1]),
        pltpu.make_async_copy(vo, stack.at[pl.ds(O0, 3)], sems.at[2]),
        pltpu.make_async_copy(po, stack.at[PO], sems.at[3]),
        pltpu.make_async_copy(coefs, coefs_out, sems.at[4]),
    ]
    for copy in copies:
        copy.start()
    for copy in copies:
        copy.wait()
    other = 1 - lax.axis_index("gy")
    for n, (f, k) in enumerate(SENT):
        give[n] = stack[f, outgoing(other, k)]
    row = 0
    for f, w in enumerate(EDGE):
        for z in range(CZ):
            out[row : row + w] = stack[f, z, CX - w :]
            out[row + w : row + 2 * w] = stack[f, z, :w]
            row += 2 * w


def pack_kernel(stack, got, main, diag):
    c = lax.axis_index("gy")
    row = 0
    for n, (f, k) in enumerate(SENT):
        src = jnp.concatenate([stack[f, outgoing(c, k)], got[n]], 1)
        main[n] = src
        w = CORNER[n]
        if w:
            diag[row : row + w] = src[CX - w :]
            diag[row + w : row + 2 * w] = src[:w]
        row += 2 * w


def inner_kernel(stack, peer, gxr, gxs, e):
    row = 0
    for f, w in enumerate(EDGE):
        mid = BASE[f] + HALO[f]
        for z in range(CZ):
            for half, x in enumerate((gxr, gxs)):
                lanes = pl.ds(CY * half, CY)
                e[mid + z, HX : HX + CX, lanes] = (stack, peer)[half][f, z]
                e[mid + z, HX - w : HX, lanes] = x[row : row + w]
                e[mid + z, HX + CX : HX + CX + w, lanes] = x[row + w : row + 2 * w]
            row += 2 * w


def at(e, field, z):
    return e[BASE[field] + HALO[field] + z]


def middle(a):
    return a[HX : HX + CX]


def provisional(e, field, z, grad, here, tension, viscosity):
    a = at(e, field, z)
    zu, zd = at(e, field, z + 1), at(e, field, z - 1)
    xu, xd, yu, yd = x_up(a), x_dn(a), y_up(a), y_dn(a)
    lap = (zu + zd) + (xu + xd) + (yu + yd) - 6.0 * a
    advect = at(e, V0, z) * (zu - zd) + at(e, V1, z) * (xu - xd) + at(e, V2, z) * (yu - yd)
    value = a - (0.5 * DT) * advect + (DT * viscosity) * lap + (DT * tension) * (here * grad)
    return value, lap


def first_kernel(coefs, inner, mr, ms, dr, ds, e, b, u, send, corner, rim, far, pot, p0):
    tension = 0.5 * coefs[1]
    viscosity = 0.1 * coefs[2]
    interface = 0.5 * coefs[3]
    c = lax.axis_index("gy")

    row = 0
    for n, (f, k) in enumerate(SENT):
        below, above = BASE[f] + HALO[f] - k, BASE[f] + HALO[f] + CZ + k - 1
        lo, hi = low_high(c, mr[n], ms[n])
        e[below, HX : HX + CX] = lo
        e[above, HX : HX + CX] = hi
        w = CORNER[n]
        if w == 0:
            continue
        lo, hi = low_high(c, dr[row : row + 2 * w], ds[row : row + 2 * w])
        for layer, part in ((below, lo), (above, hi)):
            e[layer, HX - w : HX] = part[:w]
            e[layer, HX + CX : HX + CX + w] = part[w:]
        row += 2 * w

    def potential(t):
        z = t - 1
        a = at(e, PH, z)
        pot[t] = a * a * a - a - interface * lap_of(a, at(e, PH, z + 1), at(e, PH, z - 1))

    loop(6, potential)

    def along(t):
        z = t - 1
        grad = 0.5 * (at(e, PH, z + 1) - at(e, PH, z - 1))
        value, _ = provisional(e, V0, z, grad, pot[t], tension, viscosity)
        p0[t] = middle(value)

    loop(6, along)

    def across(z):
        phase = at(e, PH, z)
        p1, _ = provisional(e, V1, z, dx(phase), pot[z + 1], tension, viscosity)
        p2, _ = provisional(e, V2, z, dy(phase), pot[z + 1], tension, viscosity)
        div = 0.5 * (p0[z + 2] - p0[z]) + middle(dx(p1) + dy(p2))
        b[z] = -div
        seen = 0.5 * middle(at(e, O0, z + 1) - at(e, O0, z - 1)) + middle(dx(at(e, O1, z)) + dy(at(e, O2, z)))
        u[z] = div - seen

    loop(4, across)

    row = 0
    for n, (name, k, w) in enumerate(AGAIN):
        src = (b if name == "b" else u)[outgoing(c, k)]
        send[CX * n : CX * (n + 1)] = src
        corner[row : row + w] = src[CX - w :]
        corner[row + w : row + 2 * w] = src[:w]
        row += 2 * w
    row = 0
    for name, z, w in RIM:
        field = b if name == "b" else u
        rim[row : row + w] = field[z, CX - w :, :CY]
        rim[row + w : row + 2 * w] = field[z, :w, :CY]
        row += 2 * w
    far[...] = b[0]


def folded(a):
    a = a[:, :CY] + a[:, CY:]
    return (a[0:8] + a[8:16]) + (a[16:24] + a[24:32])


def weight_kernel(coefs, e, adj, w, part, edge, gv, base, pot, g, q, lph, lv, p0):
    mobility, tension, viscosity, interface = constants(coefs)

    def forward(t):
        z = t - 1
        a = at(e, PH, z)
        lap = lap_of(a, at(e, PH, z + 1), at(e, PH, z - 1))
        lph[t] = lap
        here = a * a * a - a - interface * lap
        pot[t] = here
        g[0, t] = 0.5 * (at(e, PH, z + 1) - at(e, PH, z - 1))
        g[1, t] = dx(a)
        g[2, t] = dy(a)
        value, lv[0, t] = provisional(e, V0, z, g[0, t], here, tension, viscosity)
        q[0, t] = value - at(e, O0, z)

    loop(6, forward)

    def across(z):
        here = pot[z + 1]
        p1, lv[1, z] = provisional(e, V1, z, g[1, z + 1], here, tension, viscosity)
        p2, lv[2, z] = provisional(e, V2, z, g[2, z + 1], here, tension, viscosity)
        q[1, z + 1] = p1 - at(e, O1, z)
        q[2, z + 1] = p2 - at(e, O2, z)

    loop(4, across)
    sums = [jnp.zeros((8, CY), jnp.float32)] * 5
    for t in range(CZ):
        here = pot[t + 1]
        lap = lph[t + 1]
        gs = [g[i, t + 1] for i in range(3)]
        up, dn = pot[t + 2] * g[0, t + 2], pot[t] * g[0, t]
        w1 = 0.5 * (up - dn) + dx(here * gs[1]) + dy(here * gs[2])
        w2 = 0.5 * (lv[0, t + 2] - lv[0, t]) + dx(lv[1, t]) + dy(lv[2, t])
        up, dn = lph[t + 2] * g[0, t + 2], lph[t] * g[0, t]
        w3 = 0.5 * (up - dn) + dx(lap * gs[1]) + dy(lap * gs[2])
        w[0, t] = middle(w1)
        w[1, t] = middle(w2)
        w[2, t] = middle(w3)
        lap_pot = lap_of(here, pot[t + 2], pot[t])
        lap_lap = lap_of(lap, lph[t + 2], lph[t])
        flow = at(e, V0, t) * gs[0] + at(e, V1, t) * gs[1] + at(e, V2, t) * gs[2]
        c = at(e, PH, t) - DT * flow + (DT * mobility) * lap_pot - at(e, PO, t)
        adj[t] = c
        v1, v2 = at(e, V1, t), at(e, V2, t)
        base[t] = own(c + DT * (dx(v1 * c) + dy(v2 * c)))
        for i, field in enumerate((V0, V1, V2)):
            a = at(e, field, t)
            gv[0, i, t] = own(0.5 * (at(e, field, t + 1) - at(e, field, t - 1)))
            gv[1, i, t] = own(dx(a))
            gv[2, i, t] = own(dy(a))
        qs = [q[i, t + 1] for i in range(3)]
        qg = qs[0] * gs[0] + qs[1] * gs[1] + qs[2] * gs[2]
        ql = qs[0] * lv[0, t + 1] + qs[1] * lv[1, t] + qs[2] * lv[2, t]
        terms = (middle(c * lap_pot), middle(here * qg), middle(ql), middle(lap * qg), middle(c * lap_lap))
        sums = [s + folded(a) for s, a in zip(sums, terms)]
    for k in range(5):
        part[k] = sums[k]
    c = lax.axis_index("gy")
    pieces = (q[1, 1 + outgoing(c, 1)], q[2, 1 + outgoing(c, 1)], adj[outgoing(c, 1)], adj[outgoing(c, 2)])
    for n, src in enumerate(pieces):
        w = (THIRD[n] - CX) // 2
        edge[THIRD_AT[n] : THIRD_AT[n] + THIRD[n]] = src[HX - w : HX + CX + w]


def shifted(c, zu, zd):
    return (6.0 + SHIFT) * c - ((zu + zd) + (x_up(c) + x_dn(c)) + (y_up(c) + y_dn(c)))


def moment_kernel(b4, u4, r, s, d, ds, x, xs, far, fars, w, part, edge, out, bb, uu, f, af, a2f, ab, au, send, a2b, a2u):
    c = lax.axis_index("gy")
    near = pl.ds(NEAR, NARROW)
    bb[4:8, HX : HX + CX] = b4[...]
    uu[2:6, HX : HX + CX] = u4[...]
    row = 0
    for n, (name, k, width) in enumerate(AGAIN):
        dst, below = (bb, 4 - k) if name == "b" else (uu, 2 - k)
        above = 7 + k if name == "b" else 5 + k
        lo, hi = low_high(c, r[CX * n : CX * (n + 1)], s[CX * n : CX * (n + 1)])
        dst[below, HX : HX + CX] = lo
        dst[above, HX : HX + CX] = hi
        lo, hi = low_high(c, d[row : row + 2 * width], ds[row : row + 2 * width])
        for layer, part_rows in ((below, lo), (above, hi)):
            dst[layer, HX - width : HX] = part_rows[:width]
            dst[layer, HX + CX : HX + CX + width] = part_rows[width:]
        row += 2 * width
    row = 0
    for name, z, width in RIM:
        dst, layer = (bb, 4 + z) if name == "b" else (uu, 2 + z)
        for half, src in enumerate((x, xs)):
            lanes = pl.ds(CY * half, CY)
            dst[layer, HX - width : HX, lanes] = src[row : row + width]
            dst[layer, HX + CX : HX + CX + width, lanes] = src[row + width : row + 2 * width]
        row += 2 * width
    bb[12, HX : HX + CX] = jnp.where(c == 1, far[...], other_first(fars[...]))

    def wide(t):
        a = bb[t + 2]
        across = (pltpu.roll(a, ROWS - 2, 0) + pltpu.roll(a, 2, 0)) + (
            pltpu.roll(a, LANES - 2, 1) + pltpu.roll(a, 2, 1)
        )
        f[t] = 0.25 * ((bb[t + 4] + bb[t]) + across) - 1.5 * a

    loop(9, wide)

    def apply(src, dst, count):
        def body(t):
            dst[t] = shifted(src[t + 1], src[t + 2], src[t])

        loop(count, body)

    apply(f, af, 7)
    apply(af, a2f, 5)
    apply(bb.at[pl.ds(1, 10)], ab, 8)
    apply(ab.at[pl.ds(1, 6)], a2b, 4)
    apply(uu, au, 6)
    apply(au, a2u, 4)

    rows = pl.ds(HX, CX)
    acc = [jnp.zeros((8, CY), jnp.float32)] * 40
    for t in range(CZ):
        vb, vab, va2b = bb[t + 4, rows], ab[t + 2, rows], a2b[t, rows]
        vu, vau, va2u = uu[t + 2, rows], au[t + 1, rows], a2u[t, rows]
        vf, vaf, va2f = f[t + 2, rows], af[t + 1, rows], a2f[t, rows]
        a = a2f[t]
        across = (x_up(a) + x_dn(a)) + (y_up(a) + y_dn(a))
        va3f = (6.0 + SHIFT) * va2f - (2.0 * a2f[t + 1, rows] + middle(across))
        terms = [
            vb * vb, vb * vab, vab * vab, vab * va2b,
            vu * vu, vu * vau, vau * vau, vau * va2u,
            vu * vf, vu * vaf, vu * va2f, vau * va2f, va2u * va2f,
            vf * vf, vf * vaf, vaf * vaf, vaf * va2f, va2f * va2f, va2f * va3f,
        ]
        for k in range(3):
            wk = w[k, t]
            terms += [a * wk for a in (vu, vau, vf, vaf, va2f, vb, vab)]
        acc = [x + folded(a) for x, a in zip(acc, terms)]
    rows_list = [jnp.sum(a, axis=0, keepdims=True) for a in acc]
    rows_list += [jnp.sum(part[k], axis=0, keepdims=True) for k in range(5)]
    rows_list += [jnp.zeros((1, CY), jnp.float32)] * (48 - NUM_SUMS)
    table = jnp.concatenate(rows_list, axis=0)
    totals = jnp.sum(table, axis=1, keepdims=True)
    line = lax.broadcasted_iota(jnp.int32, (48, SLOTS), 1)
    which = lax.broadcasted_iota(jnp.int32, (48, SLOTS), 0)
    row = jnp.sum(jnp.where(line == which, totals, 0.0), axis=0, keepdims=True)
    out[...] = jnp.broadcast_to(row, (PARTNERS, SLOTS))
    send[0 : THIRD_AT[4]] = edge[...]
    pieces = (a2f[outgoing(c, 1)], a2f[outgoing(c, 2)], af[1 + outgoing(c, 2)], au[1 + outgoing(c, 2)])
    for n, src in enumerate(pieces, 4):
        w = (THIRD[n] - CX) // 2
        send[THIRD_AT[n] : THIRD_AT[n] + THIRD[n]] = src[HX - w : HX + CX + w]


def steps(m0, m1, m2, m3):
    alpha = m0 / m1
    second = (m1 / m0) * ((m0 * m2 - m1 * m1) / (m1 * m3 - m2 * m2))
    second = jnp.clip(second, 1.0 / (12.0 + SHIFT), 1.0 / SHIFT)
    return alpha + second * ((m0 * m2) / (m1 * m1)), -second * alpha


def solve_kernel(gathered, mobility, tension, coef_out, params):
    total = jnp.sum(gathered[...], axis=0, keepdims=True)
    line = lax.broadcasted_iota(jnp.int32, (1, SLOTS), 1)

    def s(k):
        return jnp.sum(jnp.where(line == k, total, 0.0), axis=1, keepdims=True)

    c0, c1 = steps(s(0), s(1), s(2), s(3))
    uu = [s(4 + k) for k in range(4)]
    uf = [s(8 + k) for k in range(5)]
    ff = [s(13 + k) for k in range(6)]
    moments = [
        uu[k] - 2.0 * (c0 * uf[k] + c1 * uf[k + 1])
        + (c0 * c0) * ff[k] + (2.0 * c0 * c1) * ff[k + 1] + (c1 * c1) * ff[k + 2]
        for k in range(4)
    ]
    e0, e1 = steps(*moments)
    coef = (e0, e1, -e0 * c0, -(e0 * c1 + e1 * c0), -e1 * c1, -c0, -c1)
    for j in range(7):
        coef_out[j : j + 1] = jnp.broadcast_to(coef[j], (1, CY))

    def meet(k):
        value = coef[0] * s(19 + 7 * k)
        for j in range(1, 7):
            value = value + coef[j] * s(19 + 7 * k + j)
        return value

    scale = 1.0 / (256 * 64 * 256)
    g0 = DT * s(40)
    g1 = DT * (s(41) - meet(0))
    g2 = DT * (s(42) - meet(1))
    g3 = -((DT * mobility) * s(44) + (DT * tension) * (s(43) - meet(2)))
    place = lax.broadcasted_iota(jnp.int32, (1, CY), 1)
    packed = jnp.where(place == 0, g0, jnp.where(place == 1, g1, jnp.where(place == 2, g2, g3)))
    params[...] = (packed * scale)[0, 0:4]
    return coef


def half_step(side, halo, coef, consts, basis, state, work, write):
    mobility, tension, viscosity, interface = consts
    uu, f, af, a2f, bb, ab, au = basis
    e, q, adj4, pot, g, gv, base = state
    phi, pr, pa, adj, qe, new = work
    inside, wider = pl.ds(HX, CX), pl.ds(HX - 1, CX + 2)
    for i in range(2):
        qe[i, 5 * side, inside] = halo(i)
    adj[1 + 5 * side, wider] = halo(2)
    adj[7 * side, inside] = halo(3)

    def mixed(terms):
        value = coef[0] * terms[0]
        for a, t in zip(coef[1:], terms[1:]):
            value = value + a * t
        return value

    i = 1 + 5 * side
    phi[i, wider] = mixed([
        uu[i, wider], au[i - 1, wider], f[i, wider], af[i - 1, wider], halo(4), bb[i + 2, wider], ab[i, wider],
    ])
    i = 7 * side
    phi[i, inside] = mixed([
        uu[i, inside], halo(7), f[i, inside], halo(6), halo(5), bb[i + 2, inside], ab[i, inside],
    ])

    def project(t):
        c = phi[t + 1]
        r0 = q[0, t] + 0.5 * (phi[t + 2] - phi[t])
        r1 = qe[0, t] + dx(c)
        r2 = qe[1, t] + dy(c)
        pr[0, t] = r0
        pr[1, t] = r1
        pr[2, t] = r2
        lap = lap_of(adj[t + 1], adj[t + 2], adj[t])
        pa[t] = (DT * mobility) * lap + (DT * tension) * (r0 * g[0, t] + r1 * g[1, t] + r2 * g[2, t])

    for t in new:
        project(t)

    for n in range(2):
        t = 2 * side + n
        v1, v2 = at(e, V1, t), at(e, V2, t)
        v0u, v0d = at(e, V0, t + 1), at(e, V0, t - 1)
        here = pot[t + 1]
        ph = own(at(e, PH, t))
        lam = pa[t + 1]
        up = v0u * adj[t + 3] - tension * (pot[t + 2] * pr[0, t + 2])
        dn = v0d * adj[t + 1] - tension * (pot[t] * pr[0, t])
        div = 0.5 * (up - dn) - tension * (dx(here * pr[1, t + 1]) + dy(here * pr[2, t + 1]))
        value = base[t] + DT * own(div) + (3.0 * ph * ph - 1.0) * own(lam)
        write(n, 0, value - interface * own(lap_of(lam, pa[t + 2], pa[t])))
        r = [pr[i, t + 1] for i in range(3)]
        mine = [own(a) for a in r]
        c = own(adj[t + 2])
        for k in range(3):
            mix = mine[0] * gv[k, 0, t] + mine[1] * gv[k, 1, t] + mine[2] * gv[k, 2, t]
            moved = (viscosity + 0.5 * v0u) * pr[k, t + 2] + (viscosity - 0.5 * v0d) * pr[k, t]
            moved = moved + x_up((viscosity + 0.5 * v1) * r[k]) + x_dn((viscosity - 0.5 * v1) * r[k])
            moved = moved + y_up((viscosity + 0.5 * v2) * r[k]) + y_dn((viscosity - 0.5 * v2) * r[k])
            moved = own(moved) - (6.0 * viscosity) * mine[k]
            write(n, 1 + k, mine[k] + DT * (moved - mix - c * own(g[k, t + 1])))


def constants(coefs):
    return 0.1 * coefs[0], 0.5 * coefs[1], 0.1 * coefs[2], 0.5 * coefs[3]


def near_kernel(
    coefs, gathered, uu, f, af, a2f, bb, ab, au, ri, e, q, adj4, pot, g, gv, base,
    params, table, phi_own, shared, result, phi, pr, pa, adj, qe,
):
    consts = constants(coefs)
    coef = solve_kernel(gathered, consts[0], consts[1], table, params)
    side = lax.axis_index("gy")
    adj[2:6] = adj4[...]
    for i in range(2):
        qe[i, 1:5] = q[i + 1, 1:5]
    for z in range(CZ):
        value = coef[0] * uu[z + 2] + coef[1] * au[z + 1] + coef[2] * f[z + 2] + coef[3] * af[z + 1]
        value = value + coef[4] * a2f[z] + coef[5] * bb[z + 4] + coef[6] * ab[z + 2]
        phi[z + 2] = value
        phi_own[z] = value

    def write(n, k, value):
        result[k, n] = value

    new = [2 * side + n for n in range(4)]
    half_step(
        side, lambda n: ri[THIRD_AT[n] : THIRD_AT[n] + THIRD[n]], coef, consts, (uu, f, af, a2f, bb, ab, au), (e, q, adj4, pot, g, gv, base),
        (phi, pr, pa, adj, qe, new), write,
    )
    for n in range(2):
        for i in range(3):
            shared[i, n] = pr[i, 2 + n]
        shared[3, n] = pa[2 + n]


def far_kernel(
    coefs, table, uu, f, af, a2f, bb, ab, au, si, e, q, adj4, pot, g, gv, base, phi_own, shared, result,
    phase_back, velocity_back, phi, pr, pa, adj, qe,
):
    consts = constants(coefs)
    coef = [table[j : j + 1, 0:1] for j in range(7)]
    mine = lax.axis_index("gy")
    side = 1 - mine
    adj[2:6] = adj4[...]
    for i in range(2):
        qe[i, 1:5] = q[i + 1, 1:5]
    phi[2:6] = phi_own[...]
    for n in range(2):
        for i in range(3):
            pr[i, 2 + n] = shared[i, n]
        pa[2 + n] = shared[3, n]

    def write(n, k, value):
        if k == 0:
            phase_back[2 * side + n] = value
        else:
            velocity_back[k - 1, 2 * side + n] = value

    new = [4 * side + n for n in range(2)]
    half_step(
        side, lambda n: other_first(si[THIRD_AT[n] : THIRD_AT[n] + THIRD[n]]), coef, consts, (uu, f, af, a2f, bb, ab, au),
        (e, q, adj4, pot, g, gv, base), (phi, pr, pa, adj, qe, new), write,
    )
    for n in range(2):
        phase_back[2 * mine + n] = result[0, n]
        for k in range(3):
            velocity_back[k, 2 * mine + n] = result[1 + k, n]


def f32(*shape):
    return jax.ShapeDtypeStruct(shape, jnp.float32)


def layers(*lead):
    return f32(*lead, ROWS, LANES)


def scratch(*lead):
    return pltpu.VMEM((*lead, ROWS, LANES), jnp.float32)


VM = pl.BlockSpec(memory_space=pltpu.VMEM)
SM = pl.BlockSpec(memory_space=pltpu.SMEM)
PARAMS = pltpu.CompilerParams(vmem_limit_bytes=12 * 1024 * 1024)
SWAP = [(0, 1), (1, 0)]


def role_shift(value, cross):
    gx, gy, gz = (lax.axis_size(a) for a in ("gx", "gy", "gz"))
    pairs = []
    for x in range(gx):
        for y in range(gy):
            for i in range(gz):
                target = (1 - x if cross else x, y, (i + 1 - 2 * y) % gz)
                pairs.append(((x * gy + y) * gz + i, (target[0] * gy + y) * gz + target[2]))
    return lax.ppermute(value, ("gx", "gy", "gz"), pairs)


def second_down(value):
    gx, gz = lax.axis_size("gx"), lax.axis_size("gz")
    pairs = [((2 * x + y) * gz + i, (2 * x + y) * gz + (i - 2 * y) % gz) for x in range(gx) for y in range(2) for i in range(gz)]
    return lax.ppermute(value, ("gx", "gy", "gz"), pairs)


def swap(value):
    return lax.ppermute(value, "gy", SWAP)


def call(kernel, outs, ins, scratches, name, smem, aliases={}):
    return pl.pallas_call(
        kernel,
        out_shape=outs,
        in_specs=[SM] * smem + [VM] * (len(ins) - smem),
        out_specs=jax.tree.map(lambda _: VM, outs),
        scratch_shapes=scratches,
        input_output_aliases=aliases,
        compiler_params=PARAMS,
        name=name,
    )(*ins)


def local(phase, velocity, phase_obs, velocity_obs, coefs):
    mine = (velocity, phase, phase_obs, velocity_obs)
    stack, edges, coefs, give = pl.pallas_call(
        load_kernel,
        out_shape=(f32(8, CZ, CX, CY), f32(EDGE_ROWS, CY), f32(4), f32(len(SENT), CX, CY)),
        in_specs=[pl.BlockSpec(memory_space=pltpu.HBM)] * 5,
        out_specs=(VM,) * 4,
        scratch_shapes=[pltpu.SemaphoreType.DMA((5,))],
        compiler_params=PARAMS,
        name="load",
    )(*(pltpu.with_memory_space_constraint(a, pltpu.HBM) for a in (*mine, coefs)))
    peer = swap(stack)
    gxr = lax.ppermute(edges, "gx", SWAP)
    main, diag = call(
        pack_kernel,
        (f32(len(SENT), CX, LANES), f32(CORNER_ROWS, LANES)),
        (stack, swap(give)),
        [],
        "pack",
        0,
    )
    mr = role_shift(main, False)
    dr = role_shift(diag, True)
    gxr, mr, dr = lax.optimization_barrier((gxr, mr, dr))
    gxs = swap(gxr)
    inner = call(inner_kernel, layers(TOTAL), (stack, peer, gxr, gxs), [], "inner", 0)
    ms = swap(mr)
    ds = swap(dr)
    e, b, u, send, corner, rim, far = call(
        first_kernel,
        (layers(TOTAL), f32(CZ, CX, LANES), f32(CZ, CX, LANES), f32(CX * len(AGAIN), LANES),
         f32(AGAIN_ROWS, LANES), f32(RIM_ROWS, CY), f32(CX, LANES)),
        (coefs, inner, mr, ms, dr, ds),
        [scratch(6), pltpu.VMEM((6, CX, LANES), jnp.float32)],
        "first",
        1,
        {1: 0},
    )
    r2 = role_shift(send, False)
    d2 = role_shift(corner, True)
    x2 = lax.ppermute(rim, "gx", SWAP)
    far = second_down(far)
    adj, w, part, edge, gv, base, pot, g, q = call(
        weight_kernel,
        (layers(4), f32(3, CZ, CX, LANES), f32(5, 8, CY), f32(THIRD_AT[4], LANES), f32(3, 3, CZ, CX, CY),
         f32(CZ, CX, CY), layers(6), layers(3, 6), layers(3, 6)),
        (coefs, e),
        [scratch(6), scratch(3, 6), scratch(6)],
        "weights",
        1,
    )
    r2, d2, x2, far, w, part, edge = lax.optimization_barrier((r2, d2, x2, far, w, part, edge))
    s2, ds2, xs2 = swap(r2), swap(d2), swap(x2)
    fars = swap(far)
    sums, bb, uu, f, af, a2f, ab, au, send = call(
        moment_kernel,
        (f32(PARTNERS, SLOTS), layers(13), layers(8), layers(9), layers(7), layers(5), layers(8), layers(6),
         f32(THIRD_ROWS, LANES)),
        (b, u, r2, s2, d2, ds2, x2, xs2, far, fars, w, part, edge),
        [scratch(4), scratch(4)],
        "moments",
        0,
    )
    ri = role_shift(send, False)
    gathered = lax.all_to_all(sums.reshape(PARTNERS, 1, SLOTS), ("gx", "gz"), 0, 0).reshape(PARTNERS, SLOTS)
    ri, gathered = lax.optimization_barrier((ri, gathered))
    si = swap(ri)
    basis = (uu, f, af, a2f, bb, ab, au)
    state = (e, q, adj, pot, g, gv, base)
    room = [scratch(8), scratch(3, 6), scratch(6), scratch(8), scratch(2, 6)]
    params, table, phi, shared, result = call(
        near_kernel,
        (f32(4), f32(8, CY), layers(4), layers(4, 2), f32(4, 2, CX, CY)),
        (coefs, gathered, *basis, ri, *state),
        room,
        "near",
        1,
    )
    phase_back, velocity_back = call(
        far_kernel,
        (f32(CZ, CX, CY), f32(3, CZ, CX, CY)),
        (coefs, table, *basis, si, *state, phi, shared, result),
        room,
        "far",
        1,
    )
    return phase_back, velocity_back, params


def solution(mesh):
    return jax.shard_map(
        local,
        mesh=mesh,
        in_specs=(
            P("gz", "gx", "gy"),
            P(None, "gz", "gx", "gy"),
            P("gz", "gx", "gy"),
            P(None, "gz", "gx", "gy"),
            P(),
        ),
        out_specs=(P("gz", "gx", "gy"), P(None, "gz", "gx", "gy"), P()),
        check_vma=False,
    )
```
